128 devices in a mesh: ctx: 64 (over z, y_lo, x, core), tp: 2 (over y_hi).
Axes of the slice: x: 4, y: 4 (y_hi: 2, y_lo: 2; y = y_hi * 2 + y_lo), z: 4, core: 2. Of those that a mesh axis runs over, the one named last changes fastest.
Arguments:
- tokens: bfloat16 [8192, 2048], P(('ctx', 'tp')), may hold values from -6 to 6
- norm_gain: float32 [2048], replicated, may hold values from 0.5 to 1.5
- w_query: bfloat16 [2048, 2048], P('ctx', 'tp'), may hold values from -0.125 to 0.125
- key_matrix: bfloat16 [2048, 1024], P('ctx', 'tp'), may hold values from -0.125 to 0.125
- value_matrix: bfloat16 [2048, 1024], P('ctx', 'tp'), may hold values from -0.125 to 0.125
- query_gain: float32 [128], replicated, may hold values from 1 to 2
- key_gain: float32 [128], replicated, may hold values from 1 to 2
- w_out: bfloat16 [2048, 2048], P('ctx', 'tp'), may hold values from -0.5 to 0.5
- ffn_gain: float32 [2048], replicated, may hold values from 0.5 to 1.5
- w_gate: bfloat16 [2048, 6144], P('ctx', 'tp'), may hold values from -0.125 to 0.125
- w_up: bfloat16 [2048, 6144], P('ctx', 'tp'), may hold values from -0.125 to 0.125
- w_down: bfloat16 [2048, 6144], P('ctx', 'tp'), may hold values from -0.078125 to 0.078125
- cotangent: bfloat16 [8192, 2048], P(('ctx', 'tp')), may hold values from -6 to 6
Outputs:
- result: bfloat16 [8192, 2048], P(('ctx', 'tp'))
- grad_input: float32 [8192, 2048], P(('ctx', 'tp'))
- grad_norm_gain: float32 [2048], replicated
- grad_query: float32 [2048, 2048], P('ctx', 'tp')
- grad_key: float32 [2048, 1024], P('ctx', 'tp')
- grad_value: float32 [2048, 1024], P('ctx', 'tp')
- grad_query_gain: float32 [128], replicated
- grad_key_gain: float32 [128], replicated
- grad_out: float32 [2048, 2048], P('ctx', 'tp')
- grad_ffn_gain: float32 [2048], replicated
- grad_gate: float32 [2048, 6144], P('ctx', 'tp')
- grad_up: float32 [2048, 6144], P('ctx', 'tp')
- grad_down: float32 [2048, 6144], P('ctx', 'tp')
The draws below stay inside these ranges and needn't reach their ends.
All inputs are finite; a program needn't handle non-finite values.
Results may differ from the reference program's by a relative error of at most 0.019.
Values may be sent and summed in bfloat16 or wider, within the bound.
A program may use at most 384 MiB of HBM per device.

```python
import math
import jax
import jax.numpy as jnp
from jax import lax

MODEL_DIMENSION = 2048
QUERY_HEADS = 16
KEY_VALUE_HEADS = 8
HEAD_DIMENSION = 128
FF = 6144
SEQ = 8192


def block_levels(key, extent, cuts, least, high):
    factor_of = 1.0
    for axis_at, shards_of in cuts:
        heights = jax.random.uniform(jax.random.fold_in(jax.random.fold_in(key, 6), axis_at), (shards_of,), jnp.float32, least / len(cuts), high / len(cuts))
        factor_of = factor_of * jnp.repeat(jnp.exp(heights), extent[axis_at] // shards_of).reshape((-1,) + (1,) * (len(extent) - 1 - axis_at))
    return factor_of


def noise(rng, extent, width, most, cuts=(), kind=jnp.bfloat16):
    values = jax.random.normal(rng, extent, jnp.float32) * width
    if len(cuts) > 0:
        values = block_levels(rng, extent, cuts, -0.22, 0.18) * values
    return jnp.clip(values, min=-most, max=most).astype(kind)


def setup_inputs(seed: int = 0) -> dict:
    arg_keys = jax.random.split(jax.random.key(seed), 14)
    return {
        "tokens": noise(arg_keys[0], (SEQ, MODEL_DIMENSION), 1.0, 6.0, ((0, 128),)),
        "norm_gain": jnp.clip(1.0 + 0.1 * jax.random.normal(arg_keys[1], (MODEL_DIMENSION,), jnp.float32), 0.5, 1.5),
        "w_query": noise(arg_keys[2], (MODEL_DIMENSION, QUERY_HEADS * HEAD_DIMENSION), MODEL_DIMENSION ** -0.5, 0.125, ((0, 64), (1, 2))),
        "key_matrix": noise(arg_keys[3], (MODEL_DIMENSION, KEY_VALUE_HEADS * HEAD_DIMENSION), MODEL_DIMENSION ** -0.5, 0.125, ((0, 64), (1, 2))),
        "value_matrix": noise(arg_keys[4], (MODEL_DIMENSION, KEY_VALUE_HEADS * HEAD_DIMENSION), MODEL_DIMENSION ** -0.5, 0.125, ((0, 64), (1, 2))),
        "query_gain": jnp.clip(jax.random.uniform(arg_keys[5], (HEAD_DIMENSION,), jnp.float32, 1.0, 2.0), 1.0, 2.0),
        "key_gain": jnp.clip(jax.random.uniform(arg_keys[6], (HEAD_DIMENSION,), jnp.float32, 1.0, 2.0), 1.0, 2.0),
        "w_out": noise(arg_keys[7], (MODEL_DIMENSION, QUERY_HEADS * HEAD_DIMENSION), (QUERY_HEADS * HEAD_DIMENSION // 16) ** -0.5, 0.5, ((0, 64), (1, 2))),
        "ffn_gain": jnp.clip(1.0 + 0.1 * jax.random.normal(arg_keys[8], (MODEL_DIMENSION,), jnp.float32), 0.5, 1.5),
        "w_gate": noise(arg_keys[9], (MODEL_DIMENSION, FF), MODEL_DIMENSION ** -0.5, 0.125, ((0, 64), (1, 2))),
        "w_up": noise(arg_keys[10], (MODEL_DIMENSION, FF), MODEL_DIMENSION ** -0.5, 0.125, ((0, 64), (1, 2))),
        "w_down": noise(arg_keys[11], (MODEL_DIMENSION, FF), FF ** -0.5, 0.078125, ((0, 64), (1, 2))),
        "cotangent": noise(arg_keys[12], (SEQ, MODEL_DIMENSION), 1.0, 6.0, ((0, 128),)),
    }


epsilon = 1e-06
rope_base = 1000000.0
masked_score = -1e+30

@jax.custom_vjp
def lowered_input(v):
    return lax.optimization_barrier(v.astype(jnp.bfloat16)).astype(jnp.float32)

@jax.custom_vjp
def lowered_backward(v):
    return v

def low_keep(v):
    return (lowered_input(v), None)

def low_pass(kept, grad):
    return (grad,)

def back_keep(v):
    return (v, None)

def back_low(kept, grad):
    return (lowered_input(grad),)
lowered_input.defvjp(low_keep, low_pass)
lowered_backward.defvjp(back_keep, back_low)

def rms_norm(value_rows, gain):
    return value_rows * lax.rsqrt(lax.optimization_barrier(jnp.mean(value_rows * value_rows, axis=-1, keepdims=True)) + epsilon) * gain

def rotate(value_rows, cosine, sine_table):
    middle = value_rows.shape[-1] // 2
    first_half = value_rows[..., :middle]
    second_half = value_rows[..., middle:]
    return jnp.concatenate([first_half * cosine - second_half * sine_table, second_half * cosine + first_half * sine_table], axis=-1)

def rope_tables(positions):
    exponent = jnp.arange(0, HEAD_DIMENSION, 2, dtype=jnp.float32) / HEAD_DIMENSION
    angles = positions[:, None] * (1.0 / rope_base ** exponent)[None, :]
    return (jnp.cos(angles)[:, None, :], jnp.sin(angles)[:, None, :])

def matrix_product(left_side, right_side):
    return jnp.dot(left_side, right_side, precision=lax.Precision.HIGHEST, preferred_element_type=jnp.float32)

def forward(tokens, norm_gain, w_query, key_matrix, value_matrix, query_gain, key_gain, w_out, ffn_gain, w_gate, w_up, w_down):
    sequence_length = tokens.shape[0]
    heads_per_group = QUERY_HEADS // KEY_VALUE_HEADS
    cosine, sine_table = rope_tables(jnp.arange(sequence_length).astype(jnp.float32))
    normalized_input = lowered_input(rms_norm(tokens, norm_gain))
    queries = lowered_backward(matrix_product(normalized_input, w_query)).reshape(sequence_length, QUERY_HEADS, HEAD_DIMENSION)
    heads_of_keys = lowered_backward(matrix_product(normalized_input, key_matrix)).reshape(sequence_length, KEY_VALUE_HEADS, HEAD_DIMENSION)
    value_rows = lowered_input(lowered_backward(matrix_product(normalized_input, value_matrix))).reshape(sequence_length, KEY_VALUE_HEADS, HEAD_DIMENSION)
    queries = lowered_input(rotate(rms_norm(queries, query_gain), cosine, sine_table))
    heads_of_keys = lowered_input(rotate(rms_norm(heads_of_keys, key_gain), cosine, sine_table))
    rows_per_block = math.gcd(sequence_length, 512)
    block_count = sequence_length // rows_per_block
    key_places = jnp.arange(sequence_length)
    score_scale = HEAD_DIMENSION ** (-0.5)

    def attend(payload):
        block_of_queries, first_row = payload
        grouped_heads = block_of_queries.reshape(rows_per_block, KEY_VALUE_HEADS, heads_per_group, HEAD_DIMENSION)
        scores = jnp.einsum('qgnd,kgd->gnqk', grouped_heads, heads_of_keys, precision=lax.Precision.HIGHEST) * score_scale
        scores = lowered_backward(scores)
        row_places = first_row + jnp.arange(rows_per_block)
        allowed = row_places[:, None] >= key_places[None, :]
        scores = jnp.where(allowed, scores, masked_score)
        probabilities = jax.nn.softmax(scores, axis=-1)
        mixture = jnp.einsum('gnqk,kgd->qgnd', lowered_input(probabilities), value_rows, precision=lax.Precision.HIGHEST)
        return mixture.reshape(rows_per_block, QUERY_HEADS * HEAD_DIMENSION)
    starts = (jnp.arange(block_count) * rows_per_block).astype(jnp.int32)
    context = lax.map(jax.checkpoint(attend), (queries.reshape(block_count, rows_per_block, QUERY_HEADS, HEAD_DIMENSION), starts))
    context = lowered_input(lowered_backward(context.reshape(sequence_length, QUERY_HEADS * HEAD_DIMENSION)))
    branch = lowered_backward(matrix_product(context, w_out.T))
    middle_state = tokens + branch
    normed_two = lowered_input(rms_norm(middle_state, ffn_gain))
    gate_value = lowered_backward(matrix_product(normed_two, w_gate))
    upward = lowered_backward(matrix_product(normed_two, w_up))
    hidden = lowered_input(jax.nn.silu(gate_value) * upward)
    return middle_state + matrix_product(hidden, w_down.T)

def reference(tokens, norm_gain, w_query, key_matrix, value_matrix, query_gain, key_gain, w_out, ffn_gain, w_gate, w_up, w_down, cotangent):
    inputs = tuple((array.astype(jnp.float32) for array in (tokens, norm_gain, w_query, key_matrix, value_matrix, query_gain, key_gain, w_out, ffn_gain, w_gate, w_up, w_down)))
    result, pullback = jax.vjp(forward, *inputs)
    grads = pullback(cotangent.astype(jnp.float32))
    return (result.astype(jnp.bfloat16), grads[0], grads[1], grads[2], grads[3], grads[4], grads[5], grads[6], grads[7], grads[8], grads[9], grads[10], grads[11])
```

```python
import functools

import jax
import jax.numpy as jnp
from jax import lax
from jax.experimental import pallas as pl
from jax.experimental.pallas import tpu as pltpu
from jax.sharding import Mesh
from jax.sharding import PartitionSpec as P

AXES = ("z", "yl", "x", "c", "t")
SIZES = {"z": 4, "yl": 2, "x": 4, "c": 2, "t": 2}
W_AXES = ("z", "yl")
T_AXES = ("x", "c", "t")
NW, NT = 8, 16
ROWS = 64
TOK = NW * ROWS
D = 2048
HD = 128
SEQ = 8192
QC, KC, FC = 256, 128, 768
QKV = QC + 2 * KC
COLS = QKV + QC + 3 * FC
VMEM_LIMIT = 60 << 20

epsilon = 1e-06
rope_base = 1000000.0
score_scale = HD ** (-0.5)
LOG2E = 1.4426950408889634

bf16 = jnp.bfloat16
f32 = jnp.float32
MESH = pl.DeviceIdType.MESH
VM = pl.BlockSpec(memory_space=pltpu.VMEM)
ANY = pl.BlockSpec(memory_space=pl.ANY)
DMA = pltpu.SemaphoreType.DMA


def params(cid=None):
    if cid is None:
        return pltpu.CompilerParams(vmem_limit_bytes=VMEM_LIMIT)
    return pltpu.CompilerParams(
        collective_id=cid, has_side_effects=True, vmem_limit_bytes=VMEM_LIMIT
    )


def place():
    return {a: lax.axis_index(a) for a in AXES}


def shifted(me, axis, by):
    return lax.rem(me[axis] + by, SIZES[axis])


def barrier(devices):
    sem = pltpu.get_barrier_semaphore()
    for d in devices:
        pl.semaphore_signal(sem, inc=1, device_id=d, device_id_type=MESH)
    pl.semaphore_wait(sem, len(devices))


def remote(src, dst, ssem, rsem, device):
    return pltpu.make_async_remote_copy(
        src_ref=src, dst_ref=dst, send_sem=ssem, recv_sem=rsem, device_id=device, device_id_type=MESH
    )


class Sends:
    def __init__(self, ssem, rsem, base=0):
        self.ssem, self.rsem, self.base, self.open = ssem, rsem, base, []

    def send(self, kind, src, dst, device):
        k = self.base + kind
        c = remote(src, dst, self.ssem.at[k], self.rsem.at[k], device)
        c.start()
        self.open.append(c)

    def recv(self, kind, dst, device):
        k = self.base + kind
        remote(dst, dst, self.ssem.at[k], self.rsem.at[k], device).wait_recv()

    def close(self):
        for c in self.open:
            c.wait_send()


def w_devices(me):
    return (
        {"z": shifted(me, "z", 1)},
        {"z": shifted(me, "z", 3)},
        {"yl": 1 - me["yl"]},
    )


class GatherW:
    KINDS = 14

    def __init__(self, me, dst, sends):
        self.me, self.dst, self.s = me, dst, sends
        z, y = me["z"], me["yl"]
        zp, zm, zo, yo = shifted(me, "z", 1), shifted(me, "z", 3), shifted(me, "z", 2), 1 - y
        self.own, self.own_o = 2 * z + y, 2 * z + yo
        self.gp, self.gpo = 2 * zp + y, 2 * zp + yo
        self.gm, self.gmo = 2 * zm + y, 2 * zm + yo
        self.go, self.goo = 2 * zo + y, 2 * zo + yo
        self.dp, self.dm, self.dy = w_devices(me)

    def part(self, g, lo, hi):
        return self.dst.at[g, lo:hi]

    def put(self, kind, g, lo, hi, device):
        self.s.send(kind, self.part(g, lo, hi), self.part(g, lo, hi), device)

    def got(self, kind, g, lo, hi, device):
        self.s.recv(kind, self.part(g, lo, hi), device)

    def start(self):
        self.put(0, self.own, 0, 64, self.dp)
        self.put(1, self.own, 0, 64, self.dm)
        self.put(2, self.own, 0, 64, self.dy)

    def middle(self):
        dp, dm, dy = self.dp, self.dm, self.dy
        self.got(2, self.own_o, 0, 64, dy)
        self.put(3, self.own_o, 0, 32, dp)
        self.put(4, self.own_o, 0, 32, dm)
        self.got(0, self.gm, 0, 64, dm)
        self.put(5, self.gm, 16, 48, dp)
        self.put(6, self.gm, 32, 64, dy)
        self.got(1, self.gp, 0, 64, dp)
        self.put(7, self.gp, 0, 16, dm)
        self.put(8, self.gp, 48, 64, dm)
        self.put(9, self.gp, 32, 64, dy)

    def end(self):
        dp, dm, dy = self.dp, self.dm, self.dy
        self.got(3, self.gmo, 0, 32, dm)
        self.put(10, self.gmo, 16, 32, dp)
        self.got(4, self.gpo, 0, 32, dp)
        self.put(11, self.gpo, 0, 16, dm)
        self.got(5, self.go, 16, 48, dm)
        self.put(12, self.go, 32, 48, dy)
        self.got(8, self.go, 48, 64, dp)
        self.put(13, self.go, 48, 64, dy)
        self.got(7, self.go, 0, 16, dp)
        self.got(6, self.gmo, 32, 64, dy)
        self.got(9, self.gpo, 32, 64, dy)
        self.got(10, self.goo, 16, 32, dm)
        self.got(11, self.goo, 0, 16, dp)
        self.got(12, self.goo, 32, 48, dy)
        self.got(13, self.goo, 48, 64, dy)


class SumW:
    KINDS = 11
    LAND = (32, 32, 32, 16, 16, 32, 32, 32, 32, 64, 64, 64)

    def __init__(self, me, part, land, sends):
        self.part, self.land, self.s = part, land, sends
        z, y = me["z"], me["yl"]
        zp, zm, zo, yo = shifted(me, "z", 1), shifted(me, "z", 3), shifted(me, "z", 2), 1 - y
        self.own, self.own_o = 2 * z + y, 2 * z + yo
        self.gp, self.gpo = 2 * zp + y, 2 * zp + yo
        self.gm, self.gmo = 2 * zm + y, 2 * zm + yo
        self.go, self.goo = 2 * zo + y, 2 * zo + yo
        self.dp, self.dm, self.dy = w_devices(me)
        self.offset = [sum(self.LAND[:k]) for k in range(len(self.LAND))]

    def slot(self, kind, lo=0, n=None):
        n = self.LAND[kind] if n is None else n
        return self.land.at[self.offset[kind] + lo : self.offset[kind] + lo + n]

    def put(self, kind, g, lo, hi, device):
        self.s.send(kind, self.part.at[g, lo:hi], self.slot(kind), device)

    def got(self, kind, device):
        self.s.recv(kind, self.slot(kind), device)

    def add(self, kind, g, lo, hi):
        rows = self.slot(kind)
        self.part[g, lo:hi] = (self.part[g, lo:hi].astype(f32) + rows[...].astype(f32)).astype(bf16)

    def run(self):
        dp, dm, dy = self.dp, self.dm, self.dy
        self.put(0, self.goo, 32, 64, dy)
        self.put(3, self.goo, 16, 32, dm)
        self.put(4, self.goo, 0, 16, dp)
        self.put(1, self.gmo, 32, 64, dy)
        self.put(2, self.gpo, 32, 64, dy)
        self.got(0, dy)
        self.add(0, self.go, 32, 64)
        self.put(5, self.go, 16, 48, dm)
        self.s.send(6, self.part.at[self.go, 0:16], self.slot(6, 0, 16), dp)
        self.s.send(11, self.part.at[self.go, 48:64], self.slot(6, 16, 16), dp)
        self.got(3, dp)
        self.add(3, self.gmo, 16, 32)
        self.put(7, self.gmo, 0, 32, dm)
        self.got(4, dm)
        self.add(4, self.gpo, 0, 16)
        self.put(8, self.gpo, 0, 32, dp)
        self.got(1, dy)
        self.add(1, self.gm, 32, 64)
        self.got(5, dp)
        self.add(5, self.gm, 16, 48)
        self.put(9, self.gm, 0, 64, dm)
        self.got(2, dy)
        self.add(2, self.gp, 32, 64)
        self.s.recv(6, self.slot(6, 0, 16), dm)
        self.s.recv(11, self.slot(6, 16, 16), dm)
        lo, hi = self.slot(6, 0, 16), self.slot(6, 16, 16)
        self.part[self.gp, 0:16] = (self.part[self.gp, 0:16].astype(f32) + lo[...].astype(f32)).astype(bf16)
        self.part[self.gp, 48:64] = (self.part[self.gp, 48:64].astype(f32) + hi[...].astype(f32)).astype(bf16)
        self.put(10, self.gp, 0, 64, dp)
        self.got(7, dp)
        self.add(7, self.own_o, 0, 32)
        self.got(8, dm)
        self.add(8, self.own_o, 0, 32)
        self.s.send(12, self.part.at[self.own_o], self.slot(11), dy)
        self.got(9, dp)
        self.got(10, dm)
        self.s.recv(12, self.slot(11), dy)
        total = self.part[self.own].astype(f32) + self.slot(9)[...].astype(f32)
        return total + self.slot(10)[...].astype(f32) + self.slot(11)[...].astype(f32)


SUMW_ROWS = sum(SumW.LAND)
SUMW_SEMS = 13


def t_devices(me):
    return (
        {"x": shifted(me, "x", 1)},
        {"x": shifted(me, "x", 3)},
        {"t": 1 - me["t"]},
        {"c": 1 - me["c"]},
    )


class GatherT:
    KINDS = 19

    def __init__(self, me, dst, sends):
        self.dst, self.s = dst, sends
        x, c, t = me["x"], me["c"], me["t"]
        xp, xm, xo = shifted(me, "x", 1), shifted(me, "x", 3), shifted(me, "x", 2)

        def at(x, t, c=c):
            return (x * 2 + c) * 2 + t

        to = 1 - t
        self.ids = {
            "own": at(x, t), "to": at(x, to), "p": at(xp, t), "po": at(xp, to),
            "m": at(xm, t), "mo": at(xm, to), "o": at(xo, t), "oo": at(xo, to),
        }
        self.sib = {k: v + 2 * (1 - 2 * c) for k, v in self.ids.items()}
        self.dp, self.dm, self.dt, self.dc = t_devices(me)

    def part(self, s, half):
        lo, hi = {None: (0, 8), 0: (0, 4), 1: (4, 8)}[half]
        return self.dst.at[lo:hi, s]

    def put(self, kind, name, device, half=None):
        s = self.ids[name]
        self.s.send(kind, self.part(s, half), self.part(s, half), device)

    def got(self, kind, name, device, half=None, sib=False):
        s = (self.sib if sib else self.ids)[name]
        self.s.recv(kind, self.part(s, half), device)

    def start(self):
        self.put(2, "own", self.dt)
        self.put(0, "own", self.dp)
        self.put(1, "own", self.dm)
        self.put(3, "own", self.dc)

    def middle(self):
        dp, dm, dt, dc = self.dp, self.dm, self.dt, self.dc
        self.got(0, "m", dm)
        self.put(7, "m", dp, 0)
        self.put(8, "m", dc)
        self.got(1, "p", dp)
        self.put(9, "p", dm, 1)
        self.put(10, "p", dc)
        self.got(2, "to", dt)
        self.put(4, "to", dp)
        self.put(5, "to", dm)
        self.put(6, "to", dc)

    def end(self):
        dp, dm, dt, dc = self.dp, self.dm, self.dt, self.dc
        self.got(7, "o", dm, 0)
        self.put(15, "o", dc, 0)
        self.got(9, "o", dp, 1)
        self.put(16, "o", dc, 1)
        self.got(4, "mo", dm)
        self.put(11, "mo", dp, 0)
        self.put(12, "mo", dc)
        self.got(5, "po", dp)
        self.put(13, "po", dm, 1)
        self.put(14, "po", dc)
        self.got(11, "oo", dm, 0)
        self.put(17, "oo", dc, 0)
        self.got(13, "oo", dp, 1)
        self.put(18, "oo", dc, 1)
        for kind, name, half in (
            (3, "own", None), (8, "m", None), (10, "p", None), (6, "to", None), (15, "o", 0), (16, "o", 1),
            (12, "mo", None), (14, "po", None), (17, "oo", 0), (18, "oo", 1),
        ):
            self.got(kind, name, dc, half, True)


def sems(n):
    return [DMA((n,)), DMA((n,))]


def spread_kernel(normed_ref, stage_ref, normed_all, weights, rest, ssem, rsem, local):
    me = place()
    z, y, t = me["z"], me["yl"], me["t"]
    own_g = 2 * z + y
    s = (me["x"] * 2 + me["c"]) * 2 + t
    dp, dm, dy = w_devices(me)
    sem = pltpu.get_barrier_semaphore()
    for dz in range(4):
        for dyl in range(2):
            for dt in range(2):
                if dz or dyl or dt:
                    pl.semaphore_signal(
                        sem, inc=1, device_id_type=MESH,
                        device_id={
                            "z": shifted(me, "z", dz), "yl": shifted(me, "yl", dyl), "t": shifted(me, "t", dt)
                        },
                    )
    for d in t_devices(me)[:2] + t_devices(me)[3:]:
        pl.semaphore_signal(sem, inc=1, device_id=d, device_id_type=MESH)
    pl.semaphore_wait(sem, 18)

    mine = pltpu.make_async_copy(normed_ref, normed_all.at[own_g], local.at[0])
    mine.start()
    base_b = GatherW.KINDS
    base_c = base_b + 8
    for j in range(4):
        for t2 in range(2):
            g = 4 * t + j
            dst_z, dst_y = 2 * t + j // 2, j % 2
            is_me = (dst_z == z) & (dst_y == y) & (t == t2)
            src = stage_ref.at[j, 16 * t2 : 16 * t2 + 16]
            to = {"z": dst_z, "yl": dst_y, "t": jnp.int32(t2)}
            qk = remote(
                src.at[:, :QKV], weights.at[own_g, s - t + t2], ssem.at[base_b + j * 2 + t2],
                rsem.at[base_b + own_g], to,
            )
            ot = remote(
                src.at[:, QKV:], rest.at[own_g], ssem.at[base_c + j * 2 + t2], rsem.at[base_c + own_g], to,
            )
            lq = pltpu.make_async_copy(src.at[:, :QKV], weights.at[own_g, s], local.at[1])
            lo = pltpu.make_async_copy(src.at[:, QKV:], rest.at[own_g], local.at[2])

            @pl.when(is_me)
            def _():
                lq.start()
                lo.start()
                lq.wait()
                lo.wait()

            @pl.when(jnp.logical_not(is_me))
            def _():
                qk.start()
                ot.start()

    mine.wait()
    gw = GatherW(me, normed_all, Sends(ssem, rsem))
    gw.start()
    holder = own_g // 4
    for g in range(8):
        from_me = (own_g == g) & (holder == t)

        @pl.when(jnp.logical_not(from_me))
        def _(g=g):
            dst = weights.at[g, s]
            remote(dst, dst, ssem.at[0], rsem.at[base_b + g], dy).wait_recv()

    gt = GatherT(me, weights, Sends(ssem, rsem, base_c + 8))
    gt.start()
    gw.middle()
    gt.middle()
    gw.end()
    gt.end()
    for g in range(8):
        from_me = (own_g == g) & (holder == t)

        @pl.when(jnp.logical_not(from_me))
        def _(g=g):
            dst = rest.at[g]
            remote(dst, dst, ssem.at[0], rsem.at[base_c + g], dy).wait_recv()

    for j in range(4):
        for t2 in range(2):
            is_me = (2 * t + j // 2 == z) & (j % 2 == y) & (t == t2)

            @pl.when(jnp.logical_not(is_me))
            def _(j=j, t2=t2):
                src = stage_ref.at[j, 16 * t2 : 16 * t2 + 16]
                k = j * 2 + t2
                remote(src.at[:, :QKV], src.at[:, :QKV], ssem.at[base_b + k], rsem.at[0], dy).wait_send()
                remote(src.at[:, QKV:], src.at[:, QKV:], ssem.at[base_c + k], rsem.at[0], dy).wait_send()

    gw.s.close()
    gt.s.close()


def spread(normed, stage):
    n = GatherW.KINDS + 16 + GatherT.KINDS
    return pl.pallas_call(
        spread_kernel,
        out_shape=(
            jax.ShapeDtypeStruct((NW, ROWS, D), bf16),
            jax.ShapeDtypeStruct((NW, NT, 16, QKV), bf16),
            jax.ShapeDtypeStruct((NW, 16, COLS - QKV), bf16),
        ),
        in_specs=[VM, VM],
        out_specs=(VM, VM, VM),
        scratch_shapes=sems(n) + [DMA((3,))],
        compiler_params=params(0),
        name="spread",
    )(normed, stage)


def gather_kernel(x_ref, out, ssem, rsem, local):
    me = place()
    barrier(w_devices(me))
    mine = pltpu.make_async_copy(x_ref, out.at[2 * me["z"] + me["yl"]], local)
    mine.start()
    mine.wait()
    g = GatherW(me, out, Sends(ssem, rsem))
    g.start()
    g.middle()
    g.end()
    g.s.close()


def gather_rows(x, cid):
    out = pl.pallas_call(
        gather_kernel,
        out_shape=jax.ShapeDtypeStruct((NW,) + x.shape, x.dtype),
        in_specs=[VM],
        out_specs=VM,
        scratch_shapes=sems(GatherW.KINDS) + [DMA(())],
        compiler_params=params(cid),
        name="gather_rows",
    )(x)
    return out.reshape(TOK, x.shape[1])


def keys_kernel(kv_ref, cot_ref, kv_all, cot_all, ssem, rsem, local):
    me = place()
    barrier(t_devices(me) + w_devices(me))
    s = (me["x"] * 2 + me["c"]) * 2 + me["t"]
    a = pltpu.make_async_copy(kv_ref, kv_all.at[:, s], local.at[0])
    b = pltpu.make_async_copy(cot_ref, cot_all.at[2 * me["z"] + me["yl"]], local.at[1])
    a.start()
    b.start()
    a.wait()
    b.wait()
    gt = GatherT(me, kv_all, Sends(ssem, rsem))
    gw = GatherW(me, cot_all, Sends(ssem, rsem, GatherT.KINDS))
    gt.start()
    gw.start()
    gt.middle()
    gw.middle()
    gt.end()
    gw.end()
    gt.s.close()
    gw.s.close()


def gather_keys(kv, cot, cid):
    n = GatherT.KINDS + GatherW.KINDS
    kv_all, cot_all = pl.pallas_call(
        keys_kernel,
        out_shape=(
            jax.ShapeDtypeStruct((NW, NT, ROWS, 2 * KC), bf16),
            jax.ShapeDtypeStruct((NW, ROWS, D), bf16),
        ),
        in_specs=[VM, VM],
        out_specs=(VM, VM),
        scratch_shapes=sems(n) + [DMA((2,))],
        compiler_params=params(cid),
        name="gather_keys",
    )(kv.reshape(NW, ROWS, 2 * KC), cot)
    return kv_all.reshape(SEQ, 2 * KC), cot_all.reshape(TOK, D)


def sum_kernel(x_ref, out, part, land, ssem, rsem, local):
    me = place()
    barrier(w_devices(me))
    c = pltpu.make_async_copy(x_ref, part, local)
    c.start()
    c.wait()
    s = SumW(me, part, land, Sends(ssem, rsem))
    out[...] = s.run()
    s.s.close()


def sum_rows(x, cid):
    return pl.pallas_call(
        sum_kernel,
        out_shape=jax.ShapeDtypeStruct((ROWS, D), f32),
        in_specs=[VM],
        out_specs=VM,
        scratch_shapes=[pltpu.VMEM((NW, ROWS, D), bf16), pltpu.VMEM((SUMW_ROWS, D), bf16)]
        + sems(SUMW_SEMS) + [DMA(())],
        compiler_params=params(cid),
        name="sum_rows",
    )(x.astype(bf16).reshape(NW, ROWS, D))


def sum_keys_kernel(x_ref, out, part, half, land, final, ssem, rsem, local):
    me = place()
    barrier(t_devices(me))
    x, c, t = me["x"], me["c"], me["t"]
    xp, xm, xo = shifted(me, "x", 1), shifted(me, "x", 3), shifted(me, "x", 2)
    dp, dm, dt, dc = t_devices(me)
    s = Sends(ssem, rsem)
    order = (xo, xm, xp, x)
    for i, xi in enumerate(order):
        s.send(i, x_ref.at[:, xi, 1 - c], part.at[i], dc)
    for i, xi in enumerate(order):
        s.recv(i, part.at[i], dc)
        part[i] = (part[i].astype(f32) + x_ref[:, xi, c].astype(f32)).astype(bf16)
        if i == 0:
            s.send(4, part.at[0, 0:4], half.at[0], dm)
            s.send(5, part.at[0, 4:8], half.at[1], dp)
        if i == 1:
            s.recv(4, half.at[0], dp)
            part[1, 0:4] = (part[1, 0:4].astype(f32) + half[0].astype(f32)).astype(bf16)
            s.send(6, part.at[1], land.at[0], dm)
        if i == 2:
            s.recv(5, half.at[1], dm)
            part[2, 4:8] = (part[2, 4:8].astype(f32) + half[1].astype(f32)).astype(bf16)
            s.send(7, part.at[2], land.at[1], dp)
    s.recv(6, land.at[0], dp)
    s.recv(7, land.at[1], dm)
    to = 1 - t
    part[3, :, to] = (
        part[3, :, to].astype(f32) + land[0, :, to].astype(f32) + land[1, :, to].astype(f32)
    ).astype(bf16)
    s.send(8, part.at[3, :, to], final, dt)
    own = part[3, :, t].astype(f32) + land[0, :, t].astype(f32) + land[1, :, t].astype(f32)
    s.recv(8, final, dt)
    out[...] = own + final[...].astype(f32)
    s.close()


def sum_keys(x, cid):
    out = pl.pallas_call(
        sum_keys_kernel,
        out_shape=jax.ShapeDtypeStruct((NW, ROWS, 2 * KC), f32),
        in_specs=[VM],
        out_specs=VM,
        scratch_shapes=[
            pltpu.VMEM((4, NW, 2, ROWS, 2 * KC), bf16),
            pltpu.VMEM((2, 4, 2, ROWS, 2 * KC), bf16),
            pltpu.VMEM((2, NW, 2, ROWS, 2 * KC), bf16),
            pltpu.VMEM((NW, ROWS, 2 * KC), bf16),
        ]
        + sems(9) + [DMA(())],
        compiler_params=params(cid),
        name="sum_keys",
    )(x.reshape(NW, 4, 2, 2, ROWS, 2 * KC))
    return out.reshape(TOK, 2 * KC)


def return_kernel(x_ref, out, ssem, rsem, local):
    me = place()
    z, y, t = me["z"], me["yl"], me["t"]
    own_g = 2 * z + y
    sem = pltpu.get_barrier_semaphore()
    for dz in range(4):
        for dyl in range(2):
            for dt in range(2):
                if dz or dyl or dt:
                    pl.semaphore_signal(
                        sem, inc=1, device_id_type=MESH,
                        device_id={
                            "z": shifted(me, "z", dz), "yl": shifted(me, "yl", dyl), "t": shifted(me, "t", dt)
                        },
                    )
    pl.semaphore_wait(sem, 15)
    holder = own_g // 4
    block = own_g - 4 * holder
    for g in range(8):
        is_me = (own_g == g) & (holder == t)
        dst = out.at[block, t]
        to = {"z": jnp.int32(g // 2), "yl": jnp.int32(g % 2), "t": holder}
        c = remote(x_ref.at[g], dst, ssem.at[g], rsem.at[block * 2 + t], to)
        l = pltpu.make_async_copy(x_ref.at[g], dst, local)

        @pl.when(is_me)
        def _():
            l.start()
            l.wait()

        @pl.when(jnp.logical_not(is_me))
        def _():
            c.start()

    dy = w_devices(me)[2]
    for j in range(4):
        for t2 in range(2):
            is_me = (2 * t + j // 2 == z) & (j % 2 == y) & (t == t2)

            @pl.when(jnp.logical_not(is_me))
            def _(j=j, t2=t2):
                d = out.at[j, t2]
                remote(d, d, ssem.at[0], rsem.at[j * 2 + t2], dy).wait_recv()

    for g in range(8):
        is_me = (own_g == g) & (holder == t)

        @pl.when(jnp.logical_not(is_me))
        def _(g=g):
            remote(x_ref.at[g], x_ref.at[g], ssem.at[g], rsem.at[0], dy).wait_send()


def return_weights(x, cid):
    cols = x.shape[-1]
    return pl.pallas_call(
        return_kernel,
        out_shape=jax.ShapeDtypeStruct((4, 2, 16, cols), x.dtype),
        in_specs=[VM],
        out_specs=VM,
        scratch_shapes=sems(8) + [DMA(())],
        compiler_params=params(cid),
        name="return_weights",
    )(x)


KB = 256
CH = 2 * ROWS
NROW = NW * CH


def attend_kernel(q_ref, kv_ref, o_ref, l_ref):
    s = (lax.axis_index("x") * 2 + lax.axis_index("c")) * 2 + lax.axis_index("t")
    o_ref[...] = jnp.zeros_like(o_ref)
    l_ref[...] = jnp.zeros_like(l_ref)
    factor = score_scale * LOG2E
    for g in range(NW):
        first = g * CH

        def block(b, carry, g=g, first=first):
            keys = pl.ds(pl.multiple_of(g * 1024 + b * KB, KB), KB)
            k = kv_ref[keys, :KC]
            v = kv_ref[keys, KC:]
            for r0 in range(first, NROW, 256):
                r1 = min(r0 + 256, NROW)
                sc = lax.dot_general(
                    q_ref[r0:r1], k, (((1,), (1,)), ((), ())), preferred_element_type=f32
                )
                p = jnp.exp2(sc * factor)
                if r0 == first:
                    row = lax.broadcasted_iota(jnp.int32, (r1 - r0, KB), 0)
                    col = lax.broadcasted_iota(jnp.int32, (r1 - r0, KB), 1)
                    seen = (row >= CH) | (s * ROWS + (row & (ROWS - 1)) >= b * KB + col)
                    p = jnp.where(seen, p, 0.0)
                l_ref[r0:r1] += p[:, :128] + p[:, 128:]
                o_ref[r0:r1] += jnp.dot(p.astype(bf16), v, preferred_element_type=f32)
            return carry

        lax.fori_loop(0, 1024 // KB, block, 0)


def attend(q, kv_all):
    return pl.pallas_call(
        attend_kernel,
        out_shape=(
            jax.ShapeDtypeStruct((NROW, HD), f32),
            jax.ShapeDtypeStruct((NROW, HD), f32),
        ),
        in_specs=[VM, VM],
        out_specs=(VM, VM),
        compiler_params=params(),
        name="attend",
    )(q, kv_all)


def attend_back_kernel(q_ref, do_ref, lse_ref, delta_ref, kv_ref, dq_ref, dkv_ref):
    s = (lax.axis_index("x") * 2 + lax.axis_index("c")) * 2 + lax.axis_index("t")
    dq_ref[...] = jnp.zeros_like(dq_ref)
    factor = score_scale * LOG2E
    for g in range(NW):
        first = g * CH

        def block(b, carry, g=g, first=first):
            keys = pl.ds(pl.multiple_of(g * 1024 + b * KB, KB), KB)
            k = kv_ref[keys, :KC]
            v = kv_ref[keys, KC:]
            dk = jnp.zeros((KB, HD), f32)
            dv = jnp.zeros((KB, HD), f32)
            for r0 in range(first, NROW, 256):
                r1 = min(r0 + 256, NROW)
                q = q_ref[r0:r1]
                do = do_ref[r0:r1]
                sc = lax.dot_general(k, q, (((1,), (1,)), ((), ())), preferred_element_type=f32)
                p = jnp.exp2(sc * factor - lse_ref[:, r0:r1])
                if r0 == first:
                    row = lax.broadcasted_iota(jnp.int32, (KB, r1 - r0), 1)
                    col = lax.broadcasted_iota(jnp.int32, (KB, r1 - r0), 0)
                    seen = (row >= CH) | (s * ROWS + (row & (ROWS - 1)) >= b * KB + col)
                    p = jnp.where(seen, p, 0.0)
                dp = lax.dot_general(v, do, (((1,), (1,)), ((), ())), preferred_element_type=f32)
                ds = (p * (dp - delta_ref[:, r0:r1])).astype(bf16)
                dv = dv + jnp.dot(p.astype(bf16), do, preferred_element_type=f32)
                dk = dk + jnp.dot(ds, q, preferred_element_type=f32)
                dq_ref[r0:r1] += lax.dot_general(
                    ds, k, (((0,), (0,)), ((), ())), preferred_element_type=f32
                )
            dkv_ref[keys, :KC] = (dk * score_scale).astype(bf16)
            dkv_ref[keys, KC:] = dv.astype(bf16)
            return carry

        lax.fori_loop(0, 1024 // KB, block, 0)


def attend_back(q, do, lse, delta, kv_all):
    return pl.pallas_call(
        attend_back_kernel,
        out_shape=(
            jax.ShapeDtypeStruct((NROW, HD), f32),
            jax.ShapeDtypeStruct((SEQ, 2 * KC), bf16),
        ),
        in_specs=[VM] * 5,
        out_specs=(VM, VM),
        compiler_params=params(),
        name="attend_back",
    )(q, do, lse, delta, kv_all)


def rotate(value_rows, cosine, sine_table):
    middle = value_rows.shape[-1] // 2
    first_half = value_rows[..., :middle]
    second_half = value_rows[..., middle:]
    return jnp.concatenate(
        [
            first_half * cosine - second_half * sine_table,
            second_half * cosine + first_half * sine_table,
        ],
        axis=-1,
    )


def norm_forward(value_rows):
    inverse = lax.rsqrt(jnp.mean(value_rows * value_rows, axis=-1, keepdims=True) + epsilon)
    return (value_rows * inverse, inverse)


def norm_backward(upstream, normal, inverse, gain):
    scaled = upstream * gain
    return inverse * (scaled - normal * jnp.mean(scaled * normal, axis=-1, keepdims=True))


def cross_rows(left_side, right_side):
    return lax.dot_general(
        left_side, right_side, (((1,), (1,)), ((), ())), preferred_element_type=f32
    )


def over_tokens(left_side, right_side):
    return lax.dot_general(
        left_side, right_side, (((0,), (0,)), ((), ())), preferred_element_type=f32
    ).astype(bf16)


def to_rows(v):
    return v.reshape(NW, ROWS, 2, HD).transpose(0, 2, 1, 3).reshape(NROW, HD)


def from_rows(v):
    return v.reshape(NW, 2, ROWS, HD).transpose(0, 2, 1, 3).reshape(TOK, 2 * HD)


def gather_weight(w):
    return lax.all_gather(w, T_AXES, axis=1, tiled=True).reshape(D, w.shape[-1])


def scatter_weight(w):
    return lax.psum_scatter(w.reshape(NW, NT * 16, -1), T_AXES, scatter_dimension=1, tiled=True)


def local(
    tokens, norm_gain, w_query, key_matrix, value_matrix, query_gain, key_gain, w_out, ffn_gain,
    w_gate, w_up, w_down, cotangent,
):
    s = (lax.axis_index("x") * 2 + lax.axis_index("c")) * 2 + lax.axis_index("t")
    state = tokens.astype(f32)
    normal_one, inverse_one = norm_forward(state)
    normalized_input = (normal_one * norm_gain).astype(bf16)
    stage = jnp.concatenate(
        [
            w.reshape(32, 4, -1)
            for w in (w_query, key_matrix, value_matrix, w_out, w_gate, w_up, w_down)
        ],
        axis=2,
    ).transpose(1, 0, 2)
    normed_all, qkv, rest = spread(normalized_input, stage)
    normed_all = normed_all.reshape(TOK, D)
    qkv = qkv.reshape(D, QKV)
    out_w = gather_weight(rest[:, :, :QC])
    gate_up_w = gather_weight(rest[:, :, QC : QC + 2 * FC])
    down_w = gather_weight(rest[:, :, QC + 2 * FC :])

    projected = jnp.dot(normed_all, qkv, preferred_element_type=f32)
    query_pre = projected[:, :QC].reshape(TOK, 2, HD)
    key_pre = projected[:, QC : QC + KC].reshape(TOK, 1, HD)
    value_bf = projected[:, QC + KC :].astype(bf16)
    at = jnp.arange(TOK, dtype=jnp.int32)
    position = (at // ROWS) * (NT * ROWS) + s * ROWS + at % ROWS
    exponent = jnp.arange(0, HD, 2, dtype=f32) / HD
    angles = position.astype(f32)[:, None] * (1.0 / rope_base**exponent)[None, :]
    cosine, sine_table = jnp.cos(angles)[:, None, :], jnp.sin(angles)[:, None, :]
    query_normal, query_inverse = norm_forward(query_pre)
    key_normal, key_inverse = norm_forward(key_pre)
    query_rot = rotate(query_normal * query_gain, cosine, sine_table).astype(bf16)
    key_rot = rotate(key_normal * key_gain, cosine, sine_table).astype(bf16)
    packed = jnp.concatenate([key_rot.reshape(TOK, KC), value_bf], axis=1)
    kv_all, grad_all = gather_keys(packed, cotangent, 1)
    query_rows = to_rows(query_rot)
    raw, sums = attend(query_rows, kv_all)
    total = jnp.sum(sums, axis=1, keepdims=True)
    attended_rows = raw / total
    lse2 = jnp.log2(total).reshape(1, NROW)
    context_bf = from_rows(attended_rows).astype(bf16)
    middle_state = state + sum_rows(cross_rows(context_bf, out_w), 2)
    normal_two, inverse_two = norm_forward(middle_state)
    normed_two = (normal_two * ffn_gain).astype(bf16)
    normed_two_all = gather_rows(normed_two, 3)
    gate_up = jnp.dot(normed_two_all, gate_up_w, preferred_element_type=f32)
    gate_value = gate_up[:, :FC]
    upward = gate_up[:, FC:]
    sigmoid_gate = jax.nn.sigmoid(gate_value)
    activated = gate_value * sigmoid_gate
    hidden = (activated * upward).astype(bf16)
    grad_hidden = jnp.dot(grad_all, down_w, preferred_element_type=f32)
    grad_gate = grad_hidden * upward * (sigmoid_gate * (1.0 + gate_value * (1.0 - sigmoid_gate)))
    grad_upward = grad_hidden * activated
    grad_gate_up = jnp.concatenate([grad_gate, grad_upward], axis=1).astype(bf16)
    grad_normed_two = sum_rows(cross_rows(grad_gate_up, gate_up_w), 4)
    result = (middle_state + sum_rows(cross_rows(hidden, down_w), 5)).astype(bf16)
    ffn_grads = scatter_weight(
        jnp.concatenate(
            [over_tokens(normed_two_all, grad_gate_up), over_tokens(grad_all, hidden)], axis=1
        )
    )
    grad_middle = cotangent.astype(f32) + norm_backward(
        grad_normed_two, normal_two, inverse_two, ffn_gain
    )
    gain_two = jnp.sum(grad_normed_two * normal_two, axis=0)
    grad_middle_all = gather_rows(grad_middle.astype(bf16), 6)
    grad_context = jnp.dot(grad_middle_all, out_w, preferred_element_type=f32).astype(bf16)
    grad_rows = to_rows(grad_context)
    delta = jnp.sum(grad_rows.astype(f32) * attended_rows, axis=1).reshape(1, NROW)
    grad_query_rows, grad_packed = attend_back(query_rows, grad_rows, lse2, delta, kv_all)
    grad_own = sum_keys(grad_packed, 7)
    grad_key_rot = grad_own[:, :KC].reshape(TOK, 1, HD)
    grad_value_bf = grad_own[:, KC:].astype(bf16)
    grad_query_rot = from_rows(grad_query_rows * score_scale).reshape(TOK, 2, HD)
    grad_query_norm = rotate(grad_query_rot, cosine, -sine_table)
    grad_key_norm = rotate(grad_key_rot, cosine, -sine_table)
    gain_query = jnp.sum(grad_query_norm * query_normal, axis=(0, 1))
    gain_key = jnp.sum(grad_key_norm * key_normal, axis=(0, 1))
    grad_query_pre = norm_backward(
        grad_query_norm, query_normal, query_inverse, query_gain
    ).reshape(TOK, QC)
    grad_key_pre = norm_backward(grad_key_norm, key_normal, key_inverse, key_gain).reshape(TOK, KC)
    grad_projected = jnp.concatenate(
        [grad_query_pre.astype(bf16), grad_key_pre.astype(bf16), grad_value_bf], axis=1
    )
    grad_normed = sum_rows(cross_rows(grad_projected, qkv), 8)
    grad_input = grad_middle + norm_backward(grad_normed, normal_one, inverse_one, norm_gain)
    gain_one = jnp.sum(grad_normed * normal_one, axis=0)
    attn_grads = scatter_weight(
        jnp.concatenate(
            [over_tokens(normed_all, grad_projected), over_tokens(grad_middle_all, context_bf)], axis=1
        )
    )
    back = return_weights(jnp.concatenate([attn_grads, ffn_grads], axis=2), 9)
    back = back.reshape(4, 32, COLS).transpose(1, 0, 2).astype(f32)
    cuts = [0]
    for w in (QC, KC, KC, QC, FC, FC, FC):
        cuts.append(cuts[-1] + w)
    grads = [back[:, :, a:b].reshape(32, -1) for a, b in zip(cuts[:-1], cuts[1:])]
    gain_one, gain_two, gain_query, gain_key = lax.psum(
        (gain_one, gain_two, gain_query, gain_key), AXES
    )
    return (
        result, grad_input, gain_one, grads[0], grads[1], grads[2], gain_query, gain_key, grads[3],
        gain_two, grads[4], grads[5], grads[6],
    )


def solution(mesh):
    fine = Mesh(mesh.devices.reshape(4, 2, 4, 2, 2), AXES)
    rows = P(AXES, None)
    weight = P(("z", "yl", "x", "c"), "t")
    return jax.shard_map(
        local,
        mesh=fine,
        in_specs=(rows, P(), weight, weight, weight, P(), P(), weight, P(), weight, weight, weight, rows),
        out_specs=(
            rows, rows, P(), weight, weight, weight, P(), P(), weight, P(), weight, weight, weight,
        ),
        check_vma=False,
    )
```

```python
import functools

import jax
import jax.numpy as jnp
from jax import lax
from jax.experimental import pallas as pl
from jax.experimental.pallas import tpu as pltpu
from jax.sharding import Mesh
from jax.sharding import PartitionSpec as P

AXES = ("z", "yl", "x", "c", "t")
SIZES = {"z": 4, "yl": 2, "x": 4, "c": 2, "t": 2}
W_AXES = ("z", "yl")
T_AXES = ("x", "c", "t")
NW, NT = 8, 16
ROWS = 64
TOK = NW * ROWS
D = 2048
HD = 128
SEQ = 8192
QC, KC, FC = 256, 128, 768
QKV = QC + 2 * KC
COLS = QKV + QC + 3 * FC
VMEM_LIMIT = 60 << 20
KB = 256
CH = 2 * ROWS
NROW = NW * CH

epsilon = 1e-06
rope_base = 1000000.0
score_scale = HD ** (-0.5)
LOG2E = 1.4426950408889634

bf16 = jnp.bfloat16
f32 = jnp.float32
MESH = pl.DeviceIdType.MESH
VM = pl.BlockSpec(memory_space=pltpu.VMEM)
ANY = pl.BlockSpec(memory_space=pl.ANY)
DMA = pltpu.SemaphoreType.DMA


def params(cid=None):
    if cid is None:
        return pltpu.CompilerParams(vmem_limit_bytes=VMEM_LIMIT)
    return pltpu.CompilerParams(
        collective_id=cid, has_side_effects=True, vmem_limit_bytes=VMEM_LIMIT
    )


def place():
    return {a: lax.axis_index(a) for a in AXES}


def shifted(me, axis, by):
    return lax.rem(me[axis] + by, SIZES[axis])


def barrier(devices):
    sem = pltpu.get_barrier_semaphore()
    for d in devices:
        pl.semaphore_signal(sem, inc=1, device_id=d, device_id_type=MESH)
    pl.semaphore_wait(sem, len(devices))


def remote(src, dst, ssem, rsem, device):
    return pltpu.make_async_remote_copy(
        src_ref=src, dst_ref=dst, send_sem=ssem, recv_sem=rsem, device_id=device, device_id_type=MESH
    )


class Sends:
    def __init__(self, ssem, rsem, base=0):
        self.ssem, self.rsem, self.base, self.open = ssem, rsem, base, []

    def send(self, kind, src, dst, device):
        k = self.base + kind
        c = remote(src, dst, self.ssem.at[k], self.rsem.at[k], device)
        c.start()
        self.open.append(c)

    def recv(self, kind, dst, device):
        k = self.base + kind
        remote(dst, dst, self.ssem.at[k], self.rsem.at[k], device).wait_recv()

    def close(self):
        for c in self.open:
            c.wait_send()


def w_devices(me):
    return (
        {"z": shifted(me, "z", 1)},
        {"z": shifted(me, "z", 3)},
        {"yl": 1 - me["yl"]},
    )


class GatherW:
    KINDS = 14

    def __init__(self, me, dst, sends):
        self.me, self.dst, self.s = me, dst, sends
        z, y = me["z"], me["yl"]
        zp, zm, zo, yo = shifted(me, "z", 1), shifted(me, "z", 3), shifted(me, "z", 2), 1 - y
        self.own, self.own_o = 2 * z + y, 2 * z + yo
        self.gp, self.gpo = 2 * zp + y, 2 * zp + yo
        self.gm, self.gmo = 2 * zm + y, 2 * zm + yo
        self.go, self.goo = 2 * zo + y, 2 * zo + yo
        self.dp, self.dm, self.dy = w_devices(me)

    def part(self, g, lo, hi):
        return self.dst.at[g, lo:hi]

    def put(self, kind, g, lo, hi, device):
        self.s.send(kind, self.part(g, lo, hi), self.part(g, lo, hi), device)

    def got(self, kind, g, lo, hi, device):
        self.s.recv(kind, self.part(g, lo, hi), device)

    def start(self):
        self.put(0, self.own, 0, 64, self.dp)
        self.put(1, self.own, 0, 64, self.dm)
        self.put(2, self.own, 0, 64, self.dy)

    def middle(self):
        dp, dm, dy = self.dp, self.dm, self.dy
        self.got(2, self.own_o, 0, 64, dy)
        self.put(3, self.own_o, 0, 32, dp)
        self.put(4, self.own_o, 0, 32, dm)
        self.got(0, self.gm, 0, 64, dm)
        self.put(5, self.gm, 16, 48, dp)
        self.put(6, self.gm, 32, 64, dy)
        self.got(1, self.gp, 0, 64, dp)
        self.put(7, self.gp, 0, 16, dm)
        self.put(8, self.gp, 48, 64, dm)
        self.put(9, self.gp, 32, 64, dy)

    def end(self):
        dp, dm, dy = self.dp, self.dm, self.dy
        self.got(3, self.gmo, 0, 32, dm)
        self.put(10, self.gmo, 16, 32, dp)
        self.got(4, self.gpo, 0, 32, dp)
        self.put(11, self.gpo, 0, 16, dm)
        self.got(5, self.go, 16, 48, dm)
        self.put(12, self.go, 32, 48, dy)
        self.got(8, self.go, 48, 64, dp)
        self.put(13, self.go, 48, 64, dy)
        self.got(7, self.go, 0, 16, dp)
        self.got(6, self.gmo, 32, 64, dy)
        self.got(9, self.gpo, 32, 64, dy)
        self.got(10, self.goo, 16, 32, dm)
        self.got(11, self.goo, 0, 16, dp)
        self.got(12, self.goo, 32, 48, dy)
        self.got(13, self.goo, 48, 64, dy)


class SumW:
    KINDS = 11
    LAND = (32, 32, 32, 16, 16, 32, 32, 32, 32, 64, 64, 64)

    def __init__(self, me, part, land, sends):
        self.part, self.land, self.s = part, land, sends
        z, y = me["z"], me["yl"]
        zp, zm, zo, yo = shifted(me, "z", 1), shifted(me, "z", 3), shifted(me, "z", 2), 1 - y
        self.own, self.own_o = 2 * z + y, 2 * z + yo
        self.gp, self.gpo = 2 * zp + y, 2 * zp + yo
        self.gm, self.gmo = 2 * zm + y, 2 * zm + yo
        self.go, self.goo = 2 * zo + y, 2 * zo + yo
        self.dp, self.dm, self.dy = w_devices(me)
        self.offset = [sum(self.LAND[:k]) for k in range(len(self.LAND))]

    def slot(self, kind, lo=0, n=None):
        n = self.LAND[kind] if n is None else n
        return self.land.at[self.offset[kind] + lo : self.offset[kind] + lo + n]

    def put(self, kind, g, lo, hi, device):
        self.s.send(kind, self.part.at[g, lo:hi], self.slot(kind), device)

    def got(self, kind, device):
        self.s.recv(kind, self.slot(kind), device)

    def add(self, kind, g, lo, hi):
        rows = self.slot(kind)
        self.part[g, lo:hi] = (self.part[g, lo:hi].astype(f32) + rows[...].astype(f32)).astype(bf16)

    def leaf(self):
        dp, dm, dy = self.dp, self.dm, self.dy
        self.put(0, self.goo, 32, 64, dy)
        self.put(3, self.goo, 16, 32, dm)
        self.put(4, self.goo, 0, 16, dp)
        self.put(1, self.gmo, 32, 64, dy)
        self.put(2, self.gpo, 32, 64, dy)

    def two(self):
        dp, dm, dy = self.dp, self.dm, self.dy
        self.got(0, dy)
        self.add(0, self.go, 32, 64)
        self.put(5, self.go, 16, 48, dm)
        self.s.send(6, self.part.at[self.go, 0:16], self.slot(6, 0, 16), dp)
        self.s.send(11, self.part.at[self.go, 48:64], self.slot(6, 16, 16), dp)
        self.got(3, dp)
        self.add(3, self.gmo, 16, 32)
        self.put(7, self.gmo, 0, 32, dm)
        self.got(4, dm)
        self.add(4, self.gpo, 0, 16)
        self.put(8, self.gpo, 0, 32, dp)

    def three(self):
        dp, dm, dy = self.dp, self.dm, self.dy
        self.got(1, dy)
        self.add(1, self.gm, 32, 64)
        self.got(5, dp)
        self.add(5, self.gm, 16, 48)
        self.put(9, self.gm, 0, 64, dm)
        self.got(2, dy)
        self.add(2, self.gp, 32, 64)
        self.s.recv(6, self.slot(6, 0, 16), dm)
        self.s.recv(11, self.slot(6, 16, 16), dm)
        for lo, hi, at in ((0, 16, 0), (48, 64, 16)):
            rows = self.slot(6, at, 16)
            self.part[self.gp, lo:hi] = (
                self.part[self.gp, lo:hi].astype(f32) + rows[...].astype(f32)
            ).astype(bf16)
        self.put(10, self.gp, 0, 64, dp)
        self.got(7, dp)
        self.add(7, self.own_o, 0, 32)
        self.got(8, dm)
        self.add(8, self.own_o, 0, 32)
        self.s.send(12, self.part.at[self.own_o], self.slot(11), dy)

    def total(self):
        dp, dm, dy = self.dp, self.dm, self.dy
        self.got(9, dp)
        self.got(10, dm)
        self.s.recv(12, self.slot(11), dy)
        total = self.part[self.own].astype(f32) + self.slot(9)[...].astype(f32)
        return total + self.slot(10)[...].astype(f32) + self.slot(11)[...].astype(f32)

    def run(self):
        self.leaf()
        self.two()
        self.three()
        return self.total()


SUMW_ROWS = sum(SumW.LAND)
SUMW_SEMS = 13


def t_devices(me):
    return (
        {"x": shifted(me, "x", 1)},
        {"x": shifted(me, "x", 3)},
        {"t": 1 - me["t"]},
        {"c": 1 - me["c"]},
    )


class GatherT:
    KINDS = 19

    def __init__(self, me, dst, sends):
        self.dst, self.s = dst, sends
        x, c, t = me["x"], me["c"], me["t"]
        xp, xm, xo = shifted(me, "x", 1), shifted(me, "x", 3), shifted(me, "x", 2)

        def at(x, t, c=c):
            return (x * 2 + c) * 2 + t

        to = 1 - t
        self.ids = {
            "own": at(x, t), "to": at(x, to), "p": at(xp, t), "po": at(xp, to),
            "m": at(xm, t), "mo": at(xm, to), "o": at(xo, t), "oo": at(xo, to),
        }
        self.sib = {k: v + 2 * (1 - 2 * c) for k, v in self.ids.items()}
        self.dp, self.dm, self.dt, self.dc = t_devices(me)

    def part(self, s, half):
        lo, hi = {None: (0, 8), 0: (0, 4), 1: (4, 8)}[half]
        return self.dst.at[lo:hi, s]

    def put(self, kind, name, device, half=None):
        s = self.ids[name]
        self.s.send(kind, self.part(s, half), self.part(s, half), device)

    def got(self, kind, name, device, half=None, sib=False):
        s = (self.sib if sib else self.ids)[name]
        self.s.recv(kind, self.part(s, half), device)

    def start(self):
        self.put(2, "own", self.dt)
        self.put(0, "own", self.dp)
        self.put(1, "own", self.dm)
        self.put(3, "own", self.dc)

    def middle(self):
        dp, dm, dt, dc = self.dp, self.dm, self.dt, self.dc
        self.got(0, "m", dm)
        self.put(7, "m", dp, 0)
        self.put(8, "m", dc)
        self.got(1, "p", dp)
        self.put(9, "p", dm, 1)
        self.put(10, "p", dc)
        self.got(2, "to", dt)
        self.put(4, "to", dp)
        self.put(5, "to", dm)
        self.put(6, "to", dc)

    def end(self):
        dp, dm, dt, dc = self.dp, self.dm, self.dt, self.dc
        self.got(7, "o", dm, 0)
        self.put(15, "o", dc, 0)
        self.got(9, "o", dp, 1)
        self.put(16, "o", dc, 1)
        self.got(4, "mo", dm)
        self.put(11, "mo", dp, 0)
        self.put(12, "mo", dc)
        self.got(5, "po", dp)
        self.put(13, "po", dm, 1)
        self.put(14, "po", dc)
        self.got(11, "oo", dm, 0)
        self.put(17, "oo", dc, 0)
        self.got(13, "oo", dp, 1)
        self.put(18, "oo", dc, 1)
        for kind, name, half in (
            (3, "own", None), (8, "m", None), (10, "p", None), (6, "to", None), (15, "o", 0), (16, "o", 1),
            (12, "mo", None), (14, "po", None), (17, "oo", 0), (18, "oo", 1),
        ):
            self.got(kind, name, dc, half, True)


def sems(n):
    return [DMA((n,)), DMA((n,))]


GROUPS = (QKV, QC, 2 * FC, FC)
STARTS = (0, QKV, QKV + QC, QKV + QC + 2 * FC)
PARTIAL = 3 * FC


def rms(v):
    return lax.rsqrt(jnp.mean(v * v, axis=-1, keepdims=True) + epsilon)


def mul_rows(a, b):
    return lax.dot_general(a, b, (((1,), (1,)), ((), ())), preferred_element_type=f32)


def mul(a, b):
    return jnp.dot(a, b, preferred_element_type=f32)


def mul_tokens(a, b):
    return lax.dot_general(a, b, (((0,), (0,)), ((), ())), preferred_element_type=f32)


def row_sums(v):
    ones = jnp.ones((8, v.shape[1]), f32)
    return lax.dot_general(
        ones, v, (((1,), (1,)), ((), ())), preferred_element_type=f32, precision=lax.Precision.HIGHEST
    )[0:1]


def forward_kernel(
    tok, cot, ngain, fgain, qgain, kgain, cosr, sinr, wq, wk, wv, wo, wg, wu, wd,
    middle, grad_mid, gain_two, q_rows, do_rows, lse, delta, qk_pre, ctx, part_two, gm_all,
    kv_out, qkv_out, normed_out, partial,
    stage, normed_all, cot_all, nt_all, kv_all, wqkv, wout, wgu, wdn, part, land, o_acc, l_acc,
    gate, up, gh, hidden, dgu, buf, ssem, rsem, lsem,
):
    me = place()
    z, y, t = me["z"], me["yl"], me["t"]
    own_g = 2 * z + y
    s = (me["x"] * 2 + me["c"]) * 2 + t
    dp, dm, dy = w_devices(me)
    sem = pltpu.get_barrier_semaphore()
    for dz in range(4):
        for dyl in range(2):
            for dt in range(2):
                if dz or dyl or dt:
                    pl.semaphore_signal(
                        sem, inc=1, device_id_type=MESH,
                        device_id={
                            "z": shifted(me, "z", dz), "yl": shifted(me, "yl", dyl), "t": shifted(me, "t", dt)
                        },
                    )
    for d in t_devices(me)[:2] + t_devices(me)[3:]:
        pl.semaphore_signal(sem, inc=1, device_id=d, device_id_type=MESH)

    state = tok[...].astype(f32)
    normed_all[own_g] = (state * rms(state) * ngain[...]).astype(bf16)
    cot_all[own_g] = cot[...]
    at = 0
    for w in (wq, wk, wv, wo, wg, wu, wd):
        n = w.shape[1] // 4
        for j in range(4):
            stage[j, :, at : at + n] = w[:, j * n : (j + 1) * n]
        at += n
    pl.semaphore_wait(sem, 18)

    count = [0]

    def sends(n):
        base = count[0]
        count[0] += n
        return Sends(ssem, rsem, base)

    gw = GatherW(me, normed_all, sends(GatherW.KINDS))
    gw.start()

    full = (wqkv, wout, wgu, wdn)
    base = count[0]
    count[0] += 32
    holder = own_g // 4

    def to_holders(groups):
        for j in range(4):
            for t2 in range(2):
                dst_z, dst_y = 2 * t + j // 2, j % 2
                is_me = (dst_z == z) & (dst_y == y) & (t == t2)
                src = stage.at[j, 16 * t2 : 16 * t2 + 16]
                to = {"z": dst_z, "yl": dst_y, "t": jnp.int32(t2)}
                remotes, locals_ = [], []
                for k in groups:
                    piece = src.at[:, STARTS[k] : STARTS[k] + GROUPS[k]]
                    remotes.append(
                        remote(
                            piece, full[k].at[own_g, s - t + t2], ssem.at[base + 8 * k + 2 * j + t2],
                            rsem.at[base + 8 * k + own_g], to,
                        )
                    )
                    locals_.append(pltpu.make_async_copy(piece, full[k].at[own_g, s], lsem.at[k]))

                @pl.when(is_me)
                def _():
                    for c in locals_:
                        c.start()
                    for c in locals_:
                        c.wait()

                @pl.when(jnp.logical_not(is_me))
                def _():
                    for c in remotes:
                        c.start()

    def from_owners(groups):
        for g in range(8):
            from_me = (own_g == g) & (holder == t)

            @pl.when(jnp.logical_not(from_me))
            def _(g=g):
                for k in groups:
                    dst = full[k].at[g, s]
                    remote(dst, dst, ssem.at[0], rsem.at[base + 8 * k + g], dy).wait_recv()

    to_holders((0,))
    from_owners((0,))
    gq, go, gg, gd = [GatherT(me, w, sends(GatherT.KINDS)) for w in full]
    gq.start()
    gw.middle()
    to_holders((1, 2, 3))
    gq.middle()
    gw.end()
    gq.end()

    keep = [
        pltpu.make_async_copy(wqkv, qkv_out, lsem.at[4]),
        pltpu.make_async_copy(normed_all, normed_out, lsem.at[5]),
    ]
    for c in keep:
        c.start()

    for h in range(2):
        rows = slice(h * 256, h * 256 + 256)
        pre = mul(
            normed_all[4 * h : 4 * h + 4].reshape(256, D), wqkv[...].reshape(D, QKV)
        )
        qk_pre[rows] = pre[:, : QC + KC]
        cosine, sine = cosr[rows], sinr[rows]
        for head in range(3):
            u = pre[:, head * HD : head * HD + HD]
            n = u * rms(u) * (qgain if head < 2 else kgain)[...]
            rolled = jnp.concatenate([n[:, HD // 2 :], n[:, : HD // 2]], axis=1)
            rot = (n * cosine + rolled * sine).astype(bf16)
            for i in range(4):
                g = 4 * h + i
                piece = rot[i * ROWS : i * ROWS + ROWS]
                if head < 2:
                    q_rows[g * CH + head * ROWS : g * CH + head * ROWS + ROWS] = piece
                else:
                    kv_all[g, s, :, :KC] = piece
        val = pre[:, QC + KC :].astype(bf16)
        for i in range(4):
            kv_all[4 * h + i, s, :, KC:] = val[i * ROWS : i * ROWS + ROWS]

    gk = GatherT(me, kv_all, sends(GatherT.KINDS))
    gc = GatherW(me, cot_all, sends(GatherW.KINDS))
    gk.start()
    gc.start()
    from_owners((1, 2, 3))
    go.start()
    gg.start()
    gk.middle()
    gc.middle()
    gk.end()
    keep.append(pltpu.make_async_copy(kv_all, kv_out, lsem.at[6]))
    keep[-1].start()

    o_acc[...] = jnp.zeros_like(o_acc)
    l_acc[...] = jnp.zeros_like(l_acc)
    attend_blocks(range(0, 2), s, q_rows, kv_all, o_acc, l_acc)
    go.middle()
    gg.middle()
    gc.end()
    gd.start()
    attend_blocks(range(2, 8), s, q_rows, kv_all, o_acc, l_acc)
    go.end()
    gg.end()
    gd.middle()

    lse[...] = jnp.log2(row_sums(l_acc[...]))
    for g in range(NW):
        rows = slice(g * CH, g * CH + CH)
        o = o_acc[rows] / jnp.sum(l_acc[rows], axis=1, keepdims=True)
        o_acc[rows] = o
        ctx[g * ROWS : g * ROWS + ROWS, :HD] = o[:ROWS].astype(bf16)
        ctx[g * ROWS : g * ROWS + ROWS, HD:] = o[ROWS:].astype(bf16)
    for n in range(4):
        w = wout[2 * n : 2 * n + 2].reshape(512, QC)
        part[:, :, n * 512 : n * 512 + 512] = (
            mul_rows(ctx[...], w).astype(bf16).reshape(NW, ROWS, 512)
        )
    sw = SumW(me, part, land, sends(SUMW_SEMS))
    sw.leaf()
    sw.two()
    gd.end()
    for n in range(3):
        gh[:, n * 256 : n * 256 + 256] = mul(
            cot_all[...].reshape(TOK, D), wdn[:, :, :, n * 256 : n * 256 + 256].reshape(D, 256)
        )
    sw.three()
    mid = state + sw.total()
    middle[...] = mid
    nt_all[own_g] = (mid * rms(mid) * fgain[...]).astype(bf16)
    gn = GatherW(me, nt_all, sends(GatherW.KINDS))
    gn.start()
    gn.middle()
    gn.end()

    for n in range(3):
        cols = slice(n * 256, n * 256 + 256)
        nt = nt_all[...].reshape(TOK, D)
        gate[:, cols] = mul(nt, wgu[:, :, :, n * 256 : n * 256 + 256].reshape(D, 256))
        up[:, cols] = mul(nt, wgu[:, :, :, FC + n * 256 : FC + n * 256 + 256].reshape(D, 256))

    def units(i, carry):
        rows = pl.ds(pl.multiple_of(i * 64, 64), 64)
        gv, uv, hv = gate[rows], up[rows], gh[rows]
        sig = jax.nn.sigmoid(gv)
        act = gv * sig
        hidden[rows] = (act * uv).astype(bf16)
        dgu[rows, :FC] = (hv * uv * (sig * (1.0 + gv * (1.0 - sig)))).astype(bf16)
        dgu[rows, FC:] = (hv * act).astype(bf16)
        return carry

    lax.fori_loop(0, TOK // 64, units, 0)
    sw.s.close()
    for n in range(4):
        w = wgu[2 * n : 2 * n + 2].reshape(512, 2 * FC)
        part[:, :, n * 512 : n * 512 + 512] = (
            mul_rows(dgu[...], w).astype(bf16).reshape(NW, ROWS, 512)
        )
    sb = SumW(me, part, land, sends(SUMW_SEMS))
    sb.leaf()
    for n in range(4):
        w = wdn[2 * n : 2 * n + 2].reshape(512, FC)
        part_two[:, :, n * 512 : n * 512 + 512] = (
            mul_rows(hidden[...], w).astype(bf16).reshape(NW, ROWS, 512)
        )
    sb.two()

    def weight_grads(lo, hi):
        def step(g, carry):
            slot = lax.rem(g, 2)

            @pl.when(g >= 2)
            def _():
                pltpu.make_async_copy(buf.at[slot], partial.at[g - 2], lsem.at[7 + slot]).wait()

            cols = pl.ds(pl.multiple_of(g * 256, 256), 256)
            a = nt_all[:, :, cols].reshape(TOK, 256)
            for n in range(3):
                c = slice(n * 512, n * 512 + 512)
                buf[slot, :, c] = mul_tokens(a, dgu[:, c]).astype(bf16)
            b = cot_all[:, :, cols].reshape(TOK, 256)
            for n in range(3):
                c = slice(n * 256, n * 256 + 256)
                buf[slot, :, 2 * FC + n * 256 : 2 * FC + n * 256 + 256] = mul_tokens(
                    b, hidden[:, c]
                ).astype(bf16)
            pltpu.make_async_copy(buf.at[slot], partial.at[g], lsem.at[7 + slot]).start()
            return carry

        lax.fori_loop(lo, hi, step, 0)

    weight_grads(0, 2)
    sb.three()
    weight_grads(2, 4)
    gnt = sb.total()
    mid = middle[...]
    inv = rms(mid)
    normal = mid * inv
    gain_two[...] = jnp.sum(gnt * normal, axis=0, keepdims=True)
    scaled = gnt * fgain[...]
    gm = cot[...].astype(f32) + inv * (
        scaled - normal * jnp.mean(scaled * normal, axis=-1, keepdims=True)
    )
    grad_mid[...] = gm
    gm_all[own_g] = gm.astype(bf16)
    ga = GatherW(me, gm_all, sends(GatherW.KINDS))
    ga.start()
    weight_grads(4, 6)
    ga.middle()
    weight_grads(6, 8)
    ga.end()
    grad_ctx = mul(gm_all[...].reshape(TOK, D), wout[...].reshape(D, QC)).astype(bf16)
    for g in range(NW):
        for head in range(2):
            do_rows[g * CH + head * ROWS : g * CH + head * ROWS + ROWS] = grad_ctx[
                g * ROWS : g * ROWS + ROWS, head * HD : head * HD + HD
            ]
    delta[...] = row_sums(do_rows[...].astype(f32) * o_acc[...])

    for c in keep:
        c.wait()
    for slot in range(2):
        pltpu.make_async_copy(buf.at[slot], partial.at[6 + slot], lsem.at[7 + slot]).wait()
    for j in range(4):
        for t2 in range(2):
            is_me = (2 * t + j // 2 == z) & (j % 2 == y) & (t == t2)

            @pl.when(jnp.logical_not(is_me))
            def _(j=j, t2=t2):
                src = stage.at[j, 16 * t2 : 16 * t2 + 16]
                for k in range(4):
                    piece = src.at[:, STARTS[k] : STARTS[k] + GROUPS[k]]
                    remote(
                        piece, piece, ssem.at[base + 8 * k + 2 * j + t2], rsem.at[0], dy
                    ).wait_send()
    for g in (gw, gq, go, gg, gd, gk, gc, gn, sb, ga):
        g.s.close()
    assert count[0] == FORWARD_SEMS, count[0]


FORWARD_SEMS = 4 * GatherW.KINDS + 5 * GatherT.KINDS + 2 * SUMW_SEMS + 32


def forward(tok, cot, ngain, fgain, qgain, kgain, cosr, sinr, *weights):
    def out(shape, dtype):
        return jax.ShapeDtypeStruct(shape, dtype)

    def vmem(shape, dtype=bf16):
        return pltpu.VMEM(shape, dtype)

    return pl.pallas_call(
        forward_kernel,
        out_shape=(
            out((ROWS, D), f32), out((ROWS, D), f32), out((1, D), f32), out((NROW, HD), bf16), out((NROW, HD), bf16),
            out((1, NROW), f32), out((1, NROW), f32), out((TOK, QC + KC), f32), out((TOK, QC), bf16),
            out((NW, ROWS, D), bf16), out((NW, ROWS, D), bf16),
            out((NW, NT, ROWS, 2 * KC), bf16), out((NW, NT, 16, QKV), bf16), out((NW, ROWS, D), bf16),
            out((NW, 256, PARTIAL), bf16),
        ),
        in_specs=[VM] * 15,
        out_specs=(VM,) * 11 + (ANY,) * 4,
        scratch_shapes=[
            vmem((4, 32, COLS)), vmem((NW, ROWS, D)), vmem((NW, ROWS, D)), vmem((NW, ROWS, D)),
            vmem((NW, NT, ROWS, 2 * KC)), vmem((NW, NT, 16, QKV)), vmem((NW, NT, 16, QC)),
            vmem((NW, NT, 16, 2 * FC)), vmem((NW, NT, 16, FC)), vmem((NW, ROWS, D)),
            vmem((SUMW_ROWS, D)), vmem((NROW, HD), f32), vmem((NROW, HD), f32),
            vmem((TOK, FC), f32), vmem((TOK, FC), f32), vmem((TOK, FC), f32), vmem((TOK, FC)),
            vmem((TOK, 2 * FC)), vmem((2, 256, PARTIAL)),
        ]
        + sems(FORWARD_SEMS) + [DMA((9,))],
        compiler_params=params(0),
        name="forward",
    )(tok, cot, ngain, fgain, qgain, kgain, cosr, sinr, *weights)


def sum_kernel(x_ref, out, part, land, ssem, rsem, local):
    me = place()
    barrier(w_devices(me))
    c = pltpu.make_async_copy(x_ref, part, local)
    c.start()
    c.wait()
    s = SumW(me, part, land, Sends(ssem, rsem))
    out[...] = s.run()
    s.s.close()


def sum_rows(x, cid):
    return pl.pallas_call(
        sum_kernel,
        out_shape=jax.ShapeDtypeStruct((ROWS, D), f32),
        in_specs=[VM],
        out_specs=VM,
        scratch_shapes=[pltpu.VMEM((NW, ROWS, D), bf16), pltpu.VMEM((SUMW_ROWS, D), bf16)]
        + sems(SUMW_SEMS) + [DMA(())],
        compiler_params=params(cid),
        name="sum_rows",
    )(x.astype(bf16).reshape(NW, ROWS, D))


def sum_keys_kernel(x_ref, out, part, half, land, final, ssem, rsem, local):
    me = place()
    barrier(t_devices(me))
    x, c, t = me["x"], me["c"], me["t"]
    xp, xm, xo = shifted(me, "x", 1), shifted(me, "x", 3), shifted(me, "x", 2)
    dp, dm, dt, dc = t_devices(me)
    s = Sends(ssem, rsem)
    order = (xo, xm, xp, x)
    for i, xi in enumerate(order):
        s.send(i, x_ref.at[:, xi, 1 - c], part.at[i], dc)
    for i, xi in enumerate(order):
        s.recv(i, part.at[i], dc)
        part[i] = (part[i].astype(f32) + x_ref[:, xi, c].astype(f32)).astype(bf16)
        if i == 0:
            s.send(4, part.at[0, 0:4], half.at[0], dm)
            s.send(5, part.at[0, 4:8], half.at[1], dp)
        if i == 1:
            s.recv(4, half.at[0], dp)
            part[1, 0:4] = (part[1, 0:4].astype(f32) + half[0].astype(f32)).astype(bf16)
            s.send(6, part.at[1], land.at[0], dm)
        if i == 2:
            s.recv(5, half.at[1], dm)
            part[2, 4:8] = (part[2, 4:8].astype(f32) + half[1].astype(f32)).astype(bf16)
            s.send(7, part.at[2], land.at[1], dp)
    s.recv(6, land.at[0], dp)
    s.recv(7, land.at[1], dm)
    to = 1 - t
    part[3, :, to] = (
        part[3, :, to].astype(f32) + land[0, :, to].astype(f32) + land[1, :, to].astype(f32)
    ).astype(bf16)
    s.send(8, part.at[3, :, to], final, dt)
    own = part[3, :, t].astype(f32) + land[0, :, t].astype(f32) + land[1, :, t].astype(f32)
    s.recv(8, final, dt)
    out[...] = own + final[...].astype(f32)
    s.close()


def sum_keys(x, cid):
    out = pl.pallas_call(
        sum_keys_kernel,
        out_shape=jax.ShapeDtypeStruct((NW, ROWS, 2 * KC), f32),
        in_specs=[VM],
        out_specs=VM,
        scratch_shapes=[
            pltpu.VMEM((4, NW, 2, ROWS, 2 * KC), bf16),
            pltpu.VMEM((2, 4, 2, ROWS, 2 * KC), bf16),
            pltpu.VMEM((2, NW, 2, ROWS, 2 * KC), bf16),
            pltpu.VMEM((NW, ROWS, 2 * KC), bf16),
        ]
        + sems(9) + [DMA(())],
        compiler_params=params(cid),
        name="sum_keys",
    )(x.reshape(NW, 4, 2, 2, ROWS, 2 * KC))
    return out.reshape(TOK, 2 * KC)


def return_kernel(x_ref, out, ssem, rsem, local):
    me = place()
    z, y, t = me["z"], me["yl"], me["t"]
    own_g = 2 * z + y
    sem = pltpu.get_barrier_semaphore()
    for dz in range(4):
        for dyl in range(2):
            for dt in range(2):
                if dz or dyl or dt:
                    pl.semaphore_signal(
                        sem, inc=1, device_id_type=MESH,
                        device_id={
                            "z": shifted(me, "z", dz), "yl": shifted(me, "yl", dyl), "t": shifted(me, "t", dt)
                        },
                    )
    pl.semaphore_wait(sem, 15)
    holder = own_g // 4
    block = own_g - 4 * holder
    for g in range(8):
        is_me = (own_g == g) & (holder == t)
        dst = out.at[block, t]
        to = {"z": jnp.int32(g // 2), "yl": jnp.int32(g % 2), "t": holder}
        c = remote(x_ref.at[g], dst, ssem.at[g], rsem.at[block * 2 + t], to)
        l = pltpu.make_async_copy(x_ref.at[g], dst, local)

        @pl.when(is_me)
        def _():
            l.start()
            l.wait()

        @pl.when(jnp.logical_not(is_me))
        def _():
            c.start()

    dy = w_devices(me)[2]
    for j in range(4):
        for t2 in range(2):
            is_me = (2 * t + j // 2 == z) & (j % 2 == y) & (t == t2)

            @pl.when(jnp.logical_not(is_me))
            def _(j=j, t2=t2):
                d = out.at[j, t2]
                remote(d, d, ssem.at[0], rsem.at[j * 2 + t2], dy).wait_recv()

    for g in range(8):
        is_me = (own_g == g) & (holder == t)

        @pl.when(jnp.logical_not(is_me))
        def _(g=g):
            remote(x_ref.at[g], x_ref.at[g], ssem.at[g], rsem.at[0], dy).wait_send()


def return_weights(x, cid):
    cols = x.shape[-1]
    return pl.pallas_call(
        return_kernel,
        out_shape=jax.ShapeDtypeStruct((4, 2, 16, cols), x.dtype),
        in_specs=[VM],
        out_specs=VM,
        scratch_shapes=sems(8) + [DMA(())],
        compiler_params=params(cid),
        name="return_weights",
    )(x)


def attend_blocks(slabs, s, q_ref, kv_ref, o_ref, l_ref):
    factor = score_scale * LOG2E
    for g in slabs:
        first = g * CH

        def block(b, carry, g=g, first=first):
            pair = kv_ref[g, pl.ds(b * 4, 4)].reshape(KB, 2 * KC)
            k, v = pair[:, :KC], pair[:, KC:]
            for r0 in range(first, NROW, 256):
                r1 = min(r0 + 256, NROW)
                sc = mul_rows(q_ref[r0:r1], k)
                p = jnp.exp2(sc * factor)
                if r0 == first:
                    row = lax.broadcasted_iota(jnp.int32, (r1 - r0, KB), 0)
                    col = lax.broadcasted_iota(jnp.int32, (r1 - r0, KB), 1)
                    seen = (row >= CH) | (s * ROWS + (row & (ROWS - 1)) >= b * KB + col)
                    p = jnp.where(seen, p, 0.0)
                l_ref[r0:r1] += p[:, :128] + p[:, 128:]
                o_ref[r0:r1] += mul(p.astype(bf16), v)
            return carry

        lax.fori_loop(0, 1024 // KB, block, 0)


def attend_back_kernel(q_ref, do_ref, lse_ref, delta_ref, kv_ref, dq_ref, dkv_ref):
    s = (lax.axis_index("x") * 2 + lax.axis_index("c")) * 2 + lax.axis_index("t")
    dq_ref[...] = jnp.zeros_like(dq_ref)
    factor = score_scale * LOG2E
    for g in range(NW):
        first = g * CH

        def block(b, carry, g=g, first=first):
            keys = pl.ds(pl.multiple_of(g * 1024 + b * KB, KB), KB)
            k = kv_ref[keys, :KC]
            v = kv_ref[keys, KC:]
            dk = jnp.zeros((KB, HD), f32)
            dv = jnp.zeros((KB, HD), f32)
            for r0 in range(first, NROW, 256):
                r1 = min(r0 + 256, NROW)
                q = q_ref[r0:r1]
                do = do_ref[r0:r1]
                sc = lax.dot_general(k, q, (((1,), (1,)), ((), ())), preferred_element_type=f32)
                p = jnp.exp2(sc * factor - lse_ref[:, r0:r1])
                if r0 == first:
                    row = lax.broadcasted_iota(jnp.int32, (KB, r1 - r0), 1)
                    col = lax.broadcasted_iota(jnp.int32, (KB, r1 - r0), 0)
                    seen = (row >= CH) | (s * ROWS + (row & (ROWS - 1)) >= b * KB + col)
                    p = jnp.where(seen, p, 0.0)
                dp = lax.dot_general(v, do, (((1,), (1,)), ((), ())), preferred_element_type=f32)
                ds = (p * (dp - delta_ref[:, r0:r1])).astype(bf16)
                dv = dv + jnp.dot(p.astype(bf16), do, preferred_element_type=f32)
                dk = dk + jnp.dot(ds, q, preferred_element_type=f32)
                dq_ref[r0:r1] += lax.dot_general(
                    ds, k, (((0,), (0,)), ((), ())), preferred_element_type=f32
                )
            dkv_ref[keys, :KC] = (dk * score_scale).astype(bf16)
            dkv_ref[keys, KC:] = dv.astype(bf16)
            return carry

        lax.fori_loop(0, 1024 // KB, block, 0)


def attend_back(q, do, lse, delta, kv_all):
    return pl.pallas_call(
        attend_back_kernel,
        out_shape=(
            jax.ShapeDtypeStruct((NROW, HD), f32),
            jax.ShapeDtypeStruct((SEQ, 2 * KC), bf16),
        ),
        in_specs=[VM] * 5,
        out_specs=(VM, VM),
        compiler_params=params(),
        name="attend_back",
    )(q, do, lse, delta, kv_all)


def rotate(value_rows, cosine, sine_table):
    middle = value_rows.shape[-1] // 2
    first_half = value_rows[..., :middle]
    second_half = value_rows[..., middle:]
    return jnp.concatenate(
        [
            first_half * cosine - second_half * sine_table,
            second_half * cosine + first_half * sine_table,
        ],
        axis=-1,
    )


def norm_forward(value_rows):
    inverse = lax.rsqrt(jnp.mean(value_rows * value_rows, axis=-1, keepdims=True) + epsilon)
    return (value_rows * inverse, inverse)


def norm_backward(upstream, normal, inverse, gain):
    scaled = upstream * gain
    return inverse * (scaled - normal * jnp.mean(scaled * normal, axis=-1, keepdims=True))


def cross_rows(left_side, right_side):
    return lax.dot_general(
        left_side, right_side, (((1,), (1,)), ((), ())), preferred_element_type=f32
    )


def over_tokens(left_side, right_side):
    return lax.dot_general(
        left_side, right_side, (((0,), (0,)), ((), ())), preferred_element_type=f32
    ).astype(bf16)


def to_rows(v):
    return v.reshape(NW, ROWS, 2, HD).transpose(0, 2, 1, 3).reshape(NROW, HD)


def from_rows(v):
    return v.reshape(NW, 2, ROWS, HD).transpose(0, 2, 1, 3).reshape(TOK, 2 * HD)


def gather_weight(w):
    return lax.all_gather(w, T_AXES, axis=1, tiled=True).reshape(D, w.shape[-1])


def scatter_weight(w):
    return lax.psum_scatter(w.reshape(NW, NT * 16, -1), T_AXES, scatter_dimension=1, tiled=True)


def local(
    tokens, norm_gain, w_query, key_matrix, value_matrix, query_gain, key_gain, w_out, ffn_gain,
    w_gate, w_up, w_down, cotangent,
):
    s = (lax.axis_index("x") * 2 + lax.axis_index("c")) * 2 + lax.axis_index("t")
    at = jnp.arange(TOK, dtype=jnp.int32)
    position = (at // ROWS) * (NT * ROWS) + s * ROWS + at % ROWS
    exponent = jnp.arange(0, HD, 2, dtype=f32) / HD
    angles = position.astype(f32)[:, None] * (1.0 / rope_base**exponent)[None, :]
    cosine, sine = jnp.cos(angles), jnp.sin(angles)
    (
        middle, grad_middle, gain_two, query_rows, grad_rows, lse2, delta, qk_pre, context_bf, part_two,
        grad_middle_all, kv_all, qkv, normed_all, ffn_partial,
    ) = forward(
        tokens, cotangent, norm_gain.reshape(1, D), ffn_gain.reshape(1, D), query_gain.reshape(1, HD),
        key_gain.reshape(1, HD), jnp.concatenate([cosine, cosine], axis=1),
        jnp.concatenate([-sine, sine], axis=1),
        w_query, key_matrix, value_matrix, w_out, w_gate, w_up, w_down,
    )
    state = tokens.astype(f32)
    normal_one, inverse_one = norm_forward(state)
    cosine, sine_table = cosine[:, None, :], sine[:, None, :]
    normed_all = normed_all.reshape(TOK, D)
    grad_middle_all = grad_middle_all.reshape(TOK, D)
    qkv = qkv.reshape(D, QKV)
    kv_all = kv_all.reshape(SEQ, 2 * KC)
    query_pre = qk_pre[:, :QC].reshape(TOK, 2, HD)
    key_pre = qk_pre[:, QC : QC + KC].reshape(TOK, 1, HD)
    query_normal, query_inverse = norm_forward(query_pre)
    key_normal, key_inverse = norm_forward(key_pre)
    ffn_grads = scatter_weight(ffn_partial.reshape(D, PARTIAL))
    grad_query_rows, grad_packed = attend_back(query_rows, grad_rows, lse2, delta, kv_all)
    grad_own = sum_keys(grad_packed, 7)
    grad_key_rot = grad_own[:, :KC].reshape(TOK, 1, HD)
    grad_value_bf = grad_own[:, KC:].astype(bf16)
    grad_query_rot = from_rows(grad_query_rows * score_scale).reshape(TOK, 2, HD)
    grad_query_norm = rotate(grad_query_rot, cosine, -sine_table)
    grad_key_norm = rotate(grad_key_rot, cosine, -sine_table)
    gain_query = jnp.sum(grad_query_norm * query_normal, axis=(0, 1))
    gain_key = jnp.sum(grad_key_norm * key_normal, axis=(0, 1))
    grad_query_pre = norm_backward(
        grad_query_norm, query_normal, query_inverse, query_gain
    ).reshape(TOK, QC)
    grad_key_pre = norm_backward(grad_key_norm, key_normal, key_inverse, key_gain).reshape(TOK, KC)
    grad_projected = jnp.concatenate(
        [grad_query_pre.astype(bf16), grad_key_pre.astype(bf16), grad_value_bf], axis=1
    )
    grad_normed = sum_rows(cross_rows(grad_projected, qkv), 8)
    result = (middle + sum_rows(part_two.reshape(TOK, D), 5)).astype(bf16)
    grad_input = grad_middle + norm_backward(grad_normed, normal_one, inverse_one, norm_gain)
    gain_one = jnp.sum(grad_normed * normal_one, axis=0)
    attn_grads = scatter_weight(
        jnp.concatenate(
            [over_tokens(normed_all, grad_projected), over_tokens(grad_middle_all, context_bf)], axis=1
        )
    )
    back = return_weights(jnp.concatenate([attn_grads, ffn_grads], axis=2), 9)
    back = back.reshape(4, 32, COLS).transpose(1, 0, 2).astype(f32)
    cuts = [0]
    for w in (QC, KC, KC, QC, FC, FC, FC):
        cuts.append(cuts[-1] + w)
    grads = [back[:, :, a:b].reshape(32, -1) for a, b in zip(cuts[:-1], cuts[1:])]
    gain_one, gain_two, gain_query, gain_key = lax.psum(
        (gain_one, gain_two[0], gain_query, gain_key), AXES
    )
    return (
        result, grad_input, gain_one, grads[0], grads[1], grads[2], gain_query, gain_key, grads[3],
        gain_two, grads[4], grads[5], grads[6],
    )


def solution(mesh):
    fine = Mesh(mesh.devices.reshape(4, 2, 4, 2, 2), AXES)
    rows = P(AXES, None)
    weight = P(("z", "yl", "x", "c"), "t")
    return jax.shard_map(
        local,
        mesh=fine,
        in_specs=(rows, P(), weight, weight, weight, P(), P(), weight, P(), weight, weight, weight, rows),
        out_specs=(
            rows, rows, P(), weight, weight, weight, P(), P(), weight, P(), weight, weight, weight,
        ),
        check_vma=False,
    )
```

```python
import functools

import jax
import jax.numpy as jnp
from jax import lax
from jax.experimental import pallas as pl
from jax.experimental.pallas import tpu as pltpu
from jax.sharding import Mesh
from jax.sharding import PartitionSpec as P

AXES = ("z", "yl", "x", "c", "t")
SIZES = {"z": 4, "yl": 2, "x": 4, "c": 2, "t": 2}
W_AXES = ("z", "yl")
T_AXES = ("x", "c", "t")
NW, NT = 8, 16
ROWS = 64
TOK = NW * ROWS
D = 2048
HD = 128
SEQ = 8192
QC, KC, FC = 256, 128, 768
QKV = QC + 2 * KC
COLS = QKV + QC + 3 * FC
VMEM_LIMIT = 60 << 20
KB = 256
CH = 2 * ROWS
NROW = NW * CH

epsilon = 1e-06
rope_base = 1000000.0
score_scale = HD ** (-0.5)
LOG2E = 1.4426950408889634

bf16 = jnp.bfloat16
f32 = jnp.float32
MESH = pl.DeviceIdType.MESH
VM = pl.BlockSpec(memory_space=pltpu.VMEM)
ANY = pl.BlockSpec(memory_space=pl.ANY)
DMA = pltpu.SemaphoreType.DMA


def params(cid=None):
    if cid is None:
        return pltpu.CompilerParams(vmem_limit_bytes=VMEM_LIMIT)
    return pltpu.CompilerParams(
        collective_id=cid, has_side_effects=True, vmem_limit_bytes=VMEM_LIMIT
    )


def place():
    return {a: lax.axis_index(a) for a in AXES}


def shifted(me, axis, by):
    return lax.rem(me[axis] + by, SIZES[axis])


def barrier(devices):
    sem = pltpu.get_barrier_semaphore()
    for d in devices:
        pl.semaphore_signal(sem, inc=1, device_id=d, device_id_type=MESH)
    pl.semaphore_wait(sem, len(devices))


def remote(src, dst, ssem, rsem, device):
    return pltpu.make_async_remote_copy(
        src_ref=src, dst_ref=dst, send_sem=ssem, recv_sem=rsem, device_id=device, device_id_type=MESH
    )


class Sends:
    def __init__(self, ssem, rsem, base=0):
        self.ssem, self.rsem, self.base, self.open = ssem, rsem, base, []

    def send(self, kind, src, dst, device):
        k = self.base + kind
        c = remote(src, dst, self.ssem.at[k], self.rsem.at[k], device)
        c.start()
        self.open.append(c)

    def recv(self, kind, dst, device):
        k = self.base + kind
        remote(dst, dst, self.ssem.at[k], self.rsem.at[k], device).wait_recv()

    def close(self):
        for c in self.open:
            c.wait_send()


def w_devices(me):
    return (
        {"z": shifted(me, "z", 1)},
        {"z": shifted(me, "z", 3)},
        {"yl": 1 - me["yl"]},
    )


class GatherW:
    KINDS = 14

    def __init__(self, me, dst, sends):
        self.me, self.dst, self.s = me, dst, sends
        z, y = me["z"], me["yl"]
        zp, zm, zo, yo = shifted(me, "z", 1), shifted(me, "z", 3), shifted(me, "z", 2), 1 - y
        self.own, self.own_o = 2 * z + y, 2 * z + yo
        self.gp, self.gpo = 2 * zp + y, 2 * zp + yo
        self.gm, self.gmo = 2 * zm + y, 2 * zm + yo
        self.go, self.goo = 2 * zo + y, 2 * zo + yo
        self.dp, self.dm, self.dy = w_devices(me)

    def part(self, g, lo, hi):
        return self.dst.at[g, lo:hi]

    def put(self, kind, g, lo, hi, device):
        self.s.send(kind, self.part(g, lo, hi), self.part(g, lo, hi), device)

    def got(self, kind, g, lo, hi, device):
        self.s.recv(kind, self.part(g, lo, hi), device)

    def start(self):
        self.put(0, self.own, 0, 64, self.dp)
        self.put(1, self.own, 0, 64, self.dm)
        self.put(2, self.own, 0, 64, self.dy)

    def middle(self):
        dp, dm, dy = self.dp, self.dm, self.dy
        self.got(2, self.own_o, 0, 64, dy)
        self.put(3, self.own_o, 0, 32, dp)
        self.put(4, self.own_o, 0, 32, dm)
        self.got(0, self.gm, 0, 64, dm)
        self.put(5, self.gm, 16, 48, dp)
        self.put(6, self.gm, 32, 64, dy)
        self.got(1, self.gp, 0, 64, dp)
        self.put(7, self.gp, 0, 16, dm)
        self.put(8, self.gp, 48, 64, dm)
        self.put(9, self.gp, 32, 64, dy)

    def end(self):
        dp, dm, dy = self.dp, self.dm, self.dy
        self.got(3, self.gmo, 0, 32, dm)
        self.put(10, self.gmo, 16, 32, dp)
        self.got(4, self.gpo, 0, 32, dp)
        self.put(11, self.gpo, 0, 16, dm)
        self.got(5, self.go, 16, 48, dm)
        self.put(12, self.go, 32, 48, dy)
        self.got(8, self.go, 48, 64, dp)
        self.put(13, self.go, 48, 64, dy)
        self.got(7, self.go, 0, 16, dp)
        self.got(6, self.gmo, 32, 64, dy)
        self.got(9, self.gpo, 32, 64, dy)
        self.got(10, self.goo, 16, 32, dm)
        self.got(11, self.goo, 0, 16, dp)
        self.got(12, self.goo, 32, 48, dy)
        self.got(13, self.goo, 48, 64, dy)


class SumW:
    KINDS = 11
    LAND = (32, 32, 32, 16, 16, 32, 32, 32, 32, 64, 64, 64)

    def __init__(self, me, part, land, sends):
        self.part, self.land, self.s = part, land, sends
        z, y = me["z"], me["yl"]
        zp, zm, zo, yo = shifted(me, "z", 1), shifted(me, "z", 3), shifted(me, "z", 2), 1 - y
        self.own, self.own_o = 2 * z + y, 2 * z + yo
        self.gp, self.gpo = 2 * zp + y, 2 * zp + yo
        self.gm, self.gmo = 2 * zm + y, 2 * zm + yo
        self.go, self.goo = 2 * zo + y, 2 * zo + yo
        self.dp, self.dm, self.dy = w_devices(me)
        self.offset = [sum(self.LAND[:k]) for k in range(len(self.LAND))]

    def slot(self, kind, lo=0, n=None):
        n = self.LAND[kind] if n is None else n
        return self.land.at[self.offset[kind] + lo : self.offset[kind] + lo + n]

    def put(self, kind, g, lo, hi, device):
        self.s.send(kind, self.part.at[g, lo:hi], self.slot(kind), device)

    def got(self, kind, device):
        self.s.recv(kind, self.slot(kind), device)

    def add(self, kind, g, lo, hi):
        rows = self.slot(kind)
        self.part[g, lo:hi] = (self.part[g, lo:hi].astype(f32) + rows[...].astype(f32)).astype(bf16)

    def leaf(self):
        dp, dm, dy = self.dp, self.dm, self.dy
        self.put(0, self.goo, 32, 64, dy)
        self.put(3, self.goo, 16, 32, dm)
        self.put(4, self.goo, 0, 16, dp)
        self.put(1, self.gmo, 32, 64, dy)
        self.put(2, self.gpo, 32, 64, dy)

    def two(self):
        dp, dm, dy = self.dp, self.dm, self.dy
        self.got(0, dy)
        self.add(0, self.go, 32, 64)
        self.put(5, self.go, 16, 48, dm)
        self.s.send(6, self.part.at[self.go, 0:16], self.slot(6, 0, 16), dp)
        self.s.send(11, self.part.at[self.go, 48:64], self.slot(6, 16, 16), dp)
        self.got(3, dp)
        self.add(3, self.gmo, 16, 32)
        self.put(7, self.gmo, 0, 32, dm)
        self.got(4, dm)
        self.add(4, self.gpo, 0, 16)
        self.put(8, self.gpo, 0, 32, dp)

    def three(self):
        dp, dm, dy = self.dp, self.dm, self.dy
        self.got(1, dy)
        self.add(1, self.gm, 32, 64)
        self.got(5, dp)
        self.add(5, self.gm, 16, 48)
        self.put(9, self.gm, 0, 64, dm)
        self.got(2, dy)
        self.add(2, self.gp, 32, 64)
        self.s.recv(6, self.slot(6, 0, 16), dm)
        self.s.recv(11, self.slot(6, 16, 16), dm)
        for lo, hi, at in ((0, 16, 0), (48, 64, 16)):
            rows = self.slot(6, at, 16)
            self.part[self.gp, lo:hi] = (
                self.part[self.gp, lo:hi].astype(f32) + rows[...].astype(f32)
            ).astype(bf16)
        self.put(10, self.gp, 0, 64, dp)
        self.got(7, dp)
        self.add(7, self.own_o, 0, 32)
        self.got(8, dm)
        self.add(8, self.own_o, 0, 32)
        self.s.send(12, self.part.at[self.own_o], self.slot(11), dy)

    def total(self):
        dp, dm, dy = self.dp, self.dm, self.dy
        self.got(9, dp)
        self.got(10, dm)
        self.s.recv(12, self.slot(11), dy)
        total = self.part[self.own].astype(f32) + self.slot(9)[...].astype(f32)
        return total + self.slot(10)[...].astype(f32) + self.slot(11)[...].astype(f32)

    def run(self):
        self.leaf()
        self.two()
        self.three()
        return self.total()


SUMW_ROWS = sum(SumW.LAND)
SUMW_SEMS = 13


def t_devices(me):
    return (
        {"x": shifted(me, "x", 1)},
        {"x": shifted(me, "x", 3)},
        {"t": 1 - me["t"]},
        {"c": 1 - me["c"]},
    )


class GatherT:
    KINDS = 19

    def __init__(self, me, dst, sends):
        self.dst, self.s = dst, sends
        x, c, t = me["x"], me["c"], me["t"]
        xp, xm, xo = shifted(me, "x", 1), shifted(me, "x", 3), shifted(me, "x", 2)

        def at(x, t, c=c):
            return (x * 2 + c) * 2 + t

        to = 1 - t
        self.ids = {
            "own": at(x, t), "to": at(x, to), "p": at(xp, t), "po": at(xp, to),
            "m": at(xm, t), "mo": at(xm, to), "o": at(xo, t), "oo": at(xo, to),
        }
        self.sib = {k: v + 2 * (1 - 2 * c) for k, v in self.ids.items()}
        self.dp, self.dm, self.dt, self.dc = t_devices(me)

    def part(self, s, half):
        lo, hi = {None: (0, 8), 0: (0, 4), 1: (4, 8)}[half]
        return self.dst.at[lo:hi, s]

    def put(self, kind, name, device, half=None):
        s = self.ids[name]
        self.s.send(kind, self.part(s, half), self.part(s, half), device)

    def got(self, kind, name, device, half=None, sib=False):
        s = (self.sib if sib else self.ids)[name]
        self.s.recv(kind, self.part(s, half), device)

    def start(self):
        self.put(2, "own", self.dt)
        self.put(0, "own", self.dp)
        self.put(1, "own", self.dm)
        self.put(3, "own", self.dc)

    def middle(self):
        dp, dm, dt, dc = self.dp, self.dm, self.dt, self.dc
        self.got(0, "m", dm)
        self.put(7, "m", dp, 0)
        self.put(8, "m", dc)
        self.got(1, "p", dp)
        self.put(9, "p", dm, 1)
        self.put(10, "p", dc)
        self.got(2, "to", dt)
        self.put(4, "to", dp)
        self.put(5, "to", dm)
        self.put(6, "to", dc)

    def end(self):
        dp, dm, dt, dc = self.dp, self.dm, self.dt, self.dc
        self.got(7, "o", dm, 0)
        self.put(15, "o", dc, 0)
        self.got(9, "o", dp, 1)
        self.put(16, "o", dc, 1)
        self.got(4, "mo", dm)
        self.put(11, "mo", dp, 0)
        self.put(12, "mo", dc)
        self.got(5, "po", dp)
        self.put(13, "po", dm, 1)
        self.put(14, "po", dc)
        self.got(11, "oo", dm, 0)
        self.put(17, "oo", dc, 0)
        self.got(13, "oo", dp, 1)
        self.put(18, "oo", dc, 1)
        for kind, name, half in (
            (3, "own", None), (8, "m", None), (10, "p", None), (6, "to", None), (15, "o", 0), (16, "o", 1),
            (12, "mo", None), (14, "po", None), (17, "oo", 0), (18, "oo", 1),
        ):
            self.got(kind, name, dc, half, True)


def sems(n):
    return [DMA((n,)), DMA((n,))]


GROUPS = (QKV, QC, 2 * FC, FC)
STARTS = (0, QKV, QKV + QC, QKV + QC + 2 * FC)
PARTIAL = 3 * FC


def rms(v):
    return lax.rsqrt(jnp.mean(v * v, axis=-1, keepdims=True) + epsilon)


def mul_rows(a, b):
    return lax.dot_general(a, b, (((1,), (1,)), ((), ())), preferred_element_type=f32)


def mul(a, b):
    return jnp.dot(a, b, preferred_element_type=f32)


def mul_tokens(a, b):
    return lax.dot_general(a, b, (((0,), (0,)), ((), ())), preferred_element_type=f32)


def row_sums(v):
    ones = jnp.ones((8, v.shape[1]), f32)
    return lax.dot_general(
        ones, v, (((1,), (1,)), ((), ())), preferred_element_type=f32, precision=lax.Precision.HIGHEST
    )[0:1]


def forward_kernel(
    tok, cot, ngain, fgain, qgain, kgain, cosr, sinr, wq, wk, wv, wo, wg, wu, wd,
    middle, grad_mid, gain_two, q_rows, do_rows, lse, delta, qk_pre, ctx, part_two, gm_all,
    kv_out, qkv_out, normed_out, partial,
    stage, normed_all, cot_all, nt_all, kv_all, wqkv, wout, wgu, wdn, part, land, o_acc, l_acc,
    gate, up, gh, hidden, dgu, buf, ssem, rsem, lsem,
):
    me = place()
    z, y, t = me["z"], me["yl"], me["t"]
    own_g = 2 * z + y
    s = (me["x"] * 2 + me["c"]) * 2 + t
    dp, dm, dy = w_devices(me)
    sem = pltpu.get_barrier_semaphore()
    for dz in range(4):
        for dyl in range(2):
            for dt in range(2):
                if dz or dyl or dt:
                    pl.semaphore_signal(
                        sem, inc=1, device_id_type=MESH,
                        device_id={
                            "z": shifted(me, "z", dz), "yl": shifted(me, "yl", dyl), "t": shifted(me, "t", dt)
                        },
                    )
    for d in t_devices(me)[:2] + t_devices(me)[3:]:
        pl.semaphore_signal(sem, inc=1, device_id=d, device_id_type=MESH)

    state = tok[...].astype(f32)
    normed_all[own_g] = (state * rms(state) * ngain[...]).astype(bf16)
    cot_all[own_g] = cot[...]
    at = 0
    for w in (wq, wk, wv, wo, wg, wu, wd):
        n = w.shape[1] // 4
        for j in range(4):
            stage[j, :, at : at + n] = w[:, j * n : (j + 1) * n]
        at += n
    pl.semaphore_wait(sem, 18)

    count = [0]

    def sends(n):
        base = count[0]
        count[0] += n
        return Sends(ssem, rsem, base)

    gw = GatherW(me, normed_all, sends(GatherW.KINDS))
    gw.start()

    full = (wqkv, wout, wgu, wdn)
    base = count[0]
    count[0] += 32
    holder = own_g // 4

    def to_holders(groups):
        for j in range(4):
            for t2 in range(2):
                dst_z, dst_y = 2 * t + j // 2, j % 2
                is_me = (dst_z == z) & (dst_y == y) & (t == t2)
                src = stage.at[j, 16 * t2 : 16 * t2 + 16]
                to = {"z": dst_z, "yl": dst_y, "t": jnp.int32(t2)}
                remotes, locals_ = [], []
                for k in groups:
                    piece = src.at[:, STARTS[k] : STARTS[k] + GROUPS[k]]
                    remotes.append(
                        remote(
                            piece, full[k].at[own_g, s - t + t2], ssem.at[base + 8 * k + 2 * j + t2],
                            rsem.at[base + 8 * k + own_g], to,
                        )
                    )
                    locals_.append(pltpu.make_async_copy(piece, full[k].at[own_g, s], lsem.at[k]))

                @pl.when(is_me)
                def _():
                    for c in locals_:
                        c.start()
                    for c in locals_:
                        c.wait()

                @pl.when(jnp.logical_not(is_me))
                def _():
                    for c in remotes:
                        c.start()

    def from_owners(groups):
        for g in range(8):
            from_me = (own_g == g) & (holder == t)

            @pl.when(jnp.logical_not(from_me))
            def _(g=g):
                for k in groups:
                    dst = full[k].at[g, s]
                    remote(dst, dst, ssem.at[0], rsem.at[base + 8 * k + g], dy).wait_recv()

    to_holders((0,))
    from_owners((0,))
    gq, go, gg, gd = [GatherT(me, w, sends(GatherT.KINDS)) for w in full]
    gq.start()
    gw.middle()
    to_holders((1, 2, 3))
    gq.middle()
    gw.end()
    gq.end()

    keep = [
        pltpu.make_async_copy(wqkv, qkv_out, lsem.at[4]),
        pltpu.make_async_copy(normed_all, normed_out, lsem.at[5]),
    ]
    for c in keep:
        c.start()

    for h in range(2):
        rows = slice(h * 256, h * 256 + 256)
        pre = mul(
            normed_all[4 * h : 4 * h + 4].reshape(256, D), wqkv[...].reshape(D, QKV)
        )
        qk_pre[rows] = pre[:, : QC + KC]
        cosine, sine = cosr[rows], sinr[rows]
        for head in range(3):
            u = pre[:, head * HD : head * HD + HD]
            n = u * rms(u) * (qgain if head < 2 else kgain)[...]
            rolled = jnp.concatenate([n[:, HD // 2 :], n[:, : HD // 2]], axis=1)
            rot = (n * cosine + rolled * sine).astype(bf16)
            for i in range(4):
                g = 4 * h + i
                piece = rot[i * ROWS : i * ROWS + ROWS]
                if head < 2:
                    q_rows[g * CH + head * ROWS : g * CH + head * ROWS + ROWS] = piece
                else:
                    kv_all[g, s, :, :KC] = piece
        val = pre[:, QC + KC :].astype(bf16)
        for i in range(4):
            kv_all[4 * h + i, s, :, KC:] = val[i * ROWS : i * ROWS + ROWS]

    gk = GatherT(me, kv_all, sends(GatherT.KINDS))
    gc = GatherW(me, cot_all, sends(GatherW.KINDS))
    gk.start()
    gc.start()
    from_owners((1, 2, 3))
    go.start()
    gg.start()
    gk.middle()
    gc.middle()
    gk.end()
    keep.append(pltpu.make_async_copy(kv_all, kv_out, lsem.at[6]))
    keep[-1].start()

    o_acc[...] = jnp.zeros_like(o_acc)
    l_acc[...] = jnp.zeros_like(l_acc)
    attend_blocks(range(0, 2), s, q_rows, kv_all, o_acc, l_acc)
    go.middle()
    gg.middle()
    gc.end()
    gd.start()
    attend_blocks(range(2, 8), s, q_rows, kv_all, o_acc, l_acc)
    go.end()
    gg.end()
    gd.middle()

    lse[...] = jnp.log2(row_sums(l_acc[...]))
    for g in range(NW):
        rows = slice(g * CH, g * CH + CH)
        o = o_acc[rows] / jnp.sum(l_acc[rows], axis=1, keepdims=True)
        o_acc[rows] = o
        ctx[g * ROWS : g * ROWS + ROWS, :HD] = o[:ROWS].astype(bf16)
        ctx[g * ROWS : g * ROWS + ROWS, HD:] = o[ROWS:].astype(bf16)
    for n in range(4):
        w = wout[2 * n : 2 * n + 2].reshape(512, QC)
        part[:, :, n * 512 : n * 512 + 512] = (
            mul_rows(ctx[...], w).astype(bf16).reshape(NW, ROWS, 512)
        )
    sw = SumW(me, part, land, sends(SUMW_SEMS))
    sw.leaf()
    sw.two()
    gd.end()
    for n in range(3):
        gh[:, n * 256 : n * 256 + 256] = mul(
            cot_all[...].reshape(TOK, D), wdn[:, :, :, n * 256 : n * 256 + 256].reshape(D, 256)
        )
    sw.three()
    mid = state + sw.total()
    middle[...] = mid
    nt_all[own_g] = (mid * rms(mid) * fgain[...]).astype(bf16)
    gn = GatherW(me, nt_all, sends(GatherW.KINDS))
    gn.start()
    gn.middle()
    gn.end()

    for n in range(3):
        cols = slice(n * 256, n * 256 + 256)
        nt = nt_all[...].reshape(TOK, D)
        gate[:, cols] = mul(nt, wgu[:, :, :, n * 256 : n * 256 + 256].reshape(D, 256))
        up[:, cols] = mul(nt, wgu[:, :, :, FC + n * 256 : FC + n * 256 + 256].reshape(D, 256))

    def units(i, carry):
        rows = pl.ds(pl.multiple_of(i * 64, 64), 64)
        gv, uv, hv = gate[rows], up[rows], gh[rows]
        sig = jax.nn.sigmoid(gv)
        act = gv * sig
        hidden[rows] = (act * uv).astype(bf16)
        dgu[rows, :FC] = (hv * uv * (sig * (1.0 + gv * (1.0 - sig)))).astype(bf16)
        dgu[rows, FC:] = (hv * act).astype(bf16)
        return carry

    lax.fori_loop(0, TOK // 64, units, 0)
    sw.s.close()
    for n in range(4):
        w = wgu[2 * n : 2 * n + 2].reshape(512, 2 * FC)
        part[:, :, n * 512 : n * 512 + 512] = (
            mul_rows(dgu[...], w).astype(bf16).reshape(NW, ROWS, 512)
        )
    sb = SumW(me, part, land, sends(SUMW_SEMS))
    sb.leaf()
    for n in range(4):
        w = wdn[2 * n : 2 * n + 2].reshape(512, FC)
        part_two[:, :, n * 512 : n * 512 + 512] = (
            mul_rows(hidden[...], w).astype(bf16).reshape(NW, ROWS, 512)
        )
    sb.two()

    def weight_grads(lo, hi):
        def step(g, carry):
            slot = lax.rem(g, 2)

            @pl.when(g >= 2)
            def _():
                pltpu.make_async_copy(buf.at[slot], partial.at[g - 2], lsem.at[7 + slot]).wait()

            cols = pl.ds(pl.multiple_of(g * 256, 256), 256)
            a = nt_all[:, :, cols].reshape(TOK, 256)
            for n in range(3):
                c = slice(n * 512, n * 512 + 512)
                buf[slot, :, c] = mul_tokens(a, dgu[:, c]).astype(bf16)
            b = cot_all[:, :, cols].reshape(TOK, 256)
            for n in range(3):
                c = slice(n * 256, n * 256 + 256)
                buf[slot, :, 2 * FC + n * 256 : 2 * FC + n * 256 + 256] = mul_tokens(
                    b, hidden[:, c]
                ).astype(bf16)
            pltpu.make_async_copy(buf.at[slot], partial.at[g], lsem.at[7 + slot]).start()
            return carry

        lax.fori_loop(lo, hi, step, 0)

    weight_grads(0, 2)
    sb.three()
    weight_grads(2, 4)
    gnt = sb.total()
    mid = middle[...]
    inv = rms(mid)
    normal = mid * inv
    gain_two[...] = jnp.sum(gnt * normal, axis=0, keepdims=True)
    scaled = gnt * fgain[...]
    gm = cot[...].astype(f32) + inv * (
        scaled - normal * jnp.mean(scaled * normal, axis=-1, keepdims=True)
    )
    grad_mid[...] = gm
    gm_all[own_g] = gm.astype(bf16)
    ga = GatherW(me, gm_all, sends(GatherW.KINDS))
    ga.start()
    weight_grads(4, 6)
    ga.middle()
    weight_grads(6, 8)
    ga.end()
    grad_ctx = mul(gm_all[...].reshape(TOK, D), wout[...].reshape(D, QC)).astype(bf16)
    for g in range(NW):
        for head in range(2):
            do_rows[g * CH + head * ROWS : g * CH + head * ROWS + ROWS] = grad_ctx[
                g * ROWS : g * ROWS + ROWS, head * HD : head * HD + HD
            ]
    delta[...] = row_sums(do_rows[...].astype(f32) * o_acc[...])

    for c in keep:
        c.wait()
    for slot in range(2):
        pltpu.make_async_copy(buf.at[slot], partial.at[6 + slot], lsem.at[7 + slot]).wait()
    for j in range(4):
        for t2 in range(2):
            is_me = (2 * t + j // 2 == z) & (j % 2 == y) & (t == t2)

            @pl.when(jnp.logical_not(is_me))
            def _(j=j, t2=t2):
                src = stage.at[j, 16 * t2 : 16 * t2 + 16]
                for k in range(4):
                    piece = src.at[:, STARTS[k] : STARTS[k] + GROUPS[k]]
                    remote(
                        piece, piece, ssem.at[base + 8 * k + 2 * j + t2], rsem.at[0], dy
                    ).wait_send()
    for g in (gw, gq, go, gg, gd, gk, gc, gn, sb, ga):
        g.s.close()
    assert count[0] == FORWARD_SEMS, count[0]


FORWARD_SEMS = 4 * GatherW.KINDS + 5 * GatherT.KINDS + 2 * SUMW_SEMS + 32


def forward(tok, cot, ngain, fgain, qgain, kgain, cosr, sinr, *weights):
    def out(shape, dtype):
        return jax.ShapeDtypeStruct(shape, dtype)

    def vmem(shape, dtype=bf16):
        return pltpu.VMEM(shape, dtype)

    return pl.pallas_call(
        forward_kernel,
        out_shape=(
            out((ROWS, D), f32), out((ROWS, D), f32), out((1, D), f32), out((NROW, HD), bf16), out((NROW, HD), bf16),
            out((1, NROW), f32), out((1, NROW), f32), out((TOK, QC + KC), f32), out((TOK, QC), bf16),
            out((NW, ROWS, D), bf16), out((NW, ROWS, D), bf16),
            out((NW, NT, ROWS, 2 * KC), bf16), out((NW, NT, 16, QKV), bf16), out((NW, ROWS, D), bf16),
            out((NW, 256, PARTIAL), bf16),
        ),
        in_specs=[VM] * 15,
        out_specs=(VM,) * 11 + (ANY,) * 4,
        scratch_shapes=[
            vmem((4, 32, COLS)), vmem((NW, ROWS, D)), vmem((NW, ROWS, D)), vmem((NW, ROWS, D)),
            vmem((NW, NT, ROWS, 2 * KC)), vmem((NW, NT, 16, QKV)), vmem((NW, NT, 16, QC)),
            vmem((NW, NT, 16, 2 * FC)), vmem((NW, NT, 16, FC)), vmem((NW, ROWS, D)),
            vmem((SUMW_ROWS, D)), vmem((NROW, HD), f32), vmem((NROW, HD), f32),
            vmem((TOK, FC), f32), vmem((TOK, FC), f32), vmem((TOK, FC), f32), vmem((TOK, FC)),
            vmem((TOK, 2 * FC)), vmem((2, 256, PARTIAL)),
        ]
        + sems(FORWARD_SEMS) + [DMA((9,))],
        compiler_params=params(0),
        name="forward",
    )(tok, cot, ngain, fgain, qgain, kgain, cosr, sinr, *weights)


class SumT:
    KINDS = 9

    def __init__(self, me, src, own, part, half, land, final, sends):
        self.src, self.own, self.part, self.half, self.land, self.final, self.s = (
            src, own, part, half, land, final, sends,
        )
        x = me["x"]
        self.c, self.t = me["c"], me["t"]
        self.order = (shifted(me, "x", 2), shifted(me, "x", 3), shifted(me, "x", 1), x)
        self.dp, self.dm, self.dt, self.dc = t_devices(me)
        self.h = part.shape[1] // 2

    def leaf(self):
        for i, xi in enumerate(self.order):
            self.s.send(i, self.src.at[:, xi, 1 - self.c], self.part.at[i], self.dc)

    def pair(self, i):
        self.s.recv(i, self.part.at[i], self.dc)
        mine = self.own(i, self.order[i])
        self.part[i] = (self.part[i].astype(f32) + mine.astype(f32)).astype(bf16)

    def two(self):
        self.pair(0)
        self.s.send(4, self.part.at[0, : self.h], self.half.at[0], self.dm)
        self.s.send(5, self.part.at[0, self.h :], self.half.at[1], self.dp)
        self.pair(1)
        self.pair(2)

    def three(self):
        h = self.h
        self.s.recv(4, self.half.at[0], self.dp)
        self.part[1, :h] = (self.part[1, :h].astype(f32) + self.half[0].astype(f32)).astype(bf16)
        self.s.send(6, self.part.at[1], self.land.at[0], self.dm)
        self.s.recv(5, self.half.at[1], self.dm)
        self.part[2, h:] = (self.part[2, h:].astype(f32) + self.half[1].astype(f32)).astype(bf16)
        self.s.send(7, self.part.at[2], self.land.at[1], self.dp)
        self.pair(3)

    def four(self):
        self.s.recv(6, self.land.at[0], self.dp)
        self.s.recv(7, self.land.at[1], self.dm)
        to = 1 - self.t
        self.part[3, :, to] = (
            self.part[3, :, to].astype(f32)
            + self.land[0, :, to].astype(f32)
            + self.land[1, :, to].astype(f32)
        ).astype(bf16)
        self.s.send(8, self.part.at[3, :, to], self.final, self.dt)

    def total(self):
        t = self.t
        own = (
            self.part[3, :, t].astype(f32)
            + self.land[0, :, t].astype(f32)
            + self.land[1, :, t].astype(f32)
        )
        self.s.recv(8, self.final, self.dt)
        return own + self.final[...].astype(f32)


def sum_t_scratch(slabs, rows, cols):
    return [
        pltpu.VMEM((4, slabs, 2, rows, cols), bf16),
        pltpu.VMEM((2, slabs // 2, 2, rows, cols), bf16),
        pltpu.VMEM((2, slabs, 2, rows, cols), bf16),
        pltpu.VMEM((slabs, rows, cols), bf16),
    ]


class Return:
    def __init__(self, me, x_ref, out, lo, hi, ssem, rsem, base, lsem):
        self.x, self.out, self.lo, self.hi = x_ref, out, lo, hi
        self.ssem, self.rsem, self.base, self.lsem = ssem, rsem, base, lsem
        self.z, self.y, self.t = me["z"], me["yl"], me["t"]
        self.own_g = 2 * self.z + self.y
        self.holder = self.own_g // 4
        self.block = self.own_g - 4 * self.holder
        self.dy = w_devices(me)[2]

    def each(self, act):
        for g in range(8):
            is_me = (self.own_g == g) & (self.holder == self.t)
            act(g, is_me)

    def start(self):
        def act(g, is_me):
            dst = self.out.at[self.block, self.t, :, self.lo : self.hi]
            to = {"z": jnp.int32(g // 2), "yl": jnp.int32(g % 2), "t": self.holder}
            k = self.base + self.block * 2 + self.t
            c = remote(self.x.at[g], dst, self.ssem.at[self.base + g], self.rsem.at[k], to)
            l = pltpu.make_async_copy(self.x.at[g], dst, self.lsem)

            @pl.when(is_me)
            def _():
                l.start()
                l.wait()

            @pl.when(jnp.logical_not(is_me))
            def _():
                c.start()

        self.each(act)

    def end(self):
        for j in range(4):
            for t2 in range(2):
                is_me = (2 * self.t + j // 2 == self.z) & (j % 2 == self.y) & (self.t == t2)

                @pl.when(jnp.logical_not(is_me))
                def _(j=j, t2=t2):
                    d = self.out.at[j, t2, :, self.lo : self.hi]
                    k = self.base + j * 2 + t2
                    remote(d, d, self.ssem.at[0], self.rsem.at[k], self.dy).wait_recv()

        def act(g, is_me):
            @pl.when(jnp.logical_not(is_me))
            def _():
                x = self.x.at[g]
                remote(x, x, self.ssem.at[self.base + g], self.rsem.at[0], self.dy).wait_send()

        self.each(act)


GAINS = 2 * D + 2 * HD
PEERS_W = [(dz, dy) for dz in range(4) for dy in range(2) if dz or dy]
PEERS_T = [(dx, dc, dt) for dx in range(4) for dc in range(2) for dt in range(2) if dx or dc or dt]
BACKWARD_SEMS = 5 * SumT.KINDS + 2 * SUMW_SEMS + 3 * 8 + len(PEERS_W) + len(PEERS_T)


def backward_kernel(
    tok, middle, grad_mid, gain_two, ngain, qgain, kgain, cosr, sinr, q_rows, do_rows, lse, delta, qk_pre, ctx,
    gm_in, part_two, kv_in, qkv_in, normed_in, partial,
    result, grad_input, gains, back,
    kv_all, wqkv, normed_all, gm_all, part_r, land_r, part, land, dq, dkv, gp, sa1, sa2, own_f,
    ret_f, ret_1, ret_2, gsend, gw_land, gt_send, gt_land,
    f1, f2, f3, f4, k11, k12, k13, k14, k21, k22, k23, k24, a11, a12, a13, a14, a21, a22, a23, a24,
    ssem, rsem, lsem,
):
    me = place()
    c = me["c"]
    s = (me["x"] * 2 + c) * 2 + me["t"]
    sem = pltpu.get_barrier_semaphore()
    peers = [
        {"z": shifted(me, "z", dz), "yl": shifted(me, "yl", dy), "t": shifted(me, "t", dt)}
        for dz in range(4) for dy in range(2) for dt in range(2) if dz or dy or dt
    ] + [
        {"x": shifted(me, "x", dx), "c": shifted(me, "c", dc), "t": shifted(me, "t", dt)}
        for dx in range(4) for dc in range(2) for dt in range(2) if dx or dc
    ]
    for d in peers:
        pl.semaphore_signal(sem, inc=1, device_id=d, device_id_type=MESH)

    count = [0]

    def base(n):
        count[0] += n
        return count[0] - n

    def sends(n):
        return Sends(ssem, rsem, base(n))

    sf = SumT(me, partial, lambda i, xi: own_f[i], f1, f2, f3, f4, sends(SumT.KINDS))
    loads = [
        pltpu.make_async_copy(part_two, part_r, lsem.at[0]),
        pltpu.make_async_copy(kv_in, kv_all, lsem.at[1]),
    ]
    loads += [
        pltpu.make_async_copy(partial.at[:, xi, c], own_f.at[i], lsem.at[2 + i])
        for i, xi in enumerate(sf.order)
    ]
    loads += [
        pltpu.make_async_copy(gm_in, gm_all, lsem.at[6]),
        pltpu.make_async_copy(normed_in, normed_all, lsem.at[7]),
        pltpu.make_async_copy(qkv_in, wqkv, lsem.at[8]),
    ]
    for l in loads:
        l.start()
    dq[...] = jnp.zeros_like(dq)
    pl.semaphore_wait(sem, len(peers))

    sf.leaf()
    sr = SumW(me, part_r, land_r, sends(SUMW_SEMS))
    loads[0].wait()
    sr.leaf()
    loads[1].wait()

    def attention(slabs):
        attend_back_blocks(slabs, s, q_rows, do_rows, lse, delta, kv_all, dq, dkv)

    attention(range(0, 1))
    sr.two()
    for l in loads[2:]:
        l.wait()
    sf.two()
    attention(range(1, 2))
    sr.three()
    attention(range(2, 3))
    sf.three()
    result[...] = (middle[...] + sr.total()).astype(bf16)
    attention(range(3, 4))

    def key_sum(lo, hi, bufs):
        view = dkv.at[lo:hi]
        return SumT(me, view, lambda i, xi: dkv[lo:hi, xi, c], *bufs, sends(SumT.KINDS))

    k1 = key_sum(0, 4, (k11, k12, k13, k14))
    k2 = key_sum(4, 8, (k21, k22, k23, k24))
    k1.leaf()
    sf.four()
    attention(range(4, 6))
    k1.two()
    attention(range(6, 8))
    k2.leaf()
    k1.three()
    ret_f[...] = sf.total().astype(bf16)
    rf = Return(me, ret_f, back, QKV + QC, COLS, ssem, rsem, base(8), lsem.at[9])
    rf.start()

    for head in range(2):
        u = qk_pre[:, head * HD : head * HD + HD]
        g = dq[...].reshape(NW, 2, ROWS, HD)[:, head].reshape(TOK, HD) * score_scale
        dpre, gain = head_back(u, g, qgain[...], cosr[...], sinr[...])
        gp[:, head * HD : head * HD + HD] = dpre.astype(bf16)
        gains[:, 2 * D : 2 * D + HD] = gain if head == 0 else gains[:, 2 * D : 2 * D + HD] + gain
    k2.two()
    k1.four()

    def weight_step(dst, at, a_ref, lo, hi):
        def step(g, carry):
            a = a_ref[:, :, pl.ds(pl.multiple_of(g * 256, 256), 256)].reshape(TOK, 256)
            b = ctx[...] if lo is None else gp[:, lo:hi]
            dst[g, :, :, :, :, at : at + 256] = (
                mul_tokens(a, b).astype(bf16).reshape(4, 2, 2, 16, 256)
            )
            return carry

        lax.fori_loop(0, NW, step, 0)

    weight_step(sa1, 0, gm_all, None, None)
    k2.three()
    weight_step(sa1, QC, normed_all, 0, QC)
    a1 = SumT(me, sa1, lambda i, xi: sa1[:, xi, c], a11, a12, a13, a14, sends(SumT.KINDS))
    a1.leaf()
    k2.four()
    a1.two()
    own_kv = [k1.total().reshape(TOK // 2, 2 * KC), k2.total().reshape(TOK // 2, 2 * KC)]
    for h in range(2):
        rows = slice(h * 256, h * 256 + 256)
        dpre, gain = head_back(
            qk_pre[rows, QC:], own_kv[h][:, :KC], kgain[...], cosr[rows], sinr[rows]
        )
        gp[rows, QC : QC + KC] = dpre.astype(bf16)
        gp[rows, QC + KC :] = own_kv[h][:, KC:].astype(bf16)
        cols = slice(2 * D + HD, 2 * D + 2 * HD)
        gains[:, cols] = gain if h == 0 else gains[:, cols] + gain
    for n in range(4):
        w = wqkv[2 * n : 2 * n + 2].reshape(512, QKV)
        part[:, :, n * 512 : n * 512 + 512] = (
            mul_rows(gp[...], w).astype(bf16).reshape(NW, ROWS, 512)
        )
    sw = SumW(me, part, land, sends(SUMW_SEMS))
    sw.leaf()
    weight_step(sa2, 0, normed_all, QC, QKV)
    a2 = SumT(me, sa2, lambda i, xi: sa2[:, xi, c], a21, a22, a23, a24, sends(SumT.KINDS))
    a2.leaf()
    sw.two()
    a1.three()
    a2.two()
    sw.three()
    a1.four()
    a2.three()
    gnorm = sw.total()
    x = tok[...].astype(f32)
    inv = rms(x)
    normal = x * inv
    gains[:, :D] = jnp.sum(gnorm * normal, axis=0, keepdims=True)
    gains[:, D : 2 * D] = gain_two[...]

    bw = base(len(PEERS_W))
    bt = base(len(PEERS_T))
    gsend[...] = gains[...]
    first = []
    for i, (dz, dy) in enumerate(PEERS_W):
        d = {"z": shifted(me, "z", dz), "yl": shifted(me, "yl", dy)}
        first.append(remote(gsend, gw_land.at[i], ssem.at[bw + i], rsem.at[bw + i], d))
        first[-1].start()
    scaled = gnorm * ngain[...]
    grad_input[...] = grad_mid[...] + inv * (
        scaled - normal * jnp.mean(scaled * normal, axis=-1, keepdims=True)
    )
    ret_1[...] = a1.total().astype(bf16)
    r1 = Return(me, ret_1, back, 0, 2 * QC, ssem, rsem, base(8), lsem.at[9])
    r1.start()
    a2.four()
    total = gsend[...]
    for i, r in enumerate(first):
        r.wait_recv()
        total = total + gw_land[i]
    gt_send[...] = total
    second = []
    for i, (dx, dc, dt) in enumerate(PEERS_T):
        d = {"x": shifted(me, "x", dx), "c": shifted(me, "c", dc), "t": shifted(me, "t", dt)}
        second.append(remote(gt_send, gt_land.at[i], ssem.at[bt + i], rsem.at[bt + i], d))
        second[-1].start()
    ret_2[...] = a2.total().astype(bf16)
    r2 = Return(me, ret_2, back, 2 * QC, 3 * QC, ssem, rsem, base(8), lsem.at[9])
    r2.start()
    for i, r in enumerate(second):
        r.wait_recv()
        total = total + gt_land[i]
    gains[...] = total
    for r in first + second:
        r.wait_send()
    for r in (rf, r1, r2):
        r.end()
    for g in (sf, sr, k1, k2, a1, a2, sw):
        g.s.close()
    assert count[0] == BACKWARD_SEMS, count[0]


def head_back(u, g, gain, cosine, sine):
    rolled = jnp.concatenate([g[:, HD // 2 :], g[:, : HD // 2]], axis=1)
    g = g * cosine - rolled * sine
    inv = rms(u)
    normal = u * inv
    total = jnp.sum(g * normal, axis=0, keepdims=True)
    scaled = g * gain
    return inv * (scaled - normal * jnp.mean(scaled * normal, axis=-1, keepdims=True)), total


def backward(*args):
    def out(shape, dtype):
        return jax.ShapeDtypeStruct(shape, dtype)

    def vmem(shape, dtype=bf16):
        return pltpu.VMEM(shape, dtype)

    return pl.pallas_call(
        backward_kernel,
        out_shape=(
            out((ROWS, D), bf16), out((ROWS, D), f32), out((1, GAINS), f32), out((4, 2, 16, COLS), bf16),
        ),
        in_specs=[VM] * 15 + [ANY] * 6,
        out_specs=(VM,) * 4,
        scratch_shapes=[
            vmem((NW, NT, ROWS, 2 * KC)), vmem((NW, NT, 16, QKV)), vmem((NW, ROWS, D)), vmem((NW, ROWS, D)),
            vmem((NW, ROWS, D)), vmem((SUMW_ROWS, D)), vmem((NW, ROWS, D)), vmem((SUMW_ROWS, D)),
            vmem((NROW, HD), f32), vmem((NW, 4, 2, 2, ROWS, 2 * KC)), vmem((TOK, QKV)),
            vmem((NW, 4, 2, 2, 16, 2 * QC)), vmem((NW, 4, 2, 2, 16, QC)), vmem((4, NW, 2, 16, PARTIAL)),
            vmem((NW, 16, PARTIAL)), vmem((NW, 16, 2 * QC)), vmem((NW, 16, QC)),
            vmem((1, GAINS), f32), vmem((len(PEERS_W), 1, GAINS), f32),
            vmem((1, GAINS), f32), vmem((len(PEERS_T), 1, GAINS), f32),
        ]
        + sum_t_scratch(NW, 16, PARTIAL)
        + sum_t_scratch(4, ROWS, 2 * KC)
        + sum_t_scratch(4, ROWS, 2 * KC)
        + sum_t_scratch(NW, 16, 2 * QC)
        + sum_t_scratch(NW, 16, QC)
        + sems(BACKWARD_SEMS) + [DMA((10,))],
        compiler_params=params(1),
        name="backward",
    )(*args)


def attend_blocks(slabs, s, q_ref, kv_ref, o_ref, l_ref):
    factor = score_scale * LOG2E
    for g in slabs:
        first = g * CH

        def block(b, carry, g=g, first=first):
            pair = kv_ref[g, pl.ds(b * 4, 4)].reshape(KB, 2 * KC)
            k, v = pair[:, :KC], pair[:, KC:]
            for r0 in range(first, NROW, 256):
                r1 = min(r0 + 256, NROW)
                sc = mul_rows(q_ref[r0:r1], k)
                p = jnp.exp2(sc * factor)
                if r0 == first:
                    row = lax.broadcasted_iota(jnp.int32, (r1 - r0, KB), 0)
                    col = lax.broadcasted_iota(jnp.int32, (r1 - r0, KB), 1)
                    seen = (row >= CH) | (s * ROWS + (row & (ROWS - 1)) >= b * KB + col)
                    p = jnp.where(seen, p, 0.0)
                l_ref[r0:r1] += p[:, :128] + p[:, 128:]
                o_ref[r0:r1] += mul(p.astype(bf16), v)
            return carry

        lax.fori_loop(0, 1024 // KB, block, 0)


def attend_back_blocks(slabs, s, q_ref, do_ref, lse_ref, delta_ref, kv_ref, dq_ref, dkv_ref):
    factor = score_scale * LOG2E
    for g in slabs:
        first = g * CH

        def block(b, carry, g=g, first=first):
            pair = kv_ref[g, pl.ds(b * 4, 4)].reshape(KB, 2 * KC)
            k, v = pair[:, :KC], pair[:, KC:]
            dk = jnp.zeros((KB, HD), f32)
            dv = jnp.zeros((KB, HD), f32)
            for r0 in range(first, NROW, 256):
                r1 = min(r0 + 256, NROW)
                q = q_ref[r0:r1]
                do = do_ref[r0:r1]
                p = jnp.exp2(mul_rows(k, q) * factor - lse_ref[:, r0:r1])
                if r0 == first:
                    row = lax.broadcasted_iota(jnp.int32, (KB, r1 - r0), 1)
                    col = lax.broadcasted_iota(jnp.int32, (KB, r1 - r0), 0)
                    seen = (row >= CH) | (s * ROWS + (row & (ROWS - 1)) >= b * KB + col)
                    p = jnp.where(seen, p, 0.0)
                ds = (p * (mul_rows(v, do) - delta_ref[:, r0:r1])).astype(bf16)
                dv = dv + mul(p.astype(bf16), do)
                dk = dk + mul(ds, q)
                dq_ref[r0:r1] += mul_tokens(ds, k)
            both = jnp.concatenate([dk * score_scale, dv], axis=1).astype(bf16)
            dkv_ref[g, b] = both.reshape(2, 2, ROWS, 2 * KC)
            return carry

        lax.fori_loop(0, 1024 // KB, block, 0)


def local(
    tokens, norm_gain, w_query, key_matrix, value_matrix, query_gain, key_gain, w_out, ffn_gain,
    w_gate, w_up, w_down, cotangent,
):
    s = (lax.axis_index("x") * 2 + lax.axis_index("c")) * 2 + lax.axis_index("t")
    at = jnp.arange(TOK, dtype=jnp.int32)
    position = (at // ROWS) * (NT * ROWS) + s * ROWS + at % ROWS
    exponent = jnp.arange(0, HD, 2, dtype=f32) / HD
    angles = position.astype(f32)[:, None] * (1.0 / rope_base**exponent)[None, :]
    cosine = jnp.cos(angles)
    sine = jnp.sin(angles)
    cosine = jnp.concatenate([cosine, cosine], axis=1)
    sine = jnp.concatenate([-sine, sine], axis=1)
    (
        middle, grad_middle, gain_two, query_rows, grad_rows, lse2, delta, qk_pre, context_bf, part_two,
        grad_middle_all, kv_all, qkv, normed_all, ffn_partial,
    ) = forward(
        tokens, cotangent, norm_gain.reshape(1, D), ffn_gain.reshape(1, D), query_gain.reshape(1, HD),
        key_gain.reshape(1, HD), cosine, sine,
        w_query, key_matrix, value_matrix, w_out, w_gate, w_up, w_down,
    )
    result, grad_input, gains, back = backward(
        tokens, middle, grad_middle, gain_two, norm_gain.reshape(1, D), query_gain.reshape(1, HD),
        key_gain.reshape(1, HD), cosine, sine, query_rows, grad_rows, lse2, delta, qk_pre, context_bf,
        grad_middle_all, part_two, kv_all, qkv, normed_all,
        ffn_partial.reshape(NW, 4, 2, 2, 16, PARTIAL),
    )
    gains = gains[0]
    back = back.reshape(4, 32, COLS).transpose(1, 0, 2).astype(f32)
    grads, at = [], 0
    for w in (QC, QC, KC, KC, FC, FC, FC):
        grads.append(back[:, :, at : at + w].reshape(32, -1))
        at += w
    grad_out, grad_query, grad_key, grad_value, grad_gate, grad_up, grad_down = grads
    return (
        result, grad_input, gains[:D], grad_query, grad_key, grad_value, gains[2 * D : 2 * D + HD],
        gains[2 * D + HD :], grad_out, gains[D : 2 * D], grad_gate, grad_up, grad_down,
    )


def solution(mesh):
    fine = Mesh(mesh.devices.reshape(4, 2, 4, 2, 2), AXES)
    rows = P(AXES, None)
    weight = P(("z", "yl", "x", "c"), "t")
    return jax.shard_map(
        local,
        mesh=fine,
        in_specs=(rows, P(), weight, weight, weight, P(), P(), weight, P(), weight, weight, weight, rows),
        out_specs=(
            rows, rows, P(), weight, weight, weight, P(), P(), weight, P(), weight, weight, weight,
        ),
        check_vma=False,
    )
```

```python
import functools

import jax
import jax.numpy as jnp
from jax import lax
from jax.experimental import pallas as pl
from jax.experimental.pallas import tpu as pltpu
from jax.sharding import Mesh
from jax.sharding import PartitionSpec as P

AXES = ("z", "yl", "x", "c", "t")
SIZES = {"z": 4, "yl": 2, "x": 4, "c": 2, "t": 2}
W_AXES = ("z", "yl")
T_AXES = ("x", "c", "t")
NW, NT = 8, 16
ROWS = 64
TOK = NW * ROWS
D = 2048
HD = 128
SEQ = 8192
QC, KC, FC = 256, 128, 768
QKV = QC + 2 * KC
COLS = QKV + QC + 3 * FC
VMEM_LIMIT = 63 << 20
KB = 256
CH = 2 * ROWS
NROW = NW * CH

epsilon = 1e-06
rope_base = 1000000.0
score_scale = HD ** (-0.5)
LOG2E = 1.4426950408889634

bf16 = jnp.bfloat16
f32 = jnp.float32
MESH = pl.DeviceIdType.MESH
VM = pl.BlockSpec(memory_space=pltpu.VMEM)
ANY = pl.BlockSpec(memory_space=pl.ANY)
DMA = pltpu.SemaphoreType.DMA


def params(cid=None):
    if cid is None:
        return pltpu.CompilerParams(vmem_limit_bytes=VMEM_LIMIT)
    return pltpu.CompilerParams(
        collective_id=cid, has_side_effects=True, vmem_limit_bytes=VMEM_LIMIT
    )


def place():
    return {a: lax.axis_index(a) for a in AXES}


def shifted(me, axis, by):
    return lax.rem(me[axis] + by, SIZES[axis])


def barrier(devices):
    sem = pltpu.get_barrier_semaphore()
    for d in devices:
        pl.semaphore_signal(sem, inc=1, device_id=d, device_id_type=MESH)
    pl.semaphore_wait(sem, len(devices))


def remote(src, dst, ssem, rsem, device):
    return pltpu.make_async_remote_copy(
        src_ref=src, dst_ref=dst, send_sem=ssem, recv_sem=rsem, device_id=device, device_id_type=MESH
    )


class Sends:
    def __init__(self, ssem, rsem, base=0):
        self.ssem, self.rsem, self.base, self.open = ssem, rsem, base, []

    def send(self, kind, src, dst, device):
        k = self.base + kind
        remote(src(), dst(), self.ssem.at[k], self.rsem.at[k], device).start()
        self.open.append((k, src, device))

    def recv(self, kind, dst, device):
        k = self.base + kind
        remote(dst, dst, self.ssem.at[k], self.rsem.at[k], device).wait_recv()

    def close(self):
        for k, src, device in self.open:
            remote(src(), src(), self.ssem.at[k], self.rsem.at[k], device).wait_send()
        self.open = []


def w_devices(me):
    return (
        {"z": shifted(me, "z", 1)},
        {"z": shifted(me, "z", 3)},
        {"yl": 1 - me["yl"]},
    )


class GatherW:
    SEMS = 14

    def __init__(self, me, dst, sends):
        self.me, self.dst, self.s = me, dst, sends
        z, y = me["z"], me["yl"]
        zp, zm, zo, yo = shifted(me, "z", 1), shifted(me, "z", 3), shifted(me, "z", 2), 1 - y
        self.own, self.own_o = 2 * z + y, 2 * z + yo
        self.gp, self.gpo = 2 * zp + y, 2 * zp + yo
        self.gm, self.gmo = 2 * zm + y, 2 * zm + yo
        self.go, self.goo = 2 * zo + y, 2 * zo + yo
        self.dp, self.dm, self.dy = w_devices(me)

    def part(self, g, lo, hi):
        return self.dst.at[g, lo:hi]

    def put(self, kind, g, lo, hi, device):
        def piece():
            return self.part(g, lo, hi)

        self.s.send(kind, piece, piece, device)

    def got(self, kind, g, lo, hi, device):
        self.s.recv(kind, self.part(g, lo, hi), device)

    def start(self):
        self.put(0, self.own, 0, 64, self.dp)
        self.put(1, self.own, 0, 64, self.dm)
        self.put(2, self.own, 0, 64, self.dy)

    def middle(self):
        dp, dm, dy = self.dp, self.dm, self.dy
        self.got(2, self.own_o, 0, 64, dy)
        self.put(3, self.own_o, 0, 32, dp)
        self.put(4, self.own_o, 0, 32, dm)
        self.got(0, self.gm, 0, 64, dm)
        self.put(5, self.gm, 16, 48, dp)
        self.put(6, self.gm, 32, 64, dy)
        self.got(1, self.gp, 0, 64, dp)
        self.put(7, self.gp, 0, 16, dm)
        self.put(8, self.gp, 48, 64, dm)
        self.put(9, self.gp, 32, 64, dy)

    def end(self):
        dp, dm, dy = self.dp, self.dm, self.dy
        self.got(3, self.gmo, 0, 32, dm)
        self.put(10, self.gmo, 16, 32, dp)
        self.got(4, self.gpo, 0, 32, dp)
        self.put(11, self.gpo, 0, 16, dm)
        self.got(5, self.go, 16, 48, dm)
        self.put(12, self.go, 32, 48, dy)
        self.got(8, self.go, 48, 64, dp)
        self.put(13, self.go, 48, 64, dy)
        self.got(7, self.go, 0, 16, dp)
        self.got(6, self.gmo, 32, 64, dy)
        self.got(9, self.gpo, 32, 64, dy)
        self.got(10, self.goo, 16, 32, dm)
        self.got(11, self.goo, 0, 16, dp)
        self.got(12, self.goo, 32, 48, dy)
        self.got(13, self.goo, 48, 64, dy)


class SumW:
    SEMS = 13
    LAND = (32, 32, 32, 16, 16, 32, 32, 32, 32, 64, 64, 64)

    def __init__(self, me, part, land, sends):
        self.part, self.land, self.s = part, land, sends
        z, y = me["z"], me["yl"]
        zp, zm, zo, yo = shifted(me, "z", 1), shifted(me, "z", 3), shifted(me, "z", 2), 1 - y
        self.own, self.own_o = 2 * z + y, 2 * z + yo
        self.gp, self.gpo = 2 * zp + y, 2 * zp + yo
        self.gm, self.gmo = 2 * zm + y, 2 * zm + yo
        self.go, self.goo = 2 * zo + y, 2 * zo + yo
        self.dp, self.dm, self.dy = w_devices(me)
        self.offset = [sum(self.LAND[:k]) for k in range(len(self.LAND))]

    def slot(self, kind, lo=0, n=None):
        n = self.LAND[kind] if n is None else n
        at = self.offset[kind] + lo
        return self.land.at[at // ROWS, at % ROWS : at % ROWS + n]

    def put(self, kind, g, lo, hi, device):
        self.s.send(kind, lambda: self.part.at[g, lo:hi], lambda: self.slot(kind), device)

    def got(self, kind, device):
        self.s.recv(kind, self.slot(kind), device)

    def add(self, kind, g, lo, hi):
        rows = self.slot(kind)
        self.part[g, lo:hi] = (self.part[g, lo:hi].astype(f32) + rows[...].astype(f32)).astype(bf16)

    def leaf(self):
        dp, dm, dy = self.dp, self.dm, self.dy
        self.put(0, self.goo, 32, 64, dy)
        self.put(3, self.goo, 16, 32, dm)
        self.put(4, self.goo, 0, 16, dp)
        self.put(1, self.gmo, 32, 64, dy)
        self.put(2, self.gpo, 32, 64, dy)

    def two(self):
        dp, dm, dy = self.dp, self.dm, self.dy
        self.got(0, dy)
        self.add(0, self.go, 32, 64)
        self.put(5, self.go, 16, 48, dm)
        self.s.send(6, lambda: self.part.at[self.go, 0:16], lambda: self.slot(6, 0, 16), dp)
        self.s.send(11, lambda: self.part.at[self.go, 48:64], lambda: self.slot(6, 16, 16), dp)
        self.got(3, dp)
        self.add(3, self.gmo, 16, 32)
        self.put(7, self.gmo, 0, 32, dm)
        self.got(4, dm)
        self.add(4, self.gpo, 0, 16)
        self.put(8, self.gpo, 0, 32, dp)

    def three(self):
        dp, dm, dy = self.dp, self.dm, self.dy
        self.got(1, dy)
        self.add(1, self.gm, 32, 64)
        self.got(5, dp)
        self.add(5, self.gm, 16, 48)
        self.put(9, self.gm, 0, 64, dm)
        self.got(2, dy)
        self.add(2, self.gp, 32, 64)
        self.s.recv(6, self.slot(6, 0, 16), dm)
        self.s.recv(11, self.slot(6, 16, 16), dm)
        for lo, hi, at in ((0, 16, 0), (48, 64, 16)):
            rows = self.slot(6, at, 16)
            self.part[self.gp, lo:hi] = (
                self.part[self.gp, lo:hi].astype(f32) + rows[...].astype(f32)
            ).astype(bf16)
        self.put(10, self.gp, 0, 64, dp)
        self.got(7, dp)
        self.add(7, self.own_o, 0, 32)
        self.got(8, dm)
        self.add(8, self.own_o, 0, 32)
        self.s.send(12, lambda: self.part.at[self.own_o], lambda: self.slot(11), dy)

    def total(self):
        dp, dm, dy = self.dp, self.dm, self.dy
        self.got(9, dp)
        self.got(10, dm)
        self.s.recv(12, self.slot(11), dy)
        total = self.part[self.own].astype(f32) + self.slot(9)[...].astype(f32)
        return total + self.slot(10)[...].astype(f32) + self.slot(11)[...].astype(f32)

    def run(self):
        self.leaf()
        self.two()
        self.three()
        return self.total()


def t_devices(me):
    return (
        {"x": shifted(me, "x", 1)},
        {"x": shifted(me, "x", 3)},
        {"t": 1 - me["t"]},
        {"c": 1 - me["c"]},
    )


class GatherT:
    SEMS = 19

    def __init__(self, me, dst, sends):
        self.dst, self.s = dst, sends
        x, c, t = me["x"], me["c"], me["t"]
        xp, xm, xo = shifted(me, "x", 1), shifted(me, "x", 3), shifted(me, "x", 2)
        to, oc = 1 - t, 1 - c
        places = {
            "own": (x, t), "to": (x, to), "p": (xp, t), "po": (xp, to),
            "m": (xm, t), "mo": (xm, to), "o": (xo, t), "oo": (xo, to),
        }
        self.ids = {k: (v[0], c, v[1]) for k, v in places.items()}
        self.sib = {k: (v[0], oc, v[1]) for k, v in places.items()}
        self.dp, self.dm, self.dt, self.dc = t_devices(me)

    def part(self, place, half):
        lo, hi = {None: (0, 8), 0: (0, 4), 1: (4, 8)}[half]
        return self.dst.at[(slice(lo, hi),) + place]

    def put(self, kind, name, device, half=None):
        p = self.ids[name]

        def piece():
            return self.part(p, half)

        self.s.send(kind, piece, piece, device)

    def got(self, kind, name, device, half=None, sib=False):
        p = (self.sib if sib else self.ids)[name]
        self.s.recv(kind, self.part(p, half), device)

    def start(self):
        self.put(2, "own", self.dt)
        self.put(0, "own", self.dp)
        self.put(1, "own", self.dm)
        self.put(3, "own", self.dc)

    def middle(self):
        dp, dm, dt, dc = self.dp, self.dm, self.dt, self.dc
        self.got(2, "to", dt)
        self.put(4, "to", dp)
        self.put(5, "to", dm)
        self.put(6, "to", dc)
        self.got(0, "m", dm)
        self.put(7, "m", dp, 0)
        self.put(8, "m", dc)
        self.got(1, "p", dp)
        self.put(9, "p", dm, 1)
        self.put(10, "p", dc)

    def late(self):
        dp, dm, dc = self.dp, self.dm, self.dc
        self.got(4, "mo", dm)
        self.put(11, "mo", dp, 0)
        self.put(12, "mo", dc)
        self.got(5, "po", dp)
        self.put(13, "po", dm, 1)
        self.put(14, "po", dc)
        self.got(7, "o", dm, 0)
        self.put(15, "o", dc, 0)
        self.got(9, "o", dp, 1)
        self.put(16, "o", dc, 1)

    def last(self):
        dp, dm, dc = self.dp, self.dm, self.dc
        self.got(11, "oo", dm, 0)
        self.put(17, "oo", dc, 0)
        self.got(13, "oo", dp, 1)
        self.put(18, "oo", dc, 1)

    SIBLING = (
        ((3, "own", None), (6, "to", None)),
        ((10, "p", None), (14, "po", None)),
        ((8, "m", None), (12, "mo", None)),
        ((15, "o", 0), (16, "o", 1), (17, "oo", 0), (18, "oo", 1)),
    )

    def column(self, i):
        for kind, name, half in self.SIBLING[i]:
            self.got(kind, name, self.dc, half, True)

    def end(self):
        self.late()
        self.last()
        for i in range(4):
            self.column(i)


def sems(n):
    return [DMA((n,)), DMA((n,))]


GROUPS = (QKV, QC, 2 * FC, FC)
STARTS = (0, QKV, QKV + QC, QKV + QC + 2 * FC)
GAINS = 2 * D + 2 * HD
PEERS_W = [(dz, dy) for dz in range(4) for dy in range(2) if dz or dy]
PEERS_T = [(dx, dc, dt) for dx in range(4) for dc in range(2) for dt in range(2) if dx or dc or dt]


def rms(v):
    return lax.rsqrt(jnp.mean(v * v, axis=-1, keepdims=True) + epsilon)


def mul_rows(a, b):
    return lax.dot_general(a, b, (((1,), (1,)), ((), ())), preferred_element_type=f32)


def mul(a, b):
    return jnp.dot(a, b, preferred_element_type=f32)


def mul_tokens(a, b):
    return lax.dot_general(a, b, (((0,), (0,)), ((), ())), preferred_element_type=f32)


def row_sums(v):
    ones = jnp.ones((8, v.shape[1]), f32)
    return lax.dot_general(
        ones, v, (((1,), (1,)), ((), ())), preferred_element_type=f32, precision=lax.Precision.HIGHEST
    )[0:1]


def head_back(u, g, gain, cosine, sine):
    rolled = jnp.concatenate([g[:, HD // 2 :], g[:, : HD // 2]], axis=1)
    g = g * cosine - rolled * sine
    inv = rms(u)
    normal = u * inv
    total = jnp.sum(g * normal, axis=0, keepdims=True)
    scaled = g * gain
    return inv * (scaled - normal * jnp.mean(scaled * normal, axis=-1, keepdims=True)), total


class SumT:
    SEMS = 9

    def __init__(self, me, src, part, half, land, final, sends):
        self.src, self.part, self.half, self.land, self.final, self.s = src, part, half, land, final, sends
        self.c, self.t = me["c"], me["t"]
        self.oc, self.to = 1 - me["c"], 1 - me["t"]
        self.order = (shifted(me, "x", 2), shifted(me, "x", 3), shifted(me, "x", 1), me["x"])
        self.dp, self.dm, self.dt, self.dc = t_devices(me)
        self.h = part.shape[1] // 2

    def leaf(self, which=range(4)):
        for i in which:
            self.s.send(
                i, lambda i=i: self.src.at[:, self.order[i], self.oc], lambda i=i: self.part.at[i], self.dc
            )

    def pair(self, i):
        self.s.recv(i, self.part.at[i], self.dc)
        mine = self.src[:, self.order[i], self.c]
        self.part[i] = (self.part[i].astype(f32) + mine.astype(f32)).astype(bf16)

    def halves(self):
        self.s.send(4, lambda: self.part.at[0, : self.h], lambda: self.half.at[0], self.dm)
        self.s.send(5, lambda: self.part.at[0, self.h :], lambda: self.half.at[1], self.dp)

    def left(self):
        h = self.h
        self.s.recv(4, self.half.at[0], self.dp)
        self.part[1, :h] = (self.part[1, :h].astype(f32) + self.half[0].astype(f32)).astype(bf16)
        self.s.send(6, lambda: self.part.at[1], lambda: self.land.at[0], self.dm)

    def right(self):
        h = self.h
        self.s.recv(5, self.half.at[1], self.dm)
        self.part[2, h:] = (self.part[2, h:].astype(f32) + self.half[1].astype(f32)).astype(bf16)
        self.s.send(7, lambda: self.part.at[2], lambda: self.land.at[1], self.dp)

    def two(self):
        self.pair(0)
        self.halves()
        self.pair(1)
        self.pair(2)

    def three(self):
        self.left()
        self.right()
        self.pair(3)

    def four(self):
        to = self.to
        self.s.recv(6, self.land.at[0], self.dp)
        self.s.recv(7, self.land.at[1], self.dm)
        self.part[3, :, to] = (
            self.part[3, :, to].astype(f32)
            + self.land[0, :, to].astype(f32)
            + self.land[1, :, to].astype(f32)
        ).astype(bf16)
        self.s.send(8, lambda: self.part.at[3, :, to], lambda: self.final, self.dt)

    def total(self):
        t = self.t
        own = (
            self.part[3, :, t].astype(f32)
            + self.land[0, :, t].astype(f32)
            + self.land[1, :, t].astype(f32)
        )
        self.s.recv(8, self.final, self.dt)
        return own + self.final[...].astype(f32)


def sum_t_scratch(slabs, rows, cols):
    return [
        pltpu.VMEM((4, slabs, 2, rows, cols), bf16),
        pltpu.VMEM((2, slabs // 2, 2, rows, cols), bf16),
        pltpu.VMEM((2, slabs, 2, rows, cols), bf16),
        pltpu.VMEM((slabs, rows, cols), bf16),
    ]


class Return:
    def __init__(self, me, x_ref, out, lo, hi, ssem, rsem, base, lsem):
        self.x, self.out, self.lo, self.hi = x_ref, out, lo, hi
        self.ssem, self.rsem, self.base, self.lsem = ssem, rsem, base, lsem
        self.z, self.y, self.t = me["z"], me["yl"], me["t"]
        self.own_g = 2 * self.z + self.y
        self.holder = self.own_g // 4
        self.block = self.own_g - 4 * self.holder
        self.dy = w_devices(me)[2]

    def each(self, act):
        for g in range(8):
            is_me = (self.own_g == g) & (self.holder == self.t)
            act(g, is_me)

    def start(self):
        def act(g, is_me):
            dst = self.out.at[self.block, self.t, :, self.lo : self.hi]
            to = {"z": jnp.int32(g // 2), "yl": jnp.int32(g % 2), "t": self.holder}
            k = self.base + self.block * 2 + self.t
            c = remote(self.x.at[g], dst, self.ssem.at[self.base + g], self.rsem.at[k], to)
            l = pltpu.make_async_copy(self.x.at[g], dst, self.lsem)

            @pl.when(is_me)
            def _():
                l.start()
                l.wait()

            @pl.when(jnp.logical_not(is_me))
            def _():
                c.start()

        self.each(act)

    def end(self):
        for j in range(4):
            for t2 in range(2):
                is_me = (2 * self.t + j // 2 == self.z) & (j % 2 == self.y) & (self.t == t2)

                @pl.when(jnp.logical_not(is_me))
                def _(j=j, t2=t2):
                    d = self.out.at[j, t2, :, self.lo : self.hi]
                    k = self.base + j * 2 + t2
                    remote(d, d, self.ssem.at[0], self.rsem.at[k], self.dy).wait_recv()

        def act(g, is_me):
            @pl.when(jnp.logical_not(is_me))
            def _():
                x = self.x.at[g]
                remote(x, x, self.ssem.at[self.base + g], self.rsem.at[0], self.dy).wait_send()

        self.each(act)


def rope_rows(angles):
    cosine, sine = angles[:, : HD // 2], angles[:, HD // 2 :]
    return jnp.concatenate([cosine, cosine], axis=1), jnp.concatenate([-sine, sine], axis=1)


def gray(i):
    return i + (i // 2) * (5 - 2 * i)


def seen_keys(s, b, rows, keys_first):
    shape = (KB, rows) if keys_first else (rows, KB)
    row = lax.broadcasted_iota(jnp.int32, shape, 1 if keys_first else 0)
    col = lax.broadcasted_iota(jnp.int32, shape, 0 if keys_first else 1)
    return (row >= CH) | (s * ROWS + (row & (ROWS - 1)) >= b * KB + col)


def attend_column(b, s, q_ref, kv_ref, o_ref, l_ref):
    factor = score_scale * LOG2E
    for g in range(NW):
        pair = kv_ref[g, b].reshape(KB, 2 * KC)
        k, v = pair[:, :KC], pair[:, KC:]
        for r0 in range(g * CH, NROW, 256):
            r1 = min(r0 + 256, NROW)
            p = jnp.exp2(mul_rows(q_ref[r0:r1], k) * factor)
            if r0 == g * CH:
                p = jnp.where(seen_keys(s, b, r1 - r0, False), p, 0.0)
            l_ref[r0:r1] += p[:, :128] + p[:, 128:]
            o_ref[r0:r1] += mul(p.astype(bf16), v)


def attend_back_column(b, s, q_ref, do_ref, lse_ref, delta_ref, kv_ref, dq_ref):
    factor = score_scale * LOG2E
    for g in range(NW):
        pair = kv_ref[g, b].reshape(KB, 2 * KC)
        k, v = pair[:, :KC], pair[:, KC:]
        dk = jnp.zeros((KB, HD), f32)
        dv = jnp.zeros((KB, HD), f32)
        for r0 in range(g * CH, NROW, 256):
            r1 = min(r0 + 256, NROW)
            q = q_ref[r0:r1]
            do = do_ref[r0:r1]
            p = jnp.exp2(mul_rows(k, q) * factor - lse_ref[:, r0:r1])
            if r0 == g * CH:
                p = jnp.where(seen_keys(s, b, r1 - r0, True), p, 0.0)
            ds = (p * (mul_rows(v, do) - delta_ref[:, r0:r1])).astype(bf16)
            dv = dv + mul(p.astype(bf16), do)
            dk = dk + mul(ds, q)
            dq_ref[r0:r1] += mul_tokens(ds, k)
        both = jnp.concatenate([dk * score_scale, dv], axis=1).astype(bf16)
        kv_ref[g, b] = both.reshape(2, 2, ROWS, 2 * KC)


def layer_kernel(
    tok, cot, ngain, fgain, qgain, kgain, angles, wq, wk, wv, wo, wg, wu, wd,
    result, grad_input, gains, back,
    stage, normed_all, cot_all, nt_all, gm_all, kv_all, wqkv, wout, wgu, wdn, part, part_two, land,
    o_acc, l_acc, gate, up, gh, hidden, dgu, q_rows, do_rows, lse, delta, qk_pre, ctx, middle, wdq,
    gsend, gw_land, gt_send, gt_land,
    u1, u2, u3, u4, d1, d2, d3, d4, k1, k2, k3, k4, o1, o2, o3, o4, q1, q2, q3, q4, v1, v2, v3, v4,
    ssem, rsem, lsem,
):
    me = place()
    z, y, x, c, t = (me[a] for a in AXES)
    own_g = 2 * z + y
    s = (x * 2 + c) * 2 + t
    dq = l_acc
    dp, dm, dy = w_devices(me)
    sem = pltpu.get_barrier_semaphore()
    peers = [
        {"z": shifted(me, "z", dz), "yl": shifted(me, "yl", dyl), "t": shifted(me, "t", dt)}
        for dz in range(4) for dyl in range(2) for dt in range(2) if dz or dyl or dt
    ] + [
        {"x": shifted(me, "x", dx), "c": shifted(me, "c", dc), "t": shifted(me, "t", dt)}
        for dx in range(4) for dc in range(2) for dt in range(2) if dx or dc
    ]
    for d in peers:
        pl.semaphore_signal(sem, inc=1, device_id=d, device_id_type=MESH)

    staging, at = [], 0
    for k, w in enumerate((wq, wk, wv, wo, wg, wu, wd)):
        n = w.shape[1] // 4
        for j in range(4):
            piece = w.at[:, j * n : (j + 1) * n]
            staging.append(
                pltpu.make_async_copy(piece, stage.at[j, :, at : at + n], lsem.at[7 + 4 * k + j])
            )
            staging[-1].start()
        at += n
    normed_all[own_g] = (tok[...].astype(f32) * rms(tok[...].astype(f32)) * ngain[...]).astype(bf16)
    cot_all[own_g] = cot[...]
    for l in staging:
        l.wait()
    pl.semaphore_wait(sem, len(peers))

    count = [0]
    opened = []

    def base(n):
        count[0] += n
        return count[0] - n

    def make(kind, *args):
        got = kind(me, *args, Sends(ssem, rsem, base(kind.SEMS)))
        opened.append(got)
        return got

    full = (wqkv, wout, wgu, wdn)
    to_base = base(32)
    holder = own_g // 4

    def to_holders(groups):
        for j in range(4):
            for t2 in range(2):
                dst_z, dst_y = 2 * t + j // 2, j % 2
                is_me = (dst_z == z) & (dst_y == y) & (t == t2)
                src = stage.at[j, 16 * t2 : 16 * t2 + 16]
                to = {"z": dst_z, "yl": dst_y, "t": jnp.int32(t2)}
                remotes, locals_ = [], []
                for k in groups:
                    piece = src.at[:, STARTS[k] : STARTS[k] + GROUPS[k]]
                    remotes.append(
                        remote(
                            piece, full[k].at[own_g, x, c, t2], ssem.at[to_base + 8 * k + 2 * j + t2],
                            rsem.at[to_base + 8 * k + own_g], to,
                        )
                    )
                    locals_.append(pltpu.make_async_copy(piece, full[k].at[own_g, x, c, t], lsem.at[k]))

                @pl.when(is_me)
                def _():
                    for l in locals_:
                        l.start()
                    for l in locals_:
                        l.wait()

                @pl.when(jnp.logical_not(is_me))
                def _():
                    for r in remotes:
                        r.start()

    def from_owners(groups):
        for g in range(8):
            from_me = (own_g == g) & (holder == t)

            @pl.when(jnp.logical_not(from_me))
            def _(g=g):
                for k in groups:
                    dst = full[k].at[g, x, c, t]
                    remote(dst, dst, ssem.at[0], rsem.at[to_base + 8 * k + g], dy).wait_recv()

    gw = make(GatherW, normed_all)
    gq, go, gg, gd = [make(GatherT, w) for w in full]
    gk = make(GatherT, kv_all)
    gc = make(GatherW, cot_all)

    to_holders((0,))
    gw.start()
    to_holders((1, 2, 3))
    from_owners((0,))
    gq.start()
    gw.middle()
    gq.middle()
    from_owners((1, 2, 3))
    gg.start()
    go.start()
    gw.end()
    gq.end()

    for h in range(2):
        rows = slice(h * 256, h * 256 + 256)
        pre = mul(normed_all[4 * h : 4 * h + 4].reshape(256, D), wqkv[...].reshape(D, QKV))
        qk_pre[rows] = pre[:, : QC + KC]
        cosine, sine = rope_rows(angles[rows])
        for head in range(3):
            u = pre[:, head * HD : head * HD + HD]
            n = u * rms(u) * (qgain if head < 2 else kgain)[...]
            rolled = jnp.concatenate([n[:, HD // 2 :], n[:, : HD // 2]], axis=1)
            rot = (n * cosine + rolled * sine).astype(bf16)
            for i in range(4):
                g = 4 * h + i
                piece = rot[i * ROWS : i * ROWS + ROWS]
                if head < 2:
                    q_rows[g * CH + head * ROWS : g * CH + head * ROWS + ROWS] = piece
                else:
                    kv_all[g, x, c, t, :, :KC] = piece
        val = pre[:, QC + KC :].astype(bf16)
        for i in range(4):
            kv_all[4 * h + i, x, c, t, :, KC:] = val[i * ROWS : i * ROWS + ROWS]
    gk.start()
    gc.start()
    o_acc[...] = jnp.zeros_like(o_acc)
    l_acc[...] = jnp.zeros_like(l_acc)
    gk.middle()
    gk.column(0)

    def attend_step(i, carry):
        @pl.when(i == 1)
        def _():
            gk.late()
            gk.column(1)
            go.middle()
            gg.middle()
            gc.middle()

        @pl.when(i == 2)
        def _():
            gk.last()
            gk.column(2)
            go.late()
            gd.start()

        @pl.when(i == 3)
        def _():
            gk.column(3)
            go.last()
            gc.end()

        attend_column(lax.rem(x + gray(i), 4), s, q_rows, kv_all, o_acc, l_acc)
        return carry

    lax.fori_loop(0, 4, attend_step, 0)
    for i in range(4):
        go.column(i)

    lse[...] = jnp.log2(row_sums(l_acc[...]))
    for g in range(NW):
        rows = slice(g * CH, g * CH + CH)
        o = o_acc[rows] / jnp.sum(l_acc[rows], axis=1, keepdims=True)
        o_acc[rows] = o
        ctx[g * ROWS : g * ROWS + ROWS, :HD] = o[:ROWS].astype(bf16)
        ctx[g * ROWS : g * ROWS + ROWS, HD:] = o[ROWS:].astype(bf16)

    def out_rows(dst, a, w_ref, cols):
        for n in range(4):
            w = w_ref[2 * n : 2 * n + 2].reshape(512, cols)
            dst[:, :, n * 512 : n * 512 + 512] = mul_rows(a[...], w).astype(bf16).reshape(NW, ROWS, 512)

    out_rows(part, ctx, wout, QC)
    sw = make(SumW, part, land)
    sw.leaf()
    gg.late()
    gd.middle()
    sw.two()
    sw.three()
    mid = tok[...].astype(f32) + sw.total()
    middle[...] = mid
    nt_all[own_g] = (mid * rms(mid) * fgain[...]).astype(bf16)
    gn = make(GatherW, nt_all)
    gn.start()
    gg.last()
    gd.late()
    gd.last()
    gn.middle()
    for i in range(4):
        gg.column(i)
        gd.column(i)
    for n in range(3):
        cols = slice(n * 256, n * 256 + 256)
        gh[:, cols] = mul(cot_all[...].reshape(TOK, D), wdn[:, :, :, :, :, cols].reshape(D, 256))
    gn.end()

    for n in range(3):
        cols = slice(n * 256, n * 256 + 256)
        upper = slice(FC + n * 256, FC + n * 256 + 256)
        nt = nt_all[...].reshape(TOK, D)
        gate[...] = mul(nt, wgu[:, :, :, :, :, cols].reshape(D, 256))
        up[...] = mul(nt, wgu[:, :, :, :, :, upper].reshape(D, 256))

        def units(i, carry, cols=cols, upper=upper):
            rows = pl.ds(pl.multiple_of(i * 64, 64), 64)
            gv, uv, hv = gate[rows], up[rows], gh[rows, cols]
            sig = jax.nn.sigmoid(gv)
            act = gv * sig
            hidden[rows, cols] = (act * uv).astype(bf16)
            dgu[rows, cols] = (hv * uv * (sig * (1.0 + gv * (1.0 - sig)))).astype(bf16)
            dgu[rows, upper] = (hv * act).astype(bf16)
            return carry

        lax.fori_loop(0, TOK // 64, units, 0)
    for got in (sw, gg, gd, gw, gc, gn):
        got.s.close()
    out_rows(part, dgu, wgu, 2 * FC)
    sb = make(SumW, part, land)
    sb.leaf()
    out_rows(part_two, hidden, wdn, FC)

    def weight_grads(lo, hi):
        def step(g, carry):
            cols = pl.ds(pl.multiple_of(g * 256, 256), 256)
            a = nt_all[:, :, cols].reshape(TOK, 256)
            for n in range(3):
                w = slice(n * 512, n * 512 + 512)
                wgu[g, :, :, :, :, w] = mul_tokens(a, dgu[:, w]).astype(bf16).reshape(4, 2, 2, 16, 512)
            b = cot_all[:, :, cols].reshape(TOK, 256)
            for n in range(3):
                w = slice(n * 256, n * 256 + 256)
                wdn[g, :, :, :, :, w] = mul_tokens(b, hidden[:, w]).astype(bf16).reshape(4, 2, 2, 16, 256)
            return carry

        lax.fori_loop(lo, hi, step, 0)

    weight_grads(0, 1)
    sb.two()
    weight_grads(1, 3)
    sb.three()
    weight_grads(3, 5)
    gnt = sb.total()
    mid = middle[...]
    inv = rms(mid)
    normal = mid * inv
    gsend[:, D : 2 * D] = jnp.sum(gnt * normal, axis=0, keepdims=True)
    scaled = gnt * fgain[...]
    gm = cot[...].astype(f32) + inv * (
        scaled - normal * jnp.mean(scaled * normal, axis=-1, keepdims=True)
    )
    grad_input[...] = gm
    gm_all[own_g] = gm.astype(bf16)
    ga = make(GatherW, gm_all)
    ga.start()
    weight_grads(5, 8)
    su = make(SumT, wgu, u1, u2, u3, u4)
    sd = make(SumT, wdn, d1, d2, d3, d4)
    su.leaf()
    ga.middle()
    su.pair(0)
    su.halves()
    ga.end()
    grad_ctx = mul(gm_all[...].reshape(TOK, D), wout[...].reshape(D, QC)).astype(bf16)
    for g in range(NW):
        for head in range(2):
            do_rows[g * CH + head * ROWS : g * CH + head * ROWS + ROWS] = grad_ctx[
                g * ROWS : g * ROWS + ROWS, head * HD : head * HD + HD
            ]
    delta[...] = row_sums(do_rows[...].astype(f32) * o_acc[...])
    dq[...] = jnp.zeros_like(dq)
    gk.s.close()
    sr = make(SumW, part_two, nt_all)
    sk = make(SumT, kv_all, k1, k2, k3, k4)
    sr.leaf()
    su.pair(1)
    su.pair(2)
    sd.leaf()
    def weight_step(dst, at, a_ref, b_ref, lo, hi):
        def step(g, carry):
            a = a_ref[:, :, pl.ds(pl.multiple_of(g * 256, 256), 256)].reshape(TOK, 256)
            dst[g, :, :, :, :, at : at + 256] = (
                mul_tokens(a, b_ref[:, lo:hi]).astype(bf16).reshape(4, 2, 2, 16, 256)
            )
            return carry

        lax.fori_loop(0, NW, step, 0)

    go.s.close()
    weight_step(wout, 0, gm_all, ctx, 0, QC)
    so = make(SumT, wout, o1, o2, o3, o4)
    so.leaf()

    def give_back(summed, lo, hi, l):
        summed.final[...] = summed.total().astype(bf16)
        r = Return(me, summed.final, back, lo, hi, ssem, rsem, summed.back, lsem.at[l])
        r.start()
        return r

    for summed in (su, sd, so):
        summed.back = base(8)

    def back_step(i, carry):
        attend_back_column(
            lax.rem(x + gray(3 - i), 4), s, q_rows, do_rows, lse, delta, kv_all, dq
        )

        @pl.when(i == 0)
        def _():
            sk.leaf((0,))
            su.three()
            sr.two()

        @pl.when(i == 1)
        def _():
            sk.leaf((1,))
            sk.pair(0)
            sk.halves()
            sd.two()
            sr.three()

        @pl.when(i == 2)
        def _():
            sk.leaf((2,))
            sk.pair(1)
            sk.left()
            su.four()
            sd.three()
            result[...] = (middle[...] + sr.total()).astype(bf16)

        @pl.when(i == 3)
        def _():
            sk.leaf((3,))
            sk.pair(2)
            sk.right()
            sk.pair(3)
            so.two()
            sd.four()

        return carry

    lax.fori_loop(0, 4, back_step, 0)

    gp = dgu.at[:, :QKV]
    cosine, sine = rope_rows(angles[...])
    for head in range(2):
        u = qk_pre[:, head * HD : head * HD + HD]
        g = dq[...].reshape(NW, 2, ROWS, HD)[:, head].reshape(TOK, HD) * score_scale
        dpre, gain = head_back(u, g, qgain[...], cosine, sine)
        gp[:, head * HD : head * HD + HD] = dpre.astype(bf16)
        where = slice(2 * D, 2 * D + HD)
        gsend[:, where] = gain if head == 0 else gsend[:, where] + gain

    sk.four()
    so.three()
    returns = [give_back(su, 3 * QC, 3 * QC + 2 * FC, 4)]
    weight_step(wdq, 0, normed_all, gp, 0, QC)
    sq = make(SumT, wdq, q1, q2, q3, q4)
    sq.leaf()
    own_kv = sk.total().reshape(TOK, 2 * KC)
    dpre, gain = head_back(qk_pre[:, QC:], own_kv[:, :KC], kgain[...], cosine, sine)
    gp[:, QC : QC + KC] = dpre.astype(bf16)
    gp[:, QC + KC :] = own_kv[:, KC:].astype(bf16)
    gsend[:, 2 * D + HD :] = gain
    sb.s.close()
    out_rows(part, gp, wqkv, QKV)
    sl = make(SumW, part, land)
    total = jnp.zeros((1, D), f32)
    for g in range(NW):
        both = part[g].astype(f32) * normed_all[g].astype(f32)
        total = total + jnp.sum(both, axis=0, keepdims=True)
    gsend[:, :D] = total / ngain[...]
    sl.leaf()

    bw = base(len(PEERS_W))
    bt = base(len(PEERS_T))
    first = []
    for i, (dz, dyl) in enumerate(PEERS_W):
        d = {"z": shifted(me, "z", dz), "yl": shifted(me, "yl", dyl)}
        first.append(remote(gsend, gw_land.at[i], ssem.at[bw + i], rsem.at[bw + i], d))
        first[-1].start()
    gq.s.close()
    weight_step(wqkv, QC, normed_all, gp, QC, QKV)
    sv = make(SumT, wqkv.at[:, :, :, :, :, QC:], v1, v2, v3, v4)
    sv.leaf()
    sq.two()
    sl.two()
    total = gsend[...]
    for i, r in enumerate(first):
        r.wait_recv()
        total = total + gw_land[i]
    gt_send[...] = total
    second = []
    for i, (dx, dc, dt) in enumerate(PEERS_T):
        d = {"x": shifted(me, "x", dx), "c": shifted(me, "c", dc), "t": shifted(me, "t", dt)}
        second.append(remote(gt_send, gt_land.at[i], ssem.at[bt + i], rsem.at[bt + i], d))
        second[-1].start()
    sv.two()
    sq.three()
    sl.three()
    so.four()
    returns.append(give_back(sd, 3 * QC + 2 * FC, COLS, 5))
    sv.three()
    sq.four()
    gnorm = sl.total()
    xs = tok[...].astype(f32)
    inv = rms(xs)
    normal = xs * inv
    scaled = gnorm * ngain[...]
    grad_input[...] += inv * (
        scaled - normal * jnp.mean(scaled * normal, axis=-1, keepdims=True)
    )
    sv.four()
    sq.back = base(8)
    sv.back = base(8)
    returns.append(give_back(so, 0, QC, 6))
    returns.append(give_back(sq, QC, 2 * QC, 6))
    returns.append(give_back(sv, 2 * QC, 3 * QC, 6))
    for i, r in enumerate(second):
        r.wait_recv()
        total = total + gt_land[i]
    gains[...] = total
    for r in first + second:
        r.wait_send()
    for r in returns:
        r.end()
    for j in range(4):
        for t2 in range(2):
            is_me = (2 * t + j // 2 == z) & (j % 2 == y) & (t == t2)

            @pl.when(jnp.logical_not(is_me))
            def _(j=j, t2=t2):
                src = stage.at[j, 16 * t2 : 16 * t2 + 16]
                for k in range(4):
                    piece = src.at[:, STARTS[k] : STARTS[k] + GROUPS[k]]
                    remote(
                        piece, piece, ssem.at[to_base + 8 * k + 2 * j + t2], rsem.at[0], dy
                    ).wait_send()
    for got in opened:
        got.s.close()
    assert count[0] == LAYER_SEMS, count[0]


LAYER_SEMS = (
    4 * GatherW.SEMS + 5 * GatherT.SEMS + 4 * SumW.SEMS + 6 * SumT.SEMS + 32 + 5 * 8
    + len(PEERS_W) + len(PEERS_T)
)


def layer(*args):
    def out(shape, dtype):
        return jax.ShapeDtypeStruct(shape, dtype)

    def vmem(shape, dtype=bf16):
        return pltpu.VMEM(shape, dtype)

    def weight(cols):
        return vmem((NW, 4, 2, 2, 16, cols))

    rows = vmem((NW, ROWS, D))
    return pl.pallas_call(
        layer_kernel,
        out_shape=(
            out((ROWS, D), bf16), out((ROWS, D), f32), out((1, GAINS), f32), out((4, 2, 16, COLS), bf16),
        ),
        in_specs=[VM] * 7 + [ANY] * 7,
        out_specs=(VM,) * 4,
        scratch_shapes=[
            vmem((4, 32, COLS)), rows, rows, rows, rows, vmem((NW, 4, 2, 2, ROWS, 2 * KC)),
            weight(QKV), weight(QC), weight(2 * FC), weight(FC), rows, rows,
            vmem((sum(SumW.LAND) // ROWS, ROWS, D)),
            vmem((NROW, HD), f32), vmem((NROW, HD), f32), vmem((TOK, 256), f32), vmem((TOK, 256), f32),
            vmem((TOK, FC), f32), vmem((TOK, FC)), vmem((TOK, 2 * FC)), vmem((NROW, HD)), vmem((NROW, HD)),
            vmem((1, NROW), f32), vmem((1, NROW), f32), vmem((TOK, QC + KC), f32), vmem((TOK, QC)),
            vmem((ROWS, D), f32), weight(QC),
            vmem((1, GAINS), f32), vmem((len(PEERS_W), 1, GAINS), f32),
            vmem((1, GAINS), f32), vmem((len(PEERS_T), 1, GAINS), f32),
        ]
        + sum_t_scratch(NW, 16, 2 * FC)
        + sum_t_scratch(NW, 16, FC)
        + sum_t_scratch(NW, ROWS, 2 * KC)
        + sum_t_scratch(NW, 16, QC)
        + sum_t_scratch(NW, 16, QC)
        + sum_t_scratch(NW, 16, QC)
        + sems(LAYER_SEMS) + [DMA((35,))],
        compiler_params=params(0),
        name="layer",
    )(*args)


def finish_kernel(
    result_in, grad_in, gains_in, back,
    result, grad_input, gain_one, gain_q, gain_k, gain_two, g_out, g_q, g_k, g_v, g_gate, g_up, g_down,
):
    result[...] = result_in[...]
    grad_input[...] = grad_in[...]
    gain_one[...] = gains_in[:, :D]
    gain_two[...] = gains_in[:, D : 2 * D]
    gain_q[...] = gains_in[:, 2 * D : 2 * D + HD]
    gain_k[...] = gains_in[:, 2 * D + HD :]
    at = 0
    for grad in (g_out, g_q, g_k, g_v, g_gate, g_up, g_down):
        n = grad.shape[1] // 4
        for j in range(4):
            grad[:, j * n : j * n + n] = back[j, :, :, at : at + n].reshape(32, n).astype(f32)
        at += n


def finish(*args):
    def out(rows, cols, dtype=f32):
        return jax.ShapeDtypeStruct((rows, cols), dtype)

    widths = (QC, QC, KC, KC, FC, FC, FC)
    return pl.pallas_call(
        finish_kernel,
        out_shape=(
            out(ROWS, D, bf16), out(ROWS, D), out(1, D), out(1, HD), out(1, HD), out(1, D),
        ) + tuple(out(32, 4 * n) for n in widths),
        in_specs=[VM] * 4,
        out_specs=(VM,) * 13,
        compiler_params=params(),
        name="finish",
    )(*args)


def local(
    tokens, norm_gain, w_query, key_matrix, value_matrix, query_gain, key_gain, w_out, ffn_gain,
    w_gate, w_up, w_down, cotangent,
):
    s = (lax.axis_index("x") * 2 + lax.axis_index("c")) * 2 + lax.axis_index("t")
    at = jnp.arange(TOK, dtype=jnp.int32)
    position = (at // ROWS) * (NT * ROWS) + s * ROWS + at % ROWS
    exponent = jnp.arange(0, HD, 2, dtype=f32) / HD
    angles = position.astype(f32)[:, None] * (1.0 / rope_base**exponent)[None, :]
    result, grad_input, gains, back = layer(
        tokens, cotangent, norm_gain.reshape(1, D), ffn_gain.reshape(1, D), query_gain.reshape(1, HD),
        key_gain.reshape(1, HD), jnp.concatenate([jnp.cos(angles), jnp.sin(angles)], axis=1),
        w_query, key_matrix, value_matrix, w_out, w_gate, w_up, w_down,
    )
    (
        result, grad_input, gain_one, gain_q, gain_k, gain_two, grad_out, grad_query, grad_key, grad_value,
        grad_gate, grad_up, grad_down,
    ) = finish(result, grad_input, gains, back)
    return (
        result, grad_input, gain_one.reshape(D), grad_query, grad_key, grad_value, gain_q.reshape(HD),
        gain_k.reshape(HD), grad_out, gain_two.reshape(D), grad_gate, grad_up, grad_down,
    )


def solution(mesh):
    fine = Mesh(mesh.devices.reshape(4, 2, 4, 2, 2), AXES)
    rows = P(AXES, None)
    weight = P(("z", "yl", "x", "c"), "t")
    return jax.shard_map(
        local,
        mesh=fine,
        in_specs=(rows, P(), weight, weight, weight, P(), P(), weight, P(), weight, weight, weight, rows),
        out_specs=(
            rows, rows, P(), weight, weight, weight, P(), P(), weight, P(), weight, weight, weight,
        ),
        check_vma=False,
    )
```

```python
import functools

import jax
import jax.numpy as jnp
from jax import lax
from jax.experimental import pallas as pl
from jax.experimental.pallas import tpu as pltpu
from jax.sharding import Mesh
from jax.sharding import PartitionSpec as P

AXES = ("z", "yl", "x", "c", "t")
SIZES = {"z": 4, "yl": 2, "x": 4, "c": 2, "t": 2}
W_AXES = ("z", "yl")
T_AXES = ("x", "c", "t")
NW, NT = 8, 16
ROWS = 64
TOK = NW * ROWS
D = 2048
HD = 128
SEQ = 8192
QC, KC, FC = 256, 128, 768
QKV = QC + 2 * KC
COLS = QKV + QC + 3 * FC
VMEM_LIMIT = 63 << 20
KB = 256
CH = 2 * ROWS
NROW = NW * CH

epsilon = 1e-06
rope_base = 1000000.0
score_scale = HD ** (-0.5)
LOG2E = 1.4426950408889634

bf16 = jnp.bfloat16
f32 = jnp.float32
MESH = pl.DeviceIdType.MESH
VM = pl.BlockSpec(memory_space=pltpu.VMEM)
ANY = pl.BlockSpec(memory_space=pl.ANY)
DMA = pltpu.SemaphoreType.DMA


def params(cid=None):
    if cid is None:
        return pltpu.CompilerParams(vmem_limit_bytes=VMEM_LIMIT)
    return pltpu.CompilerParams(
        collective_id=cid, has_side_effects=True, vmem_limit_bytes=VMEM_LIMIT
    )


def place():
    return {a: lax.axis_index(a) for a in AXES}


def shifted(me, axis, by):
    return lax.rem(me[axis] + by, SIZES[axis])


def barrier(devices):
    sem = pltpu.get_barrier_semaphore()
    for d in devices:
        pl.semaphore_signal(sem, inc=1, device_id=d, device_id_type=MESH)
    pl.semaphore_wait(sem, len(devices))


def remote(src, dst, ssem, rsem, device):
    return pltpu.make_async_remote_copy(
        src_ref=src, dst_ref=dst, send_sem=ssem, recv_sem=rsem, device_id=device, device_id_type=MESH
    )


class Sends:
    def __init__(self, ssem, rsem, base=0):
        self.ssem, self.rsem, self.base, self.open = ssem, rsem, base, []

    def send(self, kind, src, dst, device):
        k = self.base + kind
        remote(src(), dst(), self.ssem.at[k], self.rsem.at[k], device).start()
        self.open.append((k, src, device))

    def recv(self, kind, dst, device):
        k = self.base + kind
        remote(dst, dst, self.ssem.at[k], self.rsem.at[k], device).wait_recv()

    def close(self):
        for k, src, device in self.open:
            remote(src(), src(), self.ssem.at[k], self.rsem.at[k], device).wait_send()
        self.open = []


def w_devices(me):
    return (
        {"z": shifted(me, "z", 1)},
        {"z": shifted(me, "z", 3)},
        {"yl": 1 - me["yl"]},
    )


UNIT = D // ROWS


class PathsW:
    def __init__(self, me, side, far):
        z, y = me["z"], me["yl"]
        zp, zm, zo, yo = shifted(me, "z", 1), shifted(me, "z", 3), shifted(me, "z", 2), 1 - y
        self.own, self.own_o = 2 * z + y, 2 * z + yo
        self.gp, self.gpo = 2 * zp + y, 2 * zp + yo
        self.gm, self.gmo = 2 * zm + y, 2 * zm + yo
        self.go, self.goo = 2 * zo + y, 2 * zo + yo
        self.dp, self.dm, self.dy = w_devices(me)
        cut = ROWS - far
        self.all, self.near, self.rest = (0, ROWS), (0, side), (side, ROWS)
        self.up, self.down, self.up_near = (cut, ROWS), (0, cut), (cut, side)


class GatherW(PathsW):
    SEMS = 12

    def __init__(self, me, dst, sends, side=44, far=36):
        super().__init__(me, side, far)
        self.dst, self.s = dst, sends

    def part(self, g, cols):
        return self.dst.at[g, :, cols[0] * UNIT : cols[1] * UNIT]

    def put(self, kind, g, cols, device):
        def piece():
            return self.part(g, cols)

        if cols[0] < cols[1]:
            self.s.send(kind, piece, piece, device)

    def got(self, kind, g, cols, device):
        if cols[0] < cols[1]:
            self.s.recv(kind, self.part(g, cols), device)

    def start(self):
        self.put(2, self.own, self.all, self.dy)
        self.put(0, self.own, self.all, self.dp)
        self.put(1, self.own, self.all, self.dm)

    def middle(self):
        dp, dm, dy = self.dp, self.dm, self.dy
        self.got(2, self.own_o, self.all, dy)
        self.put(3, self.own_o, self.near, dp)
        self.put(4, self.own_o, self.near, dm)
        self.got(0, self.gm, self.all, dm)
        self.put(5, self.gm, self.up, dp)
        self.put(6, self.gm, self.rest, dy)
        self.got(1, self.gp, self.all, dp)
        self.put(7, self.gp, self.down, dm)
        self.put(8, self.gp, self.rest, dy)

    def late(self):
        dp, dm, dy = self.dp, self.dm, self.dy
        self.got(3, self.gmo, self.near, dm)
        self.put(9, self.gmo, self.up_near, dp)
        self.got(4, self.gpo, self.near, dp)
        self.put(10, self.gpo, self.down, dm)
        self.got(5, self.go, self.up, dm)
        self.put(11, self.go, self.rest, dy)

    def last(self):
        dp, dm, dy = self.dp, self.dm, self.dy
        self.got(7, self.go, self.down, dp)
        self.got(6, self.gmo, self.rest, dy)
        self.got(8, self.gpo, self.rest, dy)
        self.got(9, self.goo, self.up_near, dm)
        self.got(10, self.goo, self.down, dp)
        self.got(11, self.goo, self.rest, dy)

    def end(self):
        self.late()
        self.last()


class SumW(PathsW):
    SEMS = 12
    BLOCKS = 7

    def __init__(self, me, part, land, sends, side=44, far=36):
        super().__init__(me, side, far)
        self.part, self.land, self.s = part, land, sends
        self.cols = [
            self.rest, self.rest, self.rest, self.up_near, self.down, self.up, self.down, self.near, self.near,
            self.all, self.all, self.all,
        ]
        used, self.at = [0] * self.BLOCKS, [None] * 12
        for kind in sorted(range(12), key=lambda k: self.cols[k][0] - self.cols[k][1]):
            n = self.cols[kind][1] - self.cols[kind][0]
            block = next(i for i in range(self.BLOCKS) if used[i] + n <= ROWS)
            self.at[kind] = (block, used[block], used[block] + n)
            used[block] += n

    def piece(self, g, cols):
        return self.part.at[g, :, cols[0] * UNIT : cols[1] * UNIT]

    def slot(self, kind):
        block, lo, hi = self.at[kind]
        return self.land.at[block, :, lo * UNIT : hi * UNIT]

    def put(self, kind, g, device):
        if self.cols[kind][0] < self.cols[kind][1]:
            self.s.send(kind, lambda: self.piece(g, self.cols[kind]), lambda: self.slot(kind), device)

    def add(self, kind, g, device):
        if self.cols[kind][0] < self.cols[kind][1]:
            rows = self.slot(kind)
            self.s.recv(kind, rows, device)
            mine = self.piece(g, self.cols[kind])
            mine[...] = (mine[...].astype(f32) + rows[...].astype(f32)).astype(bf16)

    def leaf(self):
        dp, dm, dy = self.dp, self.dm, self.dy
        self.put(0, self.goo, dy)
        self.put(3, self.goo, dm)
        self.put(4, self.goo, dp)
        self.put(6, self.go, dp)
        self.put(1, self.gmo, dy)
        self.put(2, self.gpo, dy)

    def two(self):
        dp, dm, dy = self.dp, self.dm, self.dy
        self.add(0, self.go, dy)
        self.put(5, self.go, dm)
        self.add(3, self.gmo, dp)
        self.put(7, self.gmo, dm)
        self.add(4, self.gpo, dm)
        self.put(8, self.gpo, dp)

    def three(self):
        dp, dm, dy = self.dp, self.dm, self.dy
        self.add(1, self.gm, dy)
        self.add(5, self.gm, dp)
        self.put(9, self.gm, dm)
        self.add(2, self.gp, dy)
        self.add(6, self.gp, dm)
        self.put(10, self.gp, dp)
        self.add(7, self.own_o, dp)
        self.add(8, self.own_o, dm)
        self.put(11, self.own_o, dy)

    def total(self):
        self.s.recv(9, self.slot(9), self.dp)
        self.s.recv(10, self.slot(10), self.dm)
        self.s.recv(11, self.slot(11), self.dy)
        total = self.part[self.own].astype(f32) + self.slot(9)[...].astype(f32)
        return total + self.slot(10)[...].astype(f32) + self.slot(11)[...].astype(f32)


def t_devices(me):
    return (
        {"x": shifted(me, "x", 1)},
        {"x": shifted(me, "x", 3)},
        {"t": 1 - me["t"]},
        {"c": 1 - me["c"]},
    )


class GatherT:
    SEMS = 19

    def __init__(self, me, dst, sends):
        self.dst, self.s = dst, sends
        x, c, t = me["x"], me["c"], me["t"]
        xp, xm, xo = shifted(me, "x", 1), shifted(me, "x", 3), shifted(me, "x", 2)
        to, oc = 1 - t, 1 - c
        places = {
            "own": (x, t), "to": (x, to), "p": (xp, t), "po": (xp, to),
            "m": (xm, t), "mo": (xm, to), "o": (xo, t), "oo": (xo, to),
        }
        self.ids = {k: (v[0], c, v[1]) for k, v in places.items()}
        self.sib = {k: (v[0], oc, v[1]) for k, v in places.items()}
        self.dp, self.dm, self.dt, self.dc = t_devices(me)

    def part(self, place, half):
        lo, hi = {None: (0, 8), 0: (0, 4), 1: (4, 8)}[half]
        return self.dst.at[(slice(lo, hi),) + place]

    def put(self, kind, name, device, half=None):
        p = self.ids[name]

        def piece():
            return self.part(p, half)

        self.s.send(kind, piece, piece, device)

    def got(self, kind, name, device, half=None, sib=False):
        p = (self.sib if sib else self.ids)[name]
        self.s.recv(kind, self.part(p, half), device)

    def start(self):
        self.put(2, "own", self.dt)
        self.put(0, "own", self.dp)
        self.put(1, "own", self.dm)
        self.put(3, "own", self.dc)

    def middle(self):
        dp, dm, dt, dc = self.dp, self.dm, self.dt, self.dc
        self.got(2, "to", dt)
        self.put(4, "to", dp)
        self.put(5, "to", dm)
        self.put(6, "to", dc)
        self.got(0, "m", dm)
        self.put(7, "m", dp, 0)
        self.put(8, "m", dc)
        self.got(1, "p", dp)
        self.put(9, "p", dm, 1)
        self.put(10, "p", dc)

    def late(self):
        dp, dm, dc = self.dp, self.dm, self.dc
        self.got(4, "mo", dm)
        self.put(11, "mo", dp, 0)
        self.put(12, "mo", dc)
        self.got(5, "po", dp)
        self.put(13, "po", dm, 1)
        self.put(14, "po", dc)
        self.got(7, "o", dm, 0)
        self.put(15, "o", dc, 0)
        self.got(9, "o", dp, 1)
        self.put(16, "o", dc, 1)

    def last(self):
        dp, dm, dc = self.dp, self.dm, self.dc
        self.got(11, "oo", dm, 0)
        self.put(17, "oo", dc, 0)
        self.got(13, "oo", dp, 1)
        self.put(18, "oo", dc, 1)

    SIBLING = (
        ((3, "own", None), (6, "to", None)),
        ((10, "p", None), (14, "po", None)),
        ((8, "m", None), (12, "mo", None)),
        ((15, "o", 0), (16, "o", 1), (17, "oo", 0), (18, "oo", 1)),
    )

    def column(self, i):
        for kind, name, half in self.SIBLING[i]:
            self.got(kind, name, self.dc, half, True)

    def end(self):
        self.late()
        self.last()
        for i in range(4):
            self.column(i)


def sems(n):
    return [DMA((n,)), DMA((n,))]


GROUPS = (2 * KC, QC, QC, 2 * FC, FC)
STARTS = (QC, 0, QKV, QKV + QC, QKV + QC + 2 * FC)
GAINS = 2 * D + 2 * HD
PEERS_W = [(dz, dy) for dz in range(4) for dy in range(2) if dz or dy]
PEERS_T = [(dx, dc, dt) for dx in range(4) for dc in range(2) for dt in range(2) if dx or dc or dt]


def rms(v):
    return lax.rsqrt(jnp.mean(v * v, axis=-1, keepdims=True) + epsilon)


def mul_rows(a, b):
    return lax.dot_general(a, b, (((1,), (1,)), ((), ())), preferred_element_type=f32)


def mul(a, b):
    return jnp.dot(a, b, preferred_element_type=f32)


def mul_tokens(a, b):
    return lax.dot_general(a, b, (((0,), (0,)), ((), ())), preferred_element_type=f32)


def row_sums(v):
    ones = jnp.ones((8, v.shape[1]), f32)
    return lax.dot_general(
        ones, v, (((1,), (1,)), ((), ())), preferred_element_type=f32, precision=lax.Precision.HIGHEST
    )[0:1]


def head_back(u, g, gain, cosine, sine):
    rolled = jnp.concatenate([g[:, HD // 2 :], g[:, : HD // 2]], axis=1)
    g = g * cosine - rolled * sine
    inv = rms(u)
    normal = u * inv
    total = jnp.sum(g * normal, axis=0, keepdims=True)
    scaled = g * gain
    return inv * (scaled - normal * jnp.mean(scaled * normal, axis=-1, keepdims=True)), total


class SumT:
    SEMS = 9

    def __init__(self, me, src, part, half, land, final, sends):
        self.src, self.part, self.half, self.land, self.final, self.s = src, part, half, land, final, sends
        self.c, self.t = me["c"], me["t"]
        self.oc, self.to = 1 - me["c"], 1 - me["t"]
        self.order = (shifted(me, "x", 2), shifted(me, "x", 3), shifted(me, "x", 1), me["x"])
        self.dp, self.dm, self.dt, self.dc = t_devices(me)
        self.h = part.shape[1] // 2

    def leaf(self, which=range(4)):
        for i in which:
            self.s.send(
                i, lambda i=i: self.src.at[:, self.order[i], self.oc], lambda i=i: self.part.at[i], self.dc
            )

    def pair(self, i):
        self.s.recv(i, self.part.at[i], self.dc)
        mine = self.src[:, self.order[i], self.c]
        self.part[i] = (self.part[i].astype(f32) + mine.astype(f32)).astype(bf16)

    def halves(self):
        self.s.send(4, lambda: self.part.at[0, : self.h], lambda: self.half.at[0], self.dm)
        self.s.send(5, lambda: self.part.at[0, self.h :], lambda: self.half.at[1], self.dp)

    def left(self):
        h = self.h
        self.s.recv(4, self.half.at[0], self.dp)
        self.part[1, :h] = (self.part[1, :h].astype(f32) + self.half[0].astype(f32)).astype(bf16)
        self.s.send(6, lambda: self.part.at[1], lambda: self.land.at[0], self.dm)

    def right(self):
        h = self.h
        self.s.recv(5, self.half.at[1], self.dm)
        self.part[2, h:] = (self.part[2, h:].astype(f32) + self.half[1].astype(f32)).astype(bf16)
        self.s.send(7, lambda: self.part.at[2], lambda: self.land.at[1], self.dp)

    def two(self):
        self.pair(0)
        self.halves()
        self.pair(1)
        self.pair(2)

    def three(self):
        self.left()
        self.right()
        self.pair(3)

    def four(self):
        to = self.to
        self.s.recv(6, self.land.at[0], self.dp)
        self.s.recv(7, self.land.at[1], self.dm)
        self.part[3, :, to] = (
            self.part[3, :, to].astype(f32)
            + self.land[0, :, to].astype(f32)
            + self.land[1, :, to].astype(f32)
        ).astype(bf16)
        self.s.send(8, lambda: self.part.at[3, :, to], lambda: self.final, self.dt)

    def total(self):
        t = self.t
        own = (
            self.part[3, :, t].astype(f32)
            + self.land[0, :, t].astype(f32)
            + self.land[1, :, t].astype(f32)
        )
        self.s.recv(8, self.final, self.dt)
        return own + self.final[...].astype(f32)


def sum_t_scratch(slabs, rows, cols):
    return [
        pltpu.VMEM((4, slabs, 2, rows, cols), bf16),
        pltpu.VMEM((2, slabs // 2, 2, rows, cols), bf16),
        pltpu.VMEM((2, slabs, 2, rows, cols), bf16),
        pltpu.VMEM((slabs, rows, cols), bf16),
    ]


class Return:
    def __init__(self, me, x_ref, out, lo, hi, ssem, rsem, base, lsem):
        self.x, self.out, self.lo, self.hi = x_ref, out, lo, hi
        self.ssem, self.rsem, self.base, self.lsem = ssem, rsem, base, lsem
        self.z, self.y, self.t = me["z"], me["yl"], me["t"]
        self.own_g = 2 * self.z + self.y
        self.holder = self.own_g // 4
        self.block = self.own_g - 4 * self.holder
        self.dy = w_devices(me)[2]

    def each(self, act):
        for g in range(8):
            is_me = (self.own_g == g) & (self.holder == self.t)
            act(g, is_me)

    def start(self):
        def act(g, is_me):
            dst = self.out.at[self.block, self.t, :, self.lo : self.hi]
            to = {"z": jnp.int32(g // 2), "yl": jnp.int32(g % 2), "t": self.holder}
            k = self.base + self.block * 2 + self.t
            c = remote(self.x.at[g], dst, self.ssem.at[self.base + g], self.rsem.at[k], to)
            l = pltpu.make_async_copy(self.x.at[g], dst, self.lsem)

            @pl.when(is_me)
            def _():
                l.start()
                l.wait()

            @pl.when(jnp.logical_not(is_me))
            def _():
                c.start()

        self.each(act)

    def end(self):
        for j in range(4):
            for t2 in range(2):
                is_me = (2 * self.t + j // 2 == self.z) & (j % 2 == self.y) & (self.t == t2)

                @pl.when(jnp.logical_not(is_me))
                def _(j=j, t2=t2):
                    d = self.out.at[j, t2, :, self.lo : self.hi]
                    k = self.base + j * 2 + t2
                    remote(d, d, self.ssem.at[0], self.rsem.at[k], self.dy).wait_recv()

        def act(g, is_me):
            @pl.when(jnp.logical_not(is_me))
            def _():
                x = self.x.at[g]
                remote(x, x, self.ssem.at[self.base + g], self.rsem.at[0], self.dy).wait_send()

        self.each(act)


def rope_rows(angles):
    cosine, sine = angles[:, : HD // 2], angles[:, HD // 2 :]
    return jnp.concatenate([cosine, cosine], axis=1), jnp.concatenate([-sine, sine], axis=1)


def gray(i):
    return i + (i // 2) * (5 - 2 * i)


def seen_keys(s, b, rows, keys_first):
    shape = (KB, rows) if keys_first else (rows, KB)
    row = lax.broadcasted_iota(jnp.int32, shape, 1 if keys_first else 0)
    col = lax.broadcasted_iota(jnp.int32, shape, 0 if keys_first else 1)
    return (row >= CH) | (s * ROWS + (row & (ROWS - 1)) >= b * KB + col)


def attend_column(b, s, q_ref, kv_ref, o_ref, l_ref):
    factor = score_scale * LOG2E
    for g in range(NW):
        pair = kv_ref[g, b].reshape(KB, 2 * KC)
        k, v = pair[:, :KC], pair[:, KC:]
        for r0 in range(g * CH, NROW, 256):
            r1 = min(r0 + 256, NROW)
            p = jnp.exp2(mul_rows(q_ref[r0:r1], k) * factor)
            if r0 == g * CH:
                p = jnp.where(seen_keys(s, b, r1 - r0, False), p, 0.0)
            l_ref[r0:r1] += p[:, :128] + p[:, 128:]
            o_ref[r0:r1] += mul(p.astype(bf16), v)


def attend_back_column(slabs, b, s, q_ref, do_ref, lse_ref, delta_ref, kv_ref, dq_ref):
    factor = score_scale * LOG2E
    for g in slabs:
        pair = kv_ref[g, b].reshape(KB, 2 * KC)
        k, v = pair[:, :KC], pair[:, KC:]
        dk = jnp.zeros((KB, HD), f32)
        dv = jnp.zeros((KB, HD), f32)
        for r0 in range(g * CH, NROW, 256):
            r1 = min(r0 + 256, NROW)
            q = q_ref[r0:r1]
            do = do_ref[r0:r1]
            p = jnp.exp2(mul_rows(k, q) * factor - lse_ref[:, r0:r1])
            if r0 == g * CH:
                p = jnp.where(seen_keys(s, b, r1 - r0, True), p, 0.0)
            ds = (p * (mul_rows(v, do) - delta_ref[:, r0:r1])).astype(bf16)
            dv = dv + mul(p.astype(bf16), do)
            dk = dk + mul(ds, q)
            dq_ref[r0:r1] += mul_tokens(ds, k)
        both = jnp.concatenate([dk * score_scale, dv], axis=1).astype(bf16)
        kv_ref[g, b] = both.reshape(2, 2, ROWS, 2 * KC)


def layer_kernel(
    tok, cot, ngain, fgain, qgain, kgain, angles, wq, wk, wv, wo, wg, wu, wd,
    result, grad_input, gains, back,
    stage, normed_all, cot_all, nt_all, gm_all, kv_all, wqkv, wout, wgu, wdn, part, part_two, land,
    o_acc, l_acc, gate, up, gh, hidden, dgu, q_rows, do_rows, lse, delta, qk_pre, ctx, middle, wdq,
    gsend, gw_land, gt_send, gt_land,
    u1, u2, u3, u4, d1, d2, d3, d4, k1, k2, k3, k4, o1, o2, o3, o4, q1, q2, q3, q4, v1, v2, v3, v4,
    ssem, rsem, lsem,
):
    me = place()
    z, y, x, c, t = (me[a] for a in AXES)
    own_g = 2 * z + y
    s = (x * 2 + c) * 2 + t
    dq = l_acc
    dp, dm, dy = w_devices(me)
    sem = pltpu.get_barrier_semaphore()
    peers = [
        {"z": shifted(me, "z", dz), "yl": shifted(me, "yl", dyl), "t": shifted(me, "t", dt)}
        for dz in range(4) for dyl in range(2) for dt in range(2) if dz or dyl or dt
    ] + [
        {"x": shifted(me, "x", dx), "c": shifted(me, "c", dc), "t": shifted(me, "t", dt)}
        for dx in range(4) for dc in range(2) for dt in range(2) if dx or dc
    ]
    for d in peers:
        pl.semaphore_signal(sem, inc=1, device_id=d, device_id_type=MESH)

    staging, at = [], 0
    for k, w in enumerate((wq, wk, wv, wo, wg, wu, wd)):
        n = w.shape[1] // 4
        for j in range(4):
            piece = w.at[:, j * n : (j + 1) * n]
            staging.append(
                pltpu.make_async_copy(piece, stage.at[j, :, at : at + n], lsem.at[7 + 4 * k + j])
            )
            staging[-1].start()
        at += n
    normed_all[own_g] = (tok[...].astype(f32) * rms(tok[...].astype(f32)) * ngain[...]).astype(bf16)
    cot_all[own_g] = cot[...]
    for l in staging:
        l.wait()
    pl.semaphore_wait(sem, len(peers))

    count = [0]
    opened = []

    def base(n):
        count[0] += n
        return count[0] - n

    def make(kind, *args):
        got = kind(me, *args, Sends(ssem, rsem, base(kind.SEMS)))
        opened.append(got)
        return got

    full = (wqkv.at[:, :, :, :, :, QC:], wqkv.at[:, :, :, :, :, :QC], wout, wgu, wdn)
    to_base = base(40)
    holder = own_g // 4

    def to_holders(groups):
        for j in range(4):
            for t2 in range(2):
                dst_z, dst_y = 2 * t + j // 2, j % 2
                is_me = (dst_z == z) & (dst_y == y) & (t == t2)
                src = stage.at[j, 16 * t2 : 16 * t2 + 16]
                to = {"z": dst_z, "yl": dst_y, "t": jnp.int32(t2)}
                remotes, locals_ = [], []
                for k in groups:
                    piece = src.at[:, STARTS[k] : STARTS[k] + GROUPS[k]]
                    remotes.append(
                        remote(
                            piece, full[k].at[own_g, x, c, t2], ssem.at[to_base + 8 * k + 2 * j + t2],
                            rsem.at[to_base + 8 * k + own_g], to,
                        )
                    )
                    locals_.append(pltpu.make_async_copy(piece, full[k].at[own_g, x, c, t], lsem.at[k]))

                @pl.when(is_me)
                def _():
                    for l in locals_:
                        l.start()
                    for l in locals_:
                        l.wait()

                @pl.when(jnp.logical_not(is_me))
                def _():
                    for r in remotes:
                        r.start()

    def from_owners(groups):
        for g in range(8):
            from_me = (own_g == g) & (holder == t)

            @pl.when(jnp.logical_not(from_me))
            def _(g=g):
                for k in groups:
                    dst = full[k].at[g, x, c, t]
                    remote(dst, dst, ssem.at[0], rsem.at[to_base + 8 * k + g], dy).wait_recv()

    gw = make(GatherW, normed_all)
    gv, gq, go, gg, gd = [make(GatherT, w) for w in full]
    gk = make(GatherT, kv_all)
    gc = GatherW(me, cot_all, Sends(ssem, rsem, base(GatherW.SEMS)), 64, 32)
    opened.append(gc)

    def head_rows(u, gain, cosine, sine):
        n = u * rms(u) * gain
        rolled = jnp.concatenate([n[:, HD // 2 :], n[:, : HD // 2]], axis=1)
        return (n * cosine + rolled * sine).astype(bf16)

    to_holders((0,))
    gw.start()
    to_holders((1, 2))
    from_owners((0,))
    gv.start()
    to_holders((3, 4))
    gw.middle()
    gv.middle()
    gw.late()
    gv.late()
    from_owners((1, 2))
    gq.start()
    go.start()
    gv.last()
    gw.last()
    for i in range(4):
        gv.column(i)

    for h in range(2):
        rows = slice(h * 256, h * 256 + 256)
        pre = mul(
            normed_all[4 * h : 4 * h + 4].reshape(256, D), wqkv[:, :, :, :, :, QC:].reshape(D, 2 * KC)
        )
        qk_pre[rows, QC:] = pre[:, :KC]
        rot = head_rows(pre[:, :KC], kgain[...], *rope_rows(angles[rows]))
        val = pre[:, KC:].astype(bf16)
        for i in range(4):
            piece = slice(i * ROWS, i * ROWS + ROWS)
            kv_all[4 * h + i, x, c, t, :, :KC] = rot[piece]
            kv_all[4 * h + i, x, c, t, :, KC:] = val[piece]
    gk.start()
    gq.middle()
    gc.start()
    o_acc[...] = jnp.zeros_like(o_acc)
    l_acc[...] = jnp.zeros_like(l_acc)
    gk.middle()
    gq.late()
    go.middle()
    gq.last()
    for i in range(4):
        gq.column(i)
    for h in range(2):
        rows = slice(h * 256, h * 256 + 256)
        pre = mul(
            normed_all[4 * h : 4 * h + 4].reshape(256, D), wqkv[:, :, :, :, :, :QC].reshape(D, QC)
        )
        qk_pre[rows, :QC] = pre
        for head in range(2):
            rot = head_rows(pre[:, head * HD : head * HD + HD], qgain[...], *rope_rows(angles[rows]))
            for i in range(4):
                at = (4 * h + i) * CH + head * ROWS
                q_rows[at : at + ROWS] = rot[i * ROWS : i * ROWS + ROWS]
    gk.column(0)

    def attend_step(i, carry):
        @pl.when(i == 1)
        def _():
            gk.late()
            go.late()
            gk.column(1)
            from_owners((3, 4))
            gg.start()
            gc.middle()

        @pl.when(i == 2)
        def _():
            gk.last()
            gk.column(2)
            go.last()
            gc.late()

        @pl.when(i == 3)
        def _():
            gk.column(3)
            gc.last()
            gg.middle()
            gd.start()

        attend_column(lax.rem(x + gray(i), 4), s, q_rows, kv_all, o_acc, l_acc)
        return carry

    lax.fori_loop(0, 4, attend_step, 0)
    for i in range(4):
        go.column(i)

    lse[...] = jnp.log2(row_sums(l_acc[...]))
    for g in range(NW):
        rows = slice(g * CH, g * CH + CH)
        o = o_acc[rows] / jnp.sum(l_acc[rows], axis=1, keepdims=True)
        o_acc[rows] = o
        ctx[g * ROWS : g * ROWS + ROWS, :HD] = o[:ROWS].astype(bf16)
        ctx[g * ROWS : g * ROWS + ROWS, HD:] = o[ROWS:].astype(bf16)

    first_half = (gw.own, gw.own_o, gw.gm, gw.gp)
    other_half = (gw.gmo, gw.gpo, gw.go, gw.goo)

    def block(g):
        return pl.ds(pl.multiple_of(g * ROWS, ROWS), ROWS)

    def out_rows(dst, a_ref, w_ref, cols, blocks):
        a = jnp.concatenate([a_ref[block(g)] for g in blocks], axis=0)
        for n in range(4):
            w = w_ref[2 * n : 2 * n + 2].reshape(512, cols)
            r = mul_rows(a, w).astype(bf16)
            for i, g in enumerate(blocks):
                dst[g, :, n * 512 : n * 512 + 512] = r[i * ROWS : i * ROWS + ROWS]

    out_rows(part, ctx, wout, QC, other_half)
    sw = make(SumW, part, land)
    sw.leaf()
    out_rows(part, ctx, wout, QC, first_half)
    sw.two()
    gg.late()
    sw.three()
    gd.middle()
    mid = tok[...].astype(f32) + sw.total()
    middle[...] = mid
    nt_all[own_g] = (mid * rms(mid) * fgain[...]).astype(bf16)
    gn = make(GatherW, nt_all)
    gn.start()
    gg.last()
    gd.late()
    gn.middle()
    gd.last()
    gn.late()
    for i in range(4):
        gg.column(i)
        gd.column(i)
    for n in range(3):
        cols = slice(n * 256, n * 256 + 256)
        gh[:, cols] = mul(cot_all[...].reshape(TOK, D), wdn[:, :, :, :, :, cols].reshape(D, 256))
    sw.s.close()

    def feed_forward(blocks):
        nt = jnp.concatenate([nt_all[g] for g in blocks], axis=0)
        for n in range(3):
            cols = slice(n * 256, n * 256 + 256)
            upper = slice(FC + n * 256, FC + n * 256 + 256)
            gate[...] = mul(nt, wgu[:, :, :, :, :, cols].reshape(D, 256))
            up[...] = mul(nt, wgu[:, :, :, :, :, upper].reshape(D, 256))
            for i, g in enumerate(blocks):
                piece, rows = slice(i * ROWS, i * ROWS + ROWS), block(g)
                gv_, uv, hv = gate[piece], up[piece], gh[rows, cols]
                sig = jax.nn.sigmoid(gv_)
                act = gv_ * sig
                hidden[rows, cols] = (act * uv).astype(bf16)
                dgu[rows, cols] = (hv * uv * (sig * (1.0 + gv_ * (1.0 - sig)))).astype(bf16)
                dgu[rows, upper] = (hv * act).astype(bf16)
        out_rows(part, dgu, wgu, 2 * FC, blocks)

    feed_forward(first_half)
    gn.last()
    feed_forward(other_half)
    sb = make(SumW, part, land)
    sb.leaf()
    for got in (gg, gd, gw, gc, gn):
        got.s.close()
    out_rows(part_two, hidden, wdn, FC, first_half)
    out_rows(part_two, hidden, wdn, FC, other_half)

    def weight_grads(lo, hi):
        def step(g, carry):
            cols = pl.ds(pl.multiple_of(g * 256, 256), 256)
            a = nt_all[:, :, cols].reshape(TOK, 256)
            for n in range(3):
                w = slice(n * 512, n * 512 + 512)
                wgu[g, :, :, :, :, w] = mul_tokens(a, dgu[:, w]).astype(bf16).reshape(4, 2, 2, 16, 512)
            b = cot_all[:, :, cols].reshape(TOK, 256)
            for n in range(3):
                w = slice(n * 256, n * 256 + 256)
                wdn[g, :, :, :, :, w] = mul_tokens(b, hidden[:, w]).astype(bf16).reshape(4, 2, 2, 16, 256)
            return carry

        lax.fori_loop(lo, hi, step, 0)

    weight_grads(0, 1)
    sb.two()
    weight_grads(1, 3)
    sb.three()
    weight_grads(3, 5)
    gnt = sb.total()
    mid = middle[...]
    inv = rms(mid)
    normal = mid * inv
    gsend[:, D : 2 * D] = jnp.sum(gnt * normal, axis=0, keepdims=True)
    scaled = gnt * fgain[...]
    gm = cot[...].astype(f32) + inv * (
        scaled - normal * jnp.mean(scaled * normal, axis=-1, keepdims=True)
    )
    grad_input[...] = gm
    gm_all[own_g] = gm.astype(bf16)
    ga = make(GatherW, gm_all)
    ga.start()
    weight_grads(5, 8)
    su = make(SumT, wgu, u1, u2, u3, u4)
    sd = make(SumT, wdn, d1, d2, d3, d4)
    su.leaf()
    ga.middle()
    su.pair(0)
    su.halves()
    ga.end()
    grad_ctx = mul(gm_all[...].reshape(TOK, D), wout[...].reshape(D, QC)).astype(bf16)
    for g in range(NW):
        for head in range(2):
            do_rows[g * CH + head * ROWS : g * CH + head * ROWS + ROWS] = grad_ctx[
                g * ROWS : g * ROWS + ROWS, head * HD : head * HD + HD
            ]
    delta[...] = row_sums(do_rows[...].astype(f32) * o_acc[...])
    dq[...] = jnp.zeros_like(dq)
    gk.s.close()
    sr = make(SumW, part_two, nt_all)
    sk = make(SumT, kv_all, k1, k2, k3, k4)
    sr.leaf()
    su.pair(1)
    su.pair(2)
    sd.leaf()
    def weight_step(dst, at, a_ref, b_ref, lo, hi):
        def step(g, carry):
            a = a_ref[:, :, pl.ds(pl.multiple_of(g * 256, 256), 256)].reshape(TOK, 256)
            dst[g, :, :, :, :, at : at + 256] = (
                mul_tokens(a, b_ref[:, lo:hi]).astype(bf16).reshape(4, 2, 2, 16, 256)
            )
            return carry

        lax.fori_loop(0, NW, step, 0)

    go.s.close()
    so = make(SumT, wout, o1, o2, o3, o4)

    def give_back(summed, lo, hi, l):
        summed.final[...] = summed.total().astype(bf16)
        r = Return(me, summed.final, back, lo, hi, ssem, rsem, summed.back, lsem.at[l])
        r.start()
        return r

    for summed in (su, sd, so):
        summed.back = base(8)

    def back_step(i, carry):
        args = (lax.rem(x + gray(3 - i), 4), s, q_rows, do_rows, lse, delta, kv_all, dq)
        attend_back_column(range(0, 3), *args)

        @pl.when(i == 0)
        def _():
            su.left()
            su.right()
            sr.two()

        @pl.when(i == 1)
        def _():
            sk.pair(0)
            sk.halves()
            sr.three()

        @pl.when(i == 2)
        def _():
            sk.pair(1)
            sk.left()
            sd.left()
            sd.right()
            result[...] = (middle[...] + sr.total()).astype(bf16)

        @pl.when(i == 3)
        def _():
            sk.pair(2)
            sk.right()

        attend_back_column(range(3, NW), *args)

        @pl.when(i == 0)
        def _():
            sk.leaf((0,))
            su.pair(3)
            sd.pair(0)
            sd.halves()

        @pl.when(i == 1)
        def _():
            sk.leaf((1,))
            sd.pair(1)
            sd.pair(2)
            su.four()

        @pl.when(i == 2)
        def _():
            sk.leaf((2,))
            sd.pair(3)

        @pl.when(i == 3)
        def _():
            sk.leaf((3,))

        return carry

    lax.fori_loop(0, 4, back_step, 0)

    gp = dgu.at[:, :QKV]
    cosine, sine = rope_rows(angles[...])
    for head in range(2):
        u = qk_pre[:, head * HD : head * HD + HD]
        g = dq[...].reshape(NW, 2, ROWS, HD)[:, head].reshape(TOK, HD) * score_scale
        dpre, gain = head_back(u, g, qgain[...], cosine, sine)
        gp[:, head * HD : head * HD + HD] = dpre.astype(bf16)
        where = slice(2 * D, 2 * D + HD)
        gsend[:, where] = gain if head == 0 else gsend[:, where] + gain

    sk.pair(3)
    sk.four()
    sd.four()
    weight_step(wout, 0, gm_all, ctx, 0, QC)
    so.leaf()
    returns = [give_back(su, 3 * QC, 3 * QC + 2 * FC, 4)]
    weight_step(wdq, 0, normed_all, gp, 0, QC)
    sq = make(SumT, wdq, q1, q2, q3, q4)
    sq.leaf()
    own_kv = sk.total().reshape(TOK, 2 * KC)
    dpre, gain = head_back(qk_pre[:, QC:], own_kv[:, :KC], kgain[...], cosine, sine)
    gp[:, QC : QC + KC] = dpre.astype(bf16)
    gp[:, QC + KC :] = own_kv[:, KC:].astype(bf16)
    gsend[:, 2 * D + HD :] = gain
    sb.s.close()
    out_rows(part, gp, wqkv, QKV, other_half)
    sl = make(SumW, part, land)
    sl.leaf()
    out_rows(part, gp, wqkv, QKV, first_half)
    total = jnp.zeros((1, D), f32)
    for g in range(NW):
        both = part[g].astype(f32) * normed_all[g].astype(f32)
        total = total + jnp.sum(both, axis=0, keepdims=True)
    gsend[:, :D] = total / ngain[...]

    bw = base(len(PEERS_W))
    bt = base(len(PEERS_T))
    first = []
    for i, (dz, dyl) in enumerate(PEERS_W):
        d = {"z": shifted(me, "z", dz), "yl": shifted(me, "yl", dyl)}
        first.append(remote(gsend, gw_land.at[i], ssem.at[bw + i], rsem.at[bw + i], d))
        first[-1].start()
    gv.s.close()
    gq.s.close()
    weight_step(wqkv, QC, normed_all, gp, QC, QKV)
    sv = make(SumT, wqkv.at[:, :, :, :, :, QC:], v1, v2, v3, v4)
    sv.leaf()
    so.two()
    sq.two()
    sl.two()
    sv.two()
    so.three()
    sq.three()
    total = gsend[...]
    for i, r in enumerate(first):
        r.wait_recv()
        total = total + gw_land[i]
    gt_send[...] = total
    second = []
    for i, (dx, dc, dt) in enumerate(PEERS_T):
        d = {"x": shifted(me, "x", dx), "c": shifted(me, "c", dc), "t": shifted(me, "t", dt)}
        second.append(remote(gt_send, gt_land.at[i], ssem.at[bt + i], rsem.at[bt + i], d))
        second[-1].start()
    sl.three()
    sv.three()
    so.four()
    sq.four()
    sq.back = base(8)
    sv.back = base(8)
    returns.append(give_back(sd, 3 * QC + 2 * FC, COLS, 5))
    returns.append(give_back(so, 0, QC, 6))
    returns.append(give_back(sq, QC, 2 * QC, 6))
    sv.four()
    gnorm = sl.total()
    xs = tok[...].astype(f32)
    inv = rms(xs)
    normal = xs * inv
    scaled = gnorm * ngain[...]
    grad_input[...] += inv * (
        scaled - normal * jnp.mean(scaled * normal, axis=-1, keepdims=True)
    )
    returns.append(give_back(sv, 2 * QC, 3 * QC, 6))
    for i, r in enumerate(second):
        r.wait_recv()
        total = total + gt_land[i]
    gains[...] = total
    for r in first + second:
        r.wait_send()
    for r in returns:
        r.end()
    for j in range(4):
        for t2 in range(2):
            is_me = (2 * t + j // 2 == z) & (j % 2 == y) & (t == t2)

            @pl.when(jnp.logical_not(is_me))
            def _(j=j, t2=t2):
                src = stage.at[j, 16 * t2 : 16 * t2 + 16]
                for k in range(5):
                    piece = src.at[:, STARTS[k] : STARTS[k] + GROUPS[k]]
                    remote(
                        piece, piece, ssem.at[to_base + 8 * k + 2 * j + t2], rsem.at[0], dy
                    ).wait_send()
    for got in opened:
        got.s.close()
    assert count[0] == LAYER_SEMS, count[0]


LAYER_SEMS = (
    4 * GatherW.SEMS + 6 * GatherT.SEMS + 4 * SumW.SEMS + 6 * SumT.SEMS + 40 + 5 * 8
    + len(PEERS_W) + len(PEERS_T)
)


def layer(*args):
    def out(shape, dtype):
        return jax.ShapeDtypeStruct(shape, dtype)

    def vmem(shape, dtype=bf16):
        return pltpu.VMEM(shape, dtype)

    def weight(cols):
        return vmem((NW, 4, 2, 2, 16, cols))

    rows = vmem((NW, ROWS, D))
    return pl.pallas_call(
        layer_kernel,
        out_shape=(
            out((ROWS, D), bf16), out((ROWS, D), f32), out((1, GAINS), f32), out((4, 2, 16, COLS), bf16),
        ),
        in_specs=[VM] * 7 + [ANY] * 7,
        out_specs=(VM,) * 4,
        scratch_shapes=[
            vmem((4, 32, COLS)), rows, rows, rows, rows, vmem((NW, 4, 2, 2, ROWS, 2 * KC)),
            weight(QKV), weight(QC), weight(2 * FC), weight(FC), rows, rows,
            vmem((SumW.BLOCKS, ROWS, D)),
            vmem((NROW, HD), f32), vmem((NROW, HD), f32), vmem((256, 256), f32), vmem((256, 256), f32),
            vmem((TOK, FC), f32), vmem((TOK, FC)), vmem((TOK, 2 * FC)), vmem((NROW, HD)), vmem((NROW, HD)),
            vmem((1, NROW), f32), vmem((1, NROW), f32), vmem((TOK, QC + KC), f32), vmem((TOK, QC)),
            vmem((ROWS, D), f32), weight(QC),
            vmem((1, GAINS), f32), vmem((len(PEERS_W), 1, GAINS), f32),
            vmem((1, GAINS), f32), vmem((len(PEERS_T), 1, GAINS), f32),
        ]
        + sum_t_scratch(NW, 16, 2 * FC)
        + sum_t_scratch(NW, 16, FC)
        + sum_t_scratch(NW, ROWS, 2 * KC)
        + sum_t_scratch(NW, 16, QC)
        + sum_t_scratch(NW, 16, QC)
        + sum_t_scratch(NW, 16, QC)
        + sems(LAYER_SEMS) + [DMA((35,))],
        compiler_params=params(0),
        name="layer",
    )(*args)


def finish_kernel(
    result_in, grad_in, gains_in, back,
    result, grad_input, gain_one, gain_q, gain_k, gain_two, g_out, g_q, g_k, g_v, g_gate, g_up, g_down,
):
    result[...] = result_in[...]
    grad_input[...] = grad_in[...]
    gain_one[...] = gains_in[:, :D]
    gain_two[...] = gains_in[:, D : 2 * D]
    gain_q[...] = gains_in[:, 2 * D : 2 * D + HD]
    gain_k[...] = gains_in[:, 2 * D + HD :]
    at = 0
    for grad in (g_out, g_q, g_k, g_v, g_gate, g_up, g_down):
        n = grad.shape[1] // 4
        for j in range(4):
            grad[:, j * n : j * n + n] = back[j, :, :, at : at + n].reshape(32, n).astype(f32)
        at += n


def finish(*args):
    def out(rows, cols, dtype=f32):
        return jax.ShapeDtypeStruct((rows, cols), dtype)

    widths = (QC, QC, KC, KC, FC, FC, FC)
    return pl.pallas_call(
        finish_kernel,
        out_shape=(
            out(ROWS, D, bf16), out(ROWS, D), out(1, D), out(1, HD), out(1, HD), out(1, D),
        ) + tuple(out(32, 4 * n) for n in widths),
        in_specs=[VM] * 4,
        out_specs=(VM,) * 13,
        compiler_params=params(),
        name="finish",
    )(*args)


def local(
    tokens, norm_gain, w_query, key_matrix, value_matrix, query_gain, key_gain, w_out, ffn_gain,
    w_gate, w_up, w_down, cotangent,
):
    s = (lax.axis_index("x") * 2 + lax.axis_index("c")) * 2 + lax.axis_index("t")
    at = jnp.arange(TOK, dtype=jnp.int32)
    position = (at // ROWS) * (NT * ROWS) + s * ROWS + at % ROWS
    exponent = jnp.arange(0, HD, 2, dtype=f32) / HD
    angles = position.astype(f32)[:, None] * (1.0 / rope_base**exponent)[None, :]
    result, grad_input, gains, back = layer(
        tokens, cotangent, norm_gain.reshape(1, D), ffn_gain.reshape(1, D), query_gain.reshape(1, HD),
        key_gain.reshape(1, HD), jnp.concatenate([jnp.cos(angles), jnp.sin(angles)], axis=1),
        w_query, key_matrix, value_matrix, w_out, w_gate, w_up, w_down,
    )
    (
        result, grad_input, gain_one, gain_q, gain_k, gain_two, grad_out, grad_query, grad_key, grad_value,
        grad_gate, grad_up, grad_down,
    ) = finish(result, grad_input, gains, back)
    return (
        result, grad_input, gain_one.reshape(D), grad_query, grad_key, grad_value, gain_q.reshape(HD),
        gain_k.reshape(HD), grad_out, gain_two.reshape(D), grad_gate, grad_up, grad_down,
    )


def solution(mesh):
    fine = Mesh(mesh.devices.reshape(4, 2, 4, 2, 2), AXES)
    rows = P(AXES, None)
    weight = P(("z", "yl", "x", "c"), "t")
    return jax.shard_map(
        local,
        mesh=fine,
        in_specs=(rows, P(), weight, weight, weight, P(), P(), weight, P(), weight, weight, weight, rows),
        out_specs=(
            rows, rows, P(), weight, weight, weight, P(), P(), weight, P(), weight, weight, weight,
        ),
        check_vma=False,
    )
```

```python
import functools

import jax
import jax.numpy as jnp
from jax import lax
from jax.experimental import pallas as pl
from jax.experimental.pallas import tpu as pltpu
from jax.sharding import Mesh
from jax.sharding import PartitionSpec as P

AXES = ("z", "yl", "x", "c", "t")
SIZES = {"z": 4, "yl": 2, "x": 4, "c": 2, "t": 2}
W_AXES = ("z", "yl")
T_AXES = ("x", "c", "t")
NW, NT = 8, 16
ROWS = 64
TOK = NW * ROWS
D = 2048
HD = 128
SEQ = 8192
QC, KC, FC = 256, 128, 768
QKV = QC + 2 * KC
COLS = QKV + QC + 3 * FC
VMEM_LIMIT = 63 << 20
KB = 256
CH = 2 * ROWS
NROW = NW * CH

epsilon = 1e-06
rope_base = 1000000.0
score_scale = HD ** (-0.5)
LOG2E = 1.4426950408889634

bf16 = jnp.bfloat16
f32 = jnp.float32
MESH = pl.DeviceIdType.MESH
VM = pl.BlockSpec(memory_space=pltpu.VMEM)
ANY = pl.BlockSpec(memory_space=pl.ANY)
DMA = pltpu.SemaphoreType.DMA


def params(cid=None):
    if cid is None:
        return pltpu.CompilerParams(vmem_limit_bytes=VMEM_LIMIT)
    return pltpu.CompilerParams(
        collective_id=cid, has_side_effects=True, vmem_limit_bytes=VMEM_LIMIT
    )


def place():
    return {a: lax.axis_index(a) for a in AXES}


def shifted(me, axis, by):
    return lax.rem(me[axis] + by, SIZES[axis])


def barrier(devices):
    sem = pltpu.get_barrier_semaphore()
    for d in devices:
        pl.semaphore_signal(sem, inc=1, device_id=d, device_id_type=MESH)
    pl.semaphore_wait(sem, len(devices))


def remote(src, dst, ssem, rsem, device):
    return pltpu.make_async_remote_copy(
        src_ref=src, dst_ref=dst, send_sem=ssem, recv_sem=rsem, device_id=device, device_id_type=MESH
    )


class Sends:
    def __init__(self, ssem, rsem, base=0):
        self.ssem, self.rsem, self.base, self.open = ssem, rsem, base, []

    def send(self, kind, src, dst, device):
        k = self.base + kind
        remote(src(), dst(), self.ssem.at[k], self.rsem.at[k], device).start()
        self.open.append((k, src, device))

    def recv(self, kind, dst, device):
        k = self.base + kind
        remote(dst, dst, self.ssem.at[k], self.rsem.at[k], device).wait_recv()

    def close(self):
        for k, src, device in self.open:
            remote(src(), src(), self.ssem.at[k], self.rsem.at[k], device).wait_send()
        self.open = []


def w_devices(me):
    return (
        {"z": shifted(me, "z", 1)},
        {"z": shifted(me, "z", 3)},
        {"yl": 1 - me["yl"]},
    )


UNIT = D // ROWS


class PathsW:
    def __init__(self, me, side, far):
        z, y = me["z"], me["yl"]
        zp, zm, zo, yo = shifted(me, "z", 1), shifted(me, "z", 3), shifted(me, "z", 2), 1 - y
        self.own, self.own_o = 2 * z + y, 2 * z + yo
        self.gp, self.gpo = 2 * zp + y, 2 * zp + yo
        self.gm, self.gmo = 2 * zm + y, 2 * zm + yo
        self.go, self.goo = 2 * zo + y, 2 * zo + yo
        self.dp, self.dm, self.dy = w_devices(me)
        cut = ROWS - far
        self.all, self.near, self.rest = (0, ROWS), (0, side), (side, ROWS)
        self.up, self.down, self.up_near = (cut, ROWS), (0, cut), (cut, side)


class GatherW(PathsW):
    SEMS = 12

    def __init__(self, me, dst, sends, side=44, far=36):
        super().__init__(me, side, far)
        self.dst, self.s = dst, sends

    def part(self, g, cols):
        return self.dst.at[g, :, cols[0] * UNIT : cols[1] * UNIT]

    def put(self, kind, g, cols, device):
        def piece():
            return self.part(g, cols)

        if cols[0] < cols[1]:
            self.s.send(kind, piece, piece, device)

    def got(self, kind, g, cols, device):
        if cols[0] < cols[1]:
            self.s.recv(kind, self.part(g, cols), device)

    def start(self):
        self.put(2, self.own, self.all, self.dy)
        self.put(0, self.own, self.all, self.dp)
        self.put(1, self.own, self.all, self.dm)

    def middle(self):
        dp, dm, dy = self.dp, self.dm, self.dy
        self.got(2, self.own_o, self.all, dy)
        self.put(3, self.own_o, self.near, dp)
        self.put(4, self.own_o, self.near, dm)
        self.got(0, self.gm, self.all, dm)
        self.put(5, self.gm, self.up, dp)
        self.put(6, self.gm, self.rest, dy)
        self.got(1, self.gp, self.all, dp)
        self.put(7, self.gp, self.down, dm)
        self.put(8, self.gp, self.rest, dy)

    def late(self):
        dp, dm, dy = self.dp, self.dm, self.dy
        self.got(3, self.gmo, self.near, dm)
        self.put(9, self.gmo, self.up_near, dp)
        self.got(4, self.gpo, self.near, dp)
        self.put(10, self.gpo, self.down, dm)
        self.got(5, self.go, self.up, dm)
        self.put(11, self.go, self.rest, dy)

    def last(self):
        dp, dm, dy = self.dp, self.dm, self.dy
        self.got(7, self.go, self.down, dp)
        self.got(6, self.gmo, self.rest, dy)
        self.got(8, self.gpo, self.rest, dy)
        self.got(9, self.goo, self.up_near, dm)
        self.got(10, self.goo, self.down, dp)
        self.got(11, self.goo, self.rest, dy)

    def end(self):
        self.late()
        self.last()


class SumW(PathsW):
    SEMS = 12
    BLOCKS = 7

    def __init__(self, me, part, land, sends, side=44, far=36):
        super().__init__(me, side, far)
        self.part, self.land, self.s = part, land, sends
        self.cols = [
            self.rest, self.rest, self.rest, self.up_near, self.down, self.up, self.down, self.near, self.near,
            self.all, self.all, self.all,
        ]
        used, self.at = [0] * self.BLOCKS, [None] * 12
        for kind in sorted(range(12), key=lambda k: self.cols[k][0] - self.cols[k][1]):
            n = self.cols[kind][1] - self.cols[kind][0]
            block = next(i for i in range(self.BLOCKS) if used[i] + n <= ROWS)
            self.at[kind] = (block, used[block], used[block] + n)
            used[block] += n

    def piece(self, g, cols):
        return self.part.at[g, :, cols[0] * UNIT : cols[1] * UNIT]

    def slot(self, kind):
        block, lo, hi = self.at[kind]
        return self.land.at[block, :, lo * UNIT : hi * UNIT]

    def put(self, kind, g, device):
        if self.cols[kind][0] < self.cols[kind][1]:
            self.s.send(kind, lambda: self.piece(g, self.cols[kind]), lambda: self.slot(kind), device)

    def add(self, kind, g, device):
        if self.cols[kind][0] < self.cols[kind][1]:
            rows = self.slot(kind)
            self.s.recv(kind, rows, device)
            mine = self.piece(g, self.cols[kind])
            mine[...] = (mine[...].astype(f32) + rows[...].astype(f32)).astype(bf16)

    def leaf(self):
        dp, dm, dy = self.dp, self.dm, self.dy
        self.put(0, self.goo, dy)
        self.put(3, self.goo, dm)
        self.put(4, self.goo, dp)
        self.put(6, self.go, dp)
        self.put(1, self.gmo, dy)
        self.put(2, self.gpo, dy)

    def two(self):
        dp, dm, dy = self.dp, self.dm, self.dy
        self.add(0, self.go, dy)
        self.put(5, self.go, dm)
        self.add(3, self.gmo, dp)
        self.put(7, self.gmo, dm)
        self.add(4, self.gpo, dm)
        self.put(8, self.gpo, dp)

    def three(self):
        dp, dm, dy = self.dp, self.dm, self.dy
        self.add(1, self.gm, dy)
        self.add(5, self.gm, dp)
        self.put(9, self.gm, dm)
        self.add(2, self.gp, dy)
        self.add(6, self.gp, dm)
        self.put(10, self.gp, dp)
        self.add(7, self.own_o, dp)
        self.add(8, self.own_o, dm)
        self.put(11, self.own_o, dy)

    def total(self):
        self.s.recv(9, self.slot(9), self.dp)
        self.s.recv(10, self.slot(10), self.dm)
        self.s.recv(11, self.slot(11), self.dy)
        total = self.part[self.own].astype(f32) + self.slot(9)[...].astype(f32)
        return total + self.slot(10)[...].astype(f32) + self.slot(11)[...].astype(f32)


def t_devices(me):
    return (
        {"x": shifted(me, "x", 1)},
        {"x": shifted(me, "x", 3)},
        {"t": 1 - me["t"]},
        {"c": 1 - me["c"]},
    )


class GatherT:
    SEMS = 19

    def __init__(self, me, dst, sends):
        self.dst, self.s = dst, sends
        x, c, t = me["x"], me["c"], me["t"]
        xp, xm, xo = shifted(me, "x", 1), shifted(me, "x", 3), shifted(me, "x", 2)
        to, oc = 1 - t, 1 - c
        places = {
            "own": (x, t), "to": (x, to), "p": (xp, t), "po": (xp, to),
            "m": (xm, t), "mo": (xm, to), "o": (xo, t), "oo": (xo, to),
        }
        self.ids = {k: (v[0], c, v[1]) for k, v in places.items()}
        self.sib = {k: (v[0], oc, v[1]) for k, v in places.items()}
        self.dp, self.dm, self.dt, self.dc = t_devices(me)

    def part(self, place, half):
        lo, hi = {None: (0, 8), 0: (0, 4), 1: (4, 8)}[half]
        return self.dst.at[(slice(lo, hi),) + place]

    def put(self, kind, name, device, half=None):
        p = self.ids[name]

        def piece():
            return self.part(p, half)

        self.s.send(kind, piece, piece, device)

    def got(self, kind, name, device, half=None, sib=False):
        p = (self.sib if sib else self.ids)[name]
        self.s.recv(kind, self.part(p, half), device)

    def start(self):
        self.put(2, "own", self.dt)
        self.put(0, "own", self.dp)
        self.put(1, "own", self.dm)
        self.put(3, "own", self.dc)

    def middle(self):
        dp, dm, dt, dc = self.dp, self.dm, self.dt, self.dc
        self.got(2, "to", dt)
        self.put(4, "to", dp)
        self.put(5, "to", dm)
        self.put(6, "to", dc)
        self.got(0, "m", dm)
        self.put(7, "m", dp, 0)
        self.put(8, "m", dc)
        self.got(1, "p", dp)
        self.put(9, "p", dm, 1)
        self.put(10, "p", dc)

    def late(self):
        dp, dm, dc = self.dp, self.dm, self.dc
        self.got(4, "mo", dm)
        self.put(11, "mo", dp, 0)
        self.put(12, "mo", dc)
        self.got(5, "po", dp)
        self.put(13, "po", dm, 1)
        self.put(14, "po", dc)
        self.got(7, "o", dm, 0)
        self.put(15, "o", dc, 0)
        self.got(9, "o", dp, 1)
        self.put(16, "o", dc, 1)

    def last(self):
        dp, dm, dc = self.dp, self.dm, self.dc
        self.got(11, "oo", dm, 0)
        self.put(17, "oo", dc, 0)
        self.got(13, "oo", dp, 1)
        self.put(18, "oo", dc, 1)

    SIBLING = (
        ((3, "own", None), (6, "to", None)),
        ((10, "p", None), (14, "po", None)),
        ((8, "m", None), (12, "mo", None)),
        ((15, "o", 0), (16, "o", 1), (17, "oo", 0), (18, "oo", 1)),
    )

    def column(self, i):
        for kind, name, half in self.SIBLING[i]:
            self.got(kind, name, self.dc, half, True)

    def end(self):
        self.late()
        self.last()
        for i in range(4):
            self.column(i)


class GatherD(GatherT):
    SEMS = 15
    ROUTES = (
        ("p", "m"), ("m", "p"), ("to", "to"), ("po", "mo"), ("mo", "po"), ("o", "o"), ("oo", "oo"),
    )

    def start(self):
        for kind, (name, _) in enumerate(self.ROUTES):
            x, _, t = self.ids[name]
            self.put(kind, "own", {"x": x, "t": t})
        self.put(7, "own", self.dc)

    def pass_on(self, kinds):
        for kind in kinds:
            name = self.ROUTES[kind][1]
            x, _, t = self.ids[name]
            self.got(kind, name, {"x": x, "t": t})
            self.put(8 + kind, name, self.dc)

    def middle(self):
        self.pass_on((0, 1, 2))

    def late(self):
        self.pass_on((3, 4, 5, 6))

    def last(self):
        pass

    def column(self, i):
        if i == 0:
            self.got(7, "own", self.dc, None, True)
            for kind, (_, name) in enumerate(self.ROUTES):
                self.got(8 + kind, name, self.dc, None, True)


def sems(n):
    return [DMA((n,)), DMA((n,))]


GROUPS = (2 * KC, QC, QC, 2 * FC, FC)
STARTS = (QC, 0, QKV, QKV + QC, QKV + QC + 2 * FC)
GAINS = 2 * D + 2 * HD
PEERS_W = [(dz, dy) for dz in range(4) for dy in range(2) if dz or dy]
PEERS_T = [(dx, dc, dt) for dx in range(4) for dc in range(2) for dt in range(2) if dx or dc or dt]


def rms(v):
    return lax.rsqrt(jnp.mean(v * v, axis=-1, keepdims=True) + epsilon)


def mul_rows(a, b):
    return lax.dot_general(a, b, (((1,), (1,)), ((), ())), preferred_element_type=f32)


def mul(a, b):
    return jnp.dot(a, b, preferred_element_type=f32)


def mul_tokens(a, b):
    return lax.dot_general(a, b, (((0,), (0,)), ((), ())), preferred_element_type=f32)


def row_sums(v):
    ones = jnp.ones((8, v.shape[1]), f32)
    return lax.dot_general(
        ones, v, (((1,), (1,)), ((), ())), preferred_element_type=f32, precision=lax.Precision.HIGHEST
    )[0:1]


def head_back(u, g, gain, cosine, sine):
    rolled = jnp.concatenate([g[:, HD // 2 :], g[:, : HD // 2]], axis=1)
    g = g * cosine - rolled * sine
    inv = rms(u)
    normal = u * inv
    total = jnp.sum(g * normal, axis=0, keepdims=True)
    scaled = g * gain
    return inv * (scaled - normal * jnp.mean(scaled * normal, axis=-1, keepdims=True)), total


class SumT:
    SEMS = 9

    def __init__(self, me, src, part, half, land, final, sends):
        self.src, self.part, self.half, self.land, self.final, self.s = src, part, half, land, final, sends
        self.c, self.t = me["c"], me["t"]
        self.oc, self.to = 1 - me["c"], 1 - me["t"]
        self.order = (shifted(me, "x", 2), shifted(me, "x", 3), shifted(me, "x", 1), me["x"])
        self.dp, self.dm, self.dt, self.dc = t_devices(me)
        self.h = part.shape[1] // 2

    def leaf(self, which=range(4)):
        for i in which:
            self.s.send(
                i, lambda i=i: self.src.at[:, self.order[i], self.oc], lambda i=i: self.part.at[i], self.dc
            )

    def pair(self, i):
        self.s.recv(i, self.part.at[i], self.dc)
        mine = self.src[:, self.order[i], self.c]
        self.part[i] = (self.part[i].astype(f32) + mine.astype(f32)).astype(bf16)

    def halves(self):
        self.s.send(4, lambda: self.part.at[0, : self.h], lambda: self.half.at[0], self.dm)
        self.s.send(5, lambda: self.part.at[0, self.h :], lambda: self.half.at[1], self.dp)

    def left(self):
        h = self.h
        self.s.recv(4, self.half.at[0], self.dp)
        self.part[1, :h] = (self.part[1, :h].astype(f32) + self.half[0].astype(f32)).astype(bf16)
        self.s.send(6, lambda: self.part.at[1], lambda: self.land.at[0], self.dm)

    def right(self):
        h = self.h
        self.s.recv(5, self.half.at[1], self.dm)
        self.part[2, h:] = (self.part[2, h:].astype(f32) + self.half[1].astype(f32)).astype(bf16)
        self.s.send(7, lambda: self.part.at[2], lambda: self.land.at[1], self.dp)

    def two(self):
        self.pair(0)
        self.halves()
        self.pair(1)
        self.pair(2)

    def three(self):
        self.left()
        self.right()
        self.pair(3)

    def four(self):
        to = self.to
        self.s.recv(6, self.land.at[0], self.dp)
        self.s.recv(7, self.land.at[1], self.dm)
        self.part[3, :, to] = (
            self.part[3, :, to].astype(f32)
            + self.land[0, :, to].astype(f32)
            + self.land[1, :, to].astype(f32)
        ).astype(bf16)
        self.s.send(8, lambda: self.part.at[3, :, to], lambda: self.final, self.dt)

    def total(self):
        t = self.t
        own = (
            self.part[3, :, t].astype(f32)
            + self.land[0, :, t].astype(f32)
            + self.land[1, :, t].astype(f32)
        )
        self.s.recv(8, self.final, self.dt)
        return own + self.final[...].astype(f32)


class SumD(SumT):
    SEMS = 11

    def __init__(self, me, src, part, land, sends):
        super().__init__(me, src, part, None, land, None, sends)
        self.routes = [(i, t) for i in range(3) for t in (self.t, self.to)] + [(3, self.to)]

    def two(self):
        for i in range(4):
            self.pair(i)
        for k, (i, t) in enumerate(self.routes):
            self.s.send(
                4 + k, lambda i=i, t=t: self.part.at[i, :, t], lambda k=k: self.land.at[k],
                {"x": self.order[i], "t": t},
            )

    def total(self):
        own = self.part[3, :, self.t].astype(f32)
        for k in range(7):
            self.s.recv(4 + k, self.land.at[k], self.dc)
            own = own + self.land[k].astype(f32)
        return own


def sum_d_scratch(slabs, rows, cols):
    return [pltpu.VMEM((4, slabs, 2, rows, cols), bf16), pltpu.VMEM((7, slabs, rows, cols), bf16)]


def sum_t_scratch(slabs, rows, cols):
    return [
        pltpu.VMEM((4, slabs, 2, rows, cols), bf16),
        pltpu.VMEM((2, slabs // 2, 2, rows, cols), bf16),
        pltpu.VMEM((2, slabs, 2, rows, cols), bf16),
        pltpu.VMEM((slabs, rows, cols), bf16),
    ]


class Return:
    def __init__(self, me, x_ref, out, lo, hi, ssem, rsem, base, lsem):
        self.x, self.out, self.lo, self.hi = x_ref, out, lo, hi
        self.ssem, self.rsem, self.base, self.lsem = ssem, rsem, base, lsem
        self.z, self.y, self.t = me["z"], me["yl"], me["t"]
        self.own_g = 2 * self.z + self.y
        self.holder = self.own_g // 4
        self.block = self.own_g - 4 * self.holder
        self.dy = w_devices(me)[2]

    def each(self, act):
        for g in range(8):
            is_me = (self.own_g == g) & (self.holder == self.t)
            act(g, is_me)

    def start(self):
        def act(g, is_me):
            dst = self.out.at[self.block, self.t, :, self.lo : self.hi]
            to = {"z": jnp.int32(g // 2), "yl": jnp.int32(g % 2), "t": self.holder}
            k = self.base + self.block * 2 + self.t
            c = remote(self.x.at[g], dst, self.ssem.at[self.base + g], self.rsem.at[k], to)
            l = pltpu.make_async_copy(self.x.at[g], dst, self.lsem)

            @pl.when(is_me)
            def _():
                l.start()
                l.wait()

            @pl.when(jnp.logical_not(is_me))
            def _():
                c.start()

        self.each(act)

    def end(self):
        for j in range(4):
            for t2 in range(2):
                is_me = (2 * self.t + j // 2 == self.z) & (j % 2 == self.y) & (self.t == t2)

                @pl.when(jnp.logical_not(is_me))
                def _(j=j, t2=t2):
                    d = self.out.at[j, t2, :, self.lo : self.hi]
                    k = self.base + j * 2 + t2
                    remote(d, d, self.ssem.at[0], self.rsem.at[k], self.dy).wait_recv()

        def act(g, is_me):
            @pl.when(jnp.logical_not(is_me))
            def _():
                x = self.x.at[g]
                remote(x, x, self.ssem.at[self.base + g], self.rsem.at[0], self.dy).wait_send()

        self.each(act)


def rope_rows(angles):
    cosine, sine = angles[:, : HD // 2], angles[:, HD // 2 :]
    return jnp.concatenate([cosine, cosine], axis=1), jnp.concatenate([-sine, sine], axis=1)


def gray(i):
    return i + (i // 2) * (5 - 2 * i)


def seen_keys(s, b, rows, keys_first):
    shape = (KB, rows) if keys_first else (rows, KB)
    row = lax.broadcasted_iota(jnp.int32, shape, 1 if keys_first else 0)
    col = lax.broadcasted_iota(jnp.int32, shape, 0 if keys_first else 1)
    return (row >= CH) | (s * ROWS + (row & (ROWS - 1)) >= b * KB + col)


def attend_column(b, s, q_ref, kv_ref, o_ref, l_ref):
    factor = score_scale * LOG2E
    for g in range(NW):
        pair = kv_ref[g, b].reshape(KB, 2 * KC)
        k, v = pair[:, :KC], pair[:, KC:]
        for r0 in range(g * CH, NROW, 256):
            r1 = min(r0 + 256, NROW)
            p = jnp.exp2(mul_rows(q_ref[r0:r1], k) * factor)
            if r0 == g * CH:
                p = jnp.where(seen_keys(s, b, r1 - r0, False), p, 0.0)
            l_ref[r0:r1] += p[:, :128] + p[:, 128:]
            o_ref[r0:r1] += mul(p.astype(bf16), v)


def attend_back_column(slabs, b, s, q_ref, do_ref, lse_ref, delta_ref, kv_ref, dq_ref):
    factor = score_scale * LOG2E
    for g in slabs:
        pair = kv_ref[g, b].reshape(KB, 2 * KC)
        k, v = pair[:, :KC], pair[:, KC:]
        dk = jnp.zeros((KB, HD), f32)
        dv = jnp.zeros((KB, HD), f32)
        for r0 in range(g * CH, NROW, 256):
            r1 = min(r0 + 256, NROW)
            q = q_ref[r0:r1]
            do = do_ref[r0:r1]
            p = jnp.exp2(mul_rows(k, q) * factor - lse_ref[:, r0:r1])
            if r0 == g * CH:
                p = jnp.where(seen_keys(s, b, r1 - r0, True), p, 0.0)
            ds = (p * (mul_rows(v, do) - delta_ref[:, r0:r1])).astype(bf16)
            dv = dv + mul(p.astype(bf16), do)
            dk = dk + mul(ds, q)
            dq_ref[r0:r1] += mul_tokens(ds, k)
        both = jnp.concatenate([dk * score_scale, dv], axis=1).astype(bf16)
        kv_ref[g, b] = both.reshape(2, 2, ROWS, 2 * KC)


def layer_kernel(
    tok, cot, ngain, fgain, qgain, kgain, angles, wq, wk, wv, wo, wg, wu, wd,
    result, grad_input, gains, back,
    stage, normed_all, cot_all, nt_all, gm_all, kv_all, wqkv, wout, wgu, wdn, part, part_two, land,
    o_acc, l_acc, gate, up, gh, hidden, dgu, q_rows, do_rows, lse, delta, qk_pre, ctx, middle, wdq,
    ret, gsend, gw_land, gt_send, gt_land,
    u1, u2, u3, u4, d1, d2, d3, d4, k1, k2, k3, k4, k5, k6, k7, k8, o1, o2, q1, q2, v1, v2,
    ssem, rsem, lsem,
):
    me = place()
    z, y, x, c, t = (me[a] for a in AXES)
    own_g = 2 * z + y
    s = (x * 2 + c) * 2 + t
    dq = l_acc
    dp, dm, dy = w_devices(me)
    sem = pltpu.get_barrier_semaphore()
    peers = [
        {"z": shifted(me, "z", dz), "yl": shifted(me, "yl", dyl), "t": shifted(me, "t", dt)}
        for dz in range(4) for dyl in range(2) for dt in range(2) if dz or dyl or dt
    ] + [
        {"x": shifted(me, "x", dx), "c": shifted(me, "c", dc), "t": shifted(me, "t", dt)}
        for dx in range(4) for dc in range(2) for dt in range(2) if dx or dc
    ]
    for d in peers:
        pl.semaphore_signal(sem, inc=1, device_id=d, device_id_type=MESH)

    at = 0
    for w in (wq, wk, wv, wo, wg, wu, wd):
        n = w.shape[1] // 4
        for j in range(4):
            stage[j, :, at : at + n] = w[:, j * n : (j + 1) * n]
        at += n
    normed_all[own_g] = (tok[...].astype(f32) * rms(tok[...].astype(f32)) * ngain[...]).astype(bf16)
    cot_all[own_g] = cot[...]
    pl.semaphore_wait(sem, len(peers))

    count = [0]
    opened = []

    def base(n):
        count[0] += n
        return count[0] - n

    def make(kind, *args):
        got = kind(me, *args, Sends(ssem, rsem, base(kind.SEMS)))
        opened.append(got)
        return got

    full = (wqkv.at[:, :, :, :, :, QC:], wqkv.at[:, :, :, :, :, :QC], wout, wgu, wdn)
    to_base = base(40)
    holder = own_g // 4

    def to_holders(groups):
        for j in range(4):
            for t2 in range(2):
                dst_z, dst_y = 2 * t + j // 2, j % 2
                is_me = (dst_z == z) & (dst_y == y) & (t == t2)
                src = stage.at[j, 16 * t2 : 16 * t2 + 16]
                to = {"z": dst_z, "yl": dst_y, "t": jnp.int32(t2)}
                remotes, locals_ = [], []
                for k in groups:
                    piece = src.at[:, STARTS[k] : STARTS[k] + GROUPS[k]]
                    remotes.append(
                        remote(
                            piece, full[k].at[own_g, x, c, t2], ssem.at[to_base + 8 * k + 2 * j + t2],
                            rsem.at[to_base + 8 * k + own_g], to,
                        )
                    )
                    locals_.append(pltpu.make_async_copy(piece, full[k].at[own_g, x, c, t], lsem.at[k]))

                @pl.when(is_me)
                def _():
                    for l in locals_:
                        l.start()
                    for l in locals_:
                        l.wait()

                @pl.when(jnp.logical_not(is_me))
                def _():
                    for r in remotes:
                        r.start()

    def from_owners(groups):
        for g in range(8):
            from_me = (own_g == g) & (holder == t)

            @pl.when(jnp.logical_not(from_me))
            def _(g=g):
                for k in groups:
                    dst = full[k].at[g, x, c, t]
                    remote(dst, dst, ssem.at[0], rsem.at[to_base + 8 * k + g], dy).wait_recv()

    gw = make(GatherW, normed_all)
    gv, gq, go, gg, gd = [
        make(kind, w) for kind, w in zip((GatherD, GatherD, GatherD, GatherT, GatherT), full)
    ]
    gk = make(GatherT, kv_all)
    gc = GatherW(me, cot_all, Sends(ssem, rsem, base(GatherW.SEMS)), 64, 32)
    opened.append(gc)

    def head_rows(u, gain, cosine, sine):
        n = u * rms(u) * gain
        rolled = jnp.concatenate([n[:, HD // 2 :], n[:, : HD // 2]], axis=1)
        return (n * cosine + rolled * sine).astype(bf16)

    to_holders((0,))
    gw.start()
    to_holders((1, 2))
    from_owners((0,))
    gv.start()
    to_holders((3, 4))
    gw.middle()
    gv.middle()
    gw.late()
    gv.late()
    from_owners((1, 2))
    gq.start()
    go.start()
    gv.last()
    gw.last()
    for i in range(4):
        gv.column(i)

    for h in range(2):
        rows = slice(h * 256, h * 256 + 256)
        pre = mul(
            normed_all[4 * h : 4 * h + 4].reshape(256, D), wqkv[:, :, :, :, :, QC:].reshape(D, 2 * KC)
        )
        qk_pre[rows, QC:] = pre[:, :KC]
        rot = head_rows(pre[:, :KC], kgain[...], *rope_rows(angles[rows]))
        val = pre[:, KC:].astype(bf16)
        for i in range(4):
            piece = slice(i * ROWS, i * ROWS + ROWS)
            kv_all[4 * h + i, x, c, t, :, :KC] = rot[piece]
            kv_all[4 * h + i, x, c, t, :, KC:] = val[piece]
    gk.start()
    gq.middle()
    gc.start()
    o_acc[...] = jnp.zeros_like(o_acc)
    l_acc[...] = jnp.zeros_like(l_acc)
    gk.middle()
    gq.late()
    go.middle()
    gq.last()
    for i in range(4):
        gq.column(i)
    for h in range(2):
        rows = slice(h * 256, h * 256 + 256)
        pre = mul(
            normed_all[4 * h : 4 * h + 4].reshape(256, D), wqkv[:, :, :, :, :, :QC].reshape(D, QC)
        )
        qk_pre[rows, :QC] = pre
        for head in range(2):
            rot = head_rows(pre[:, head * HD : head * HD + HD], qgain[...], *rope_rows(angles[rows]))
            for i in range(4):
                at = (4 * h + i) * CH + head * ROWS
                q_rows[at : at + ROWS] = rot[i * ROWS : i * ROWS + ROWS]
    gk.column(0)

    def attend_step(i, carry):
        @pl.when(i == 1)
        def _():
            gk.late()
            go.late()
            gk.column(1)
            from_owners((3, 4))
            gg.start()
            gc.middle()

        @pl.when(i == 2)
        def _():
            gk.last()
            gk.column(2)
            go.last()
            gc.late()

        @pl.when(i == 3)
        def _():
            gk.column(3)
            gc.last()
            gg.middle()
            gd.start()

        attend_column(lax.rem(x + gray(i), 4), s, q_rows, kv_all, o_acc, l_acc)
        return carry

    lax.fori_loop(0, 4, attend_step, 0)
    for i in range(4):
        go.column(i)

    lse[...] = jnp.log2(row_sums(l_acc[...]))
    for g in range(NW):
        rows = slice(g * CH, g * CH + CH)
        o = o_acc[rows] / jnp.sum(l_acc[rows], axis=1, keepdims=True)
        o_acc[rows] = o
        ctx[g * ROWS : g * ROWS + ROWS, :HD] = o[:ROWS].astype(bf16)
        ctx[g * ROWS : g * ROWS + ROWS, HD:] = o[ROWS:].astype(bf16)

    first_half = (gw.own, gw.own_o, gw.gm, gw.gp)
    other_half = (gw.gmo, gw.gpo, gw.go, gw.goo)

    def block(g):
        return pl.ds(pl.multiple_of(g * ROWS, ROWS), ROWS)

    def out_rows(dst, a_ref, w_ref, cols, blocks):
        a = jnp.concatenate([a_ref[block(g)] for g in blocks], axis=0)
        for n in range(4):
            w = w_ref[2 * n : 2 * n + 2].reshape(512, cols)
            r = mul_rows(a, w).astype(bf16)
            for i, g in enumerate(blocks):
                dst[g, :, n * 512 : n * 512 + 512] = r[i * ROWS : i * ROWS + ROWS]

    out_rows(part, ctx, wout, QC, other_half)
    sw = make(SumW, part, land)
    sw.leaf()
    out_rows(part, ctx, wout, QC, first_half)
    sw.two()
    gg.late()
    sw.three()
    gd.middle()
    mid = tok[...].astype(f32) + sw.total()
    middle[...] = mid
    nt_all[own_g] = (mid * rms(mid) * fgain[...]).astype(bf16)
    gn = make(GatherW, nt_all)
    gn.start()
    gg.last()
    gd.late()
    gn.middle()
    gd.last()
    gn.late()
    for i in range(4):
        gg.column(i)
        gd.column(i)
    for n in range(3):
        cols = slice(n * 256, n * 256 + 256)
        gh[:, cols] = mul(cot_all[...].reshape(TOK, D), wdn[:, :, :, :, :, cols].reshape(D, 256))
    sw.s.close()

    def feed_forward(blocks):
        nt = jnp.concatenate([nt_all[g] for g in blocks], axis=0)
        for n in range(3):
            cols = slice(n * 256, n * 256 + 256)
            upper = slice(FC + n * 256, FC + n * 256 + 256)
            gate[...] = mul(nt, wgu[:, :, :, :, :, cols].reshape(D, 256))
            up[...] = mul(nt, wgu[:, :, :, :, :, upper].reshape(D, 256))
            for i, g in enumerate(blocks):
                piece, rows = slice(i * ROWS, i * ROWS + ROWS), block(g)
                gv_, uv, hv = gate[piece], up[piece], gh[rows, cols]
                sig = jax.nn.sigmoid(gv_)
                act = gv_ * sig
                hidden[rows, cols] = (act * uv).astype(bf16)
                dgu[rows, cols] = (hv * uv * (sig * (1.0 + gv_ * (1.0 - sig)))).astype(bf16)
                dgu[rows, upper] = (hv * act).astype(bf16)
        out_rows(part, dgu, wgu, 2 * FC, blocks)

    feed_forward(first_half)
    gn.last()
    feed_forward(other_half)
    sb = make(SumW, part, land)
    sb.leaf()
    for got in (gg, gd, gw, gc, gn):
        got.s.close()
    out_rows(part_two, hidden, wdn, FC, first_half)
    out_rows(part_two, hidden, wdn, FC, other_half)

    def weight_grads(lo, hi):
        def step(g, carry):
            cols = pl.ds(pl.multiple_of(g * 256, 256), 256)
            a = nt_all[:, :, cols].reshape(TOK, 256)
            for n in range(3):
                w = slice(n * 512, n * 512 + 512)
                wgu[g, :, :, :, :, w] = mul_tokens(a, dgu[:, w]).astype(bf16).reshape(4, 2, 2, 16, 512)
            b = cot_all[:, :, cols].reshape(TOK, 256)
            for n in range(3):
                w = slice(n * 256, n * 256 + 256)
                wdn[g, :, :, :, :, w] = mul_tokens(b, hidden[:, w]).astype(bf16).reshape(4, 2, 2, 16, 256)
            return carry

        lax.fori_loop(lo, hi, step, 0)

    weight_grads(0, 2)
    sb.two()
    for j in range(4):
        for t2 in range(2):
            is_me = (2 * t + j // 2 == z) & (j % 2 == y) & (t == t2)

            @pl.when(jnp.logical_not(is_me))
            def _(j=j, t2=t2):
                src = stage.at[j, 16 * t2 : 16 * t2 + 16]
                for k in range(5):
                    piece = src.at[:, STARTS[k] : STARTS[k] + GROUPS[k]]
                    remote(
                        piece, piece, ssem.at[to_base + 8 * k + 2 * j + t2], rsem.at[0], dy
                    ).wait_send()
    weight_grads(2, 5)
    sb.three()
    weight_grads(5, 8)
    su = make(SumT, wgu, u1, u2, u3, u4)
    sd = make(SumT, wdn, d1, d2, d3, d4)
    su.leaf()
    sd.leaf()
    gnt = sb.total()
    mid = middle[...]
    inv = rms(mid)
    normal = mid * inv
    gsend[:, D : 2 * D] = jnp.sum(gnt * normal, axis=0, keepdims=True)
    scaled = gnt * fgain[...]
    gm = cot[...].astype(f32) + inv * (
        scaled - normal * jnp.mean(scaled * normal, axis=-1, keepdims=True)
    )
    grad_input[...] = gm
    gm_all[own_g] = gm.astype(bf16)
    ga = make(GatherW, gm_all)
    ga.start()
    su.pair(0)
    su.halves()
    sd.pair(0)
    sd.halves()
    ga.middle()
    su.pair(1)
    su.left()
    su.pair(2)
    su.right()
    ga.late()
    sd.pair(1)
    sd.left()
    sd.pair(2)
    sd.right()
    ga.last()
    grad_ctx = mul(gm_all[...].reshape(TOK, D), wout[...].reshape(D, QC)).astype(bf16)
    for g in range(NW):
        for head in range(2):
            do_rows[g * CH + head * ROWS : g * CH + head * ROWS + ROWS] = grad_ctx[
                g * ROWS : g * ROWS + ROWS, head * HD : head * HD + HD
            ]
    delta[...] = row_sums(do_rows[...].astype(f32) * o_acc[...])
    dq[...] = jnp.zeros_like(dq)
    gk.s.close()
    sr = make(SumW, part_two, nt_all)
    ka = make(SumT, kv_all.at[0:4], k1, k2, k3, k4)
    kb = make(SumT, kv_all.at[4:8], k5, k6, k7, k8)
    sr.leaf()

    def weight_step(dst, at, a_ref, b_ref, lo, hi):
        def step(g, carry):
            a = a_ref[:, :, pl.ds(pl.multiple_of(g * 256, 256), 256)].reshape(TOK, 256)
            dst[g, :, :, :, :, at : at + 256] = (
                mul_tokens(a, b_ref[:, lo:hi]).astype(bf16).reshape(4, 2, 2, 16, 256)
            )
            return carry

        lax.fori_loop(0, NW, step, 0)

    go.s.close()
    weight_step(wout, 0, gm_all, ctx, 0, QC)
    so = make(SumD, wout, o1, o2)
    so.leaf()
    su.pair(3)
    su.four()
    sd.pair(3)
    sq = make(SumD, wdq, q1, q2)
    sv = make(SumD, wqkv.at[:, :, :, :, :, QC:], v1, v2)
    edges = (0, 3 * QC, 3 * QC + 2 * FC, COLS)
    ra, ru, rd = returns = [
        Return(me, m, back, lo, hi, ssem, rsem, base(8), lsem.at[6])
        for m, lo, hi in zip((ret, su.final, sd.final), edges[:-1], edges[1:])
    ]

    def give_back(summed, r):
        summed.final[...] = summed.total().astype(bf16)
        r.start()

    def back_light(i, carry):
        attend_back_column(
            range(4, 8), lax.rem(x + gray(3 - i), 4), s, q_rows, do_rows, lse, delta, kv_all, dq
        )
        for k in range(4):

            @pl.when(i == k)
            def _(k=k):
                kb.leaf((k,))

        @pl.when(i == 0)
        def _():
            sd.four()

        @pl.when(i == 1)
        def _():
            sr.two()

        @pl.when(i == 2)
        def _():
            so.two()

        @pl.when(i == 3)
        def _():
            give_back(su, ru)

        return carry

    def back_heavy(i, carry):
        args = (lax.rem(x + gray(3 - i), 4), s, q_rows, do_rows, lse, delta, kv_all, dq)
        attend_back_column(range(0, 1), *args)

        @pl.when(i == 0)
        def _():
            kb.pair(0)
            kb.halves()
            kb.pair(1)
            kb.pair(2)

        @pl.when(i == 1)
        def _():
            ka.pair(0)
            ka.halves()
            kb.pair(3)

        @pl.when(i == 2)
        def _():
            ka.pair(1)
            ka.left()
            kb.four()

        @pl.when(i == 3)
        def _():
            ka.pair(2)
            ka.right()

        attend_back_column(range(1, 4), *args)
        for k in range(4):

            @pl.when(i == k)
            def _(k=k):
                ka.leaf((k,))

        @pl.when(i == 0)
        def _():
            kb.left()
            kb.right()
            sr.three()

        @pl.when(i == 1)
        def _():
            give_back(sd, rd)

        @pl.when(i == 2)
        def _():
            result[...] = (middle[...] + sr.total()).astype(bf16)

        return carry

    lax.fori_loop(0, 4, back_light, 0)
    lax.fori_loop(0, 4, back_heavy, 0)

    gp = dgu.at[:, :QKV]
    cosine, sine = rope_rows(angles[...])
    for head in range(2):
        u = qk_pre[:, head * HD : head * HD + HD]
        g = dq[...].reshape(NW, 2, ROWS, HD)[:, head].reshape(TOK, HD) * score_scale
        dpre, gain = head_back(u, g, qgain[...], cosine, sine)
        gp[:, head * HD : head * HD + HD] = dpre.astype(bf16)
        where = slice(2 * D, 2 * D + HD)
        gsend[:, where] = gain if head == 0 else gsend[:, where] + gain

    ka.pair(3)
    ka.four()
    ret[:, :, :QC] = so.total().astype(bf16)
    weight_step(wdq, 0, normed_all, gp, 0, QC)
    sq.leaf()
    for h, summed in ((1, kb), (0, ka)):
        if h == 0:
            sq.two()
        rows = slice(h * 256, h * 256 + 256)
        own_kv = summed.total().reshape(256, 2 * KC)
        dpre, gain = head_back(qk_pre[rows, QC:], own_kv[:, :KC], kgain[...], cosine[rows], sine[rows])
        gp[rows, QC : QC + KC] = dpre.astype(bf16)
        gp[rows, QC + KC :] = own_kv[:, KC:].astype(bf16)
        where = slice(2 * D + HD, 2 * D + 2 * HD)
        gsend[:, where] = gain if h == 1 else gsend[:, where] + gain
    sb.s.close()
    out_rows(part, gp, wqkv, QKV, other_half)
    sl = make(SumW, part, land)
    sl.leaf()
    out_rows(part, gp, wqkv, QKV, first_half)
    gv.s.close()
    gq.s.close()
    weight_step(wqkv, QC, normed_all, gp, QC, QKV)
    sv.leaf()
    total = jnp.zeros((1, D), f32)
    for g in range(NW):
        both = part[g].astype(f32) * normed_all[g].astype(f32)
        total = total + jnp.sum(both, axis=0, keepdims=True)
    gsend[:, :D] = total / ngain[...]
    sl.two()
    sv.two()

    bw = base(len(PEERS_W))
    bt = base(len(PEERS_T))
    first = []
    for i, (dz, dyl) in enumerate(PEERS_W):
        d = {"z": shifted(me, "z", dz), "yl": shifted(me, "yl", dyl)}
        first.append(remote(gsend, gw_land.at[i], ssem.at[bw + i], rsem.at[bw + i], d))
        first[-1].start()
    sl.three()
    ret[:, :, QC : 2 * QC] = sq.total().astype(bf16)
    total = gsend[...]
    for i, r in enumerate(first):
        r.wait_recv()
        total = total + gw_land[i]
    gt_send[...] = total
    second = []
    for i, (dx, dc, dt) in enumerate(PEERS_T):
        d = {"x": shifted(me, "x", dx), "c": shifted(me, "c", dc), "t": shifted(me, "t", dt)}
        second.append(remote(gt_send, gt_land.at[i], ssem.at[bt + i], rsem.at[bt + i], d))
        second[-1].start()
    ret[:, :, 2 * QC :] = sv.total().astype(bf16)
    ra.start()
    for got in opened:
        if got not in (sl, sv):
            got.s.close()
    gnorm = sl.total()
    xs = tok[...].astype(f32)
    inv = rms(xs)
    normal = xs * inv
    scaled = gnorm * ngain[...]
    grad_input[...] += inv * (
        scaled - normal * jnp.mean(scaled * normal, axis=-1, keepdims=True)
    )
    for i, r in enumerate(second):
        r.wait_recv()
        total = total + gt_land[i]
    gains[...] = total
    for r in first + second:
        r.wait_send()
    for r in returns:
        r.end()
    for got in opened:
        got.s.close()
    assert count[0] == LAYER_SEMS, count[0]


LAYER_SEMS = (
    4 * GatherW.SEMS + 3 * GatherT.SEMS + 3 * GatherD.SEMS + 4 * SumW.SEMS + 4 * SumT.SEMS + 3 * SumD.SEMS + 40 + 3 * 8
    + len(PEERS_W) + len(PEERS_T)
)


def layer(*args):
    def out(shape, dtype):
        return jax.ShapeDtypeStruct(shape, dtype)

    def vmem(shape, dtype=bf16):
        return pltpu.VMEM(shape, dtype)

    def weight(cols):
        return vmem((NW, 4, 2, 2, 16, cols))

    rows = vmem((NW, ROWS, D))
    return pl.pallas_call(
        layer_kernel,
        out_shape=(
            out((ROWS, D), bf16), out((ROWS, D), f32), out((1, GAINS), f32), out((4, 2, 16, COLS), bf16),
        ),
        in_specs=[VM] * len(args),
        out_specs=(VM,) * 4,
        scratch_shapes=[
            vmem((4, 32, COLS)), rows, rows, rows, rows, vmem((NW, 4, 2, 2, ROWS, 2 * KC)),
            weight(QKV), weight(QC), weight(2 * FC), weight(FC), rows, rows,
            vmem((SumW.BLOCKS, ROWS, D)),
            vmem((NROW, HD), f32), vmem((NROW, HD), f32), vmem((256, 256), f32), vmem((256, 256), f32),
            vmem((TOK, FC), f32), vmem((TOK, FC)), vmem((TOK, 2 * FC)), vmem((NROW, HD)), vmem((NROW, HD)),
            vmem((1, NROW), f32), vmem((1, NROW), f32), vmem((TOK, QC + KC), f32), vmem((TOK, QC)),
            vmem((ROWS, D), f32), weight(QC),
            vmem((NW, 16, 3 * QC)), vmem((1, GAINS), f32), vmem((len(PEERS_W), 1, GAINS), f32),
            vmem((1, GAINS), f32), vmem((len(PEERS_T), 1, GAINS), f32),
        ]
        + sum_t_scratch(NW, 16, 2 * FC)
        + sum_t_scratch(NW, 16, FC)
        + sum_t_scratch(4, ROWS, 2 * KC)
        + sum_t_scratch(4, ROWS, 2 * KC)
        + sum_d_scratch(NW, 16, QC)
        + sum_d_scratch(NW, 16, QC)
        + sum_d_scratch(NW, 16, QC)
        + sems(LAYER_SEMS) + [DMA((7,))],
        compiler_params=params(0),
        name="layer",
    )(*args)


def finish_kernel(
    result_in, grad_in, gains_in, back,
    result, grad_input, gain_one, gain_q, gain_k, gain_two, g_out, g_q, g_k, g_v, g_gate, g_up, g_down,
):
    result[...] = result_in[...]
    grad_input[...] = grad_in[...]
    gain_one[...] = gains_in[:, :D]
    gain_two[...] = gains_in[:, D : 2 * D]
    gain_q[...] = gains_in[:, 2 * D : 2 * D + HD]
    gain_k[...] = gains_in[:, 2 * D + HD :]
    at = 0
    for grad in (g_out, g_q, g_k, g_v, g_gate, g_up, g_down):
        n = grad.shape[1] // 4
        for j in range(4):
            grad[:, j * n : j * n + n] = back[j, :, :, at : at + n].reshape(32, n).astype(f32)
        at += n


def finish(*args):
    def out(rows, cols, dtype=f32):
        return jax.ShapeDtypeStruct((rows, cols), dtype)

    widths = (QC, QC, KC, KC, FC, FC, FC)
    return pl.pallas_call(
        finish_kernel,
        out_shape=(
            out(ROWS, D, bf16), out(ROWS, D), out(1, D), out(1, HD), out(1, HD), out(1, D),
        ) + tuple(out(32, 4 * n) for n in widths),
        in_specs=[VM] * 4,
        out_specs=(VM,) * 13,
        compiler_params=params(),
        name="finish",
    )(*args)


def local(
    tokens, norm_gain, w_query, key_matrix, value_matrix, query_gain, key_gain, w_out, ffn_gain,
    w_gate, w_up, w_down, cotangent,
):
    s = (lax.axis_index("x") * 2 + lax.axis_index("c")) * 2 + lax.axis_index("t")
    at = jnp.arange(TOK, dtype=jnp.int32)
    position = (at // ROWS) * (NT * ROWS) + s * ROWS + at % ROWS
    exponent = jnp.arange(0, HD, 2, dtype=f32) / HD
    angles = position.astype(f32)[:, None] * (1.0 / rope_base**exponent)[None, :]
    result, grad_input, gains, back = layer(
        tokens, cotangent, norm_gain.reshape(1, D), ffn_gain.reshape(1, D), query_gain.reshape(1, HD),
        key_gain.reshape(1, HD), jnp.concatenate([jnp.cos(angles), jnp.sin(angles)], axis=1),
        w_query, key_matrix, value_matrix, w_out, w_gate, w_up, w_down,
    )
    (
        result, grad_input, gain_one, gain_q, gain_k, gain_two, grad_out, grad_query, grad_key, grad_value,
        grad_gate, grad_up, grad_down,
    ) = finish(result, grad_input, gains, back)
    return (
        result, grad_input, gain_one.reshape(D), grad_query, grad_key, grad_value, gain_q.reshape(HD),
        gain_k.reshape(HD), grad_out, gain_two.reshape(D), grad_gate, grad_up, grad_down,
    )


def solution(mesh):
    fine = Mesh(mesh.devices.reshape(4, 2, 4, 2, 2), AXES)
    rows = P(AXES, None)
    weight = P(("z", "yl", "x", "c"), "t")
    return jax.shard_map(
        local,
        mesh=fine,
        in_specs=(rows, P(), weight, weight, weight, P(), P(), weight, P(), weight, weight, weight, rows),
        out_specs=(
            rows, rows, P(), weight, weight, weight, P(), P(), weight, P(), weight, weight, weight,
        ),
        check_vma=False,
    )
```

```python
import functools

import jax
import jax.numpy as jnp
from jax import lax
from jax.experimental import pallas as pl
from jax.experimental.pallas import tpu as pltpu
from jax.sharding import Mesh
from jax.sharding import PartitionSpec as P

AXES = ("z", "yl", "x", "c", "t")
SIZES = {"z": 4, "yl": 2, "x": 4, "c": 2, "t": 2}
W_AXES = ("z", "yl")
T_AXES = ("x", "c", "t")
NW, NT = 8, 16
ROWS = 64
TOK = NW * ROWS
D = 2048
HD = 128
SEQ = 8192
QC, KC, FC = 256, 128, 768
QKV = QC + 2 * KC
COLS = QKV + QC + 3 * FC
VMEM_LIMIT = 63 << 20
KB = 256
CH = 2 * ROWS
NROW = NW * CH

epsilon = 1e-06
rope_base = 1000000.0
score_scale = HD ** (-0.5)
LOG2E = 1.4426950408889634

bf16 = jnp.bfloat16
f32 = jnp.float32
MESH = pl.DeviceIdType.MESH
VM = pl.BlockSpec(memory_space=pltpu.VMEM)
ANY = pl.BlockSpec(memory_space=pl.ANY)
DMA = pltpu.SemaphoreType.DMA


def params(cid=None):
    if cid is None:
        return pltpu.CompilerParams(vmem_limit_bytes=VMEM_LIMIT)
    return pltpu.CompilerParams(
        collective_id=cid, has_side_effects=True, vmem_limit_bytes=VMEM_LIMIT
    )


def place():
    return {a: lax.axis_index(a) for a in AXES}


def shifted(me, axis, by):
    return lax.rem(me[axis] + by, SIZES[axis])


def barrier(devices):
    sem = pltpu.get_barrier_semaphore()
    for d in devices:
        pl.semaphore_signal(sem, inc=1, device_id=d, device_id_type=MESH)
    pl.semaphore_wait(sem, len(devices))


def remote(src, dst, ssem, rsem, device):
    return pltpu.make_async_remote_copy(
        src_ref=src, dst_ref=dst, send_sem=ssem, recv_sem=rsem, device_id=device, device_id_type=MESH
    )


class Sends:
    def __init__(self, ssem, rsem, base=0):
        self.ssem, self.rsem, self.base, self.open = ssem, rsem, base, []

    def send(self, kind, src, dst, device):
        k = self.base + kind
        remote(src(), dst(), self.ssem.at[k], self.rsem.at[k], device).start()
        self.open.append((k, src, device))

    def recv(self, kind, dst, device):
        k = self.base + kind
        remote(dst, dst, self.ssem.at[k], self.rsem.at[k], device).wait_recv()

    def close(self):
        for k, src, device in self.open:
            remote(src(), src(), self.ssem.at[k], self.rsem.at[k], device).wait_send()
        self.open = []


def w_devices(me):
    return (
        {"z": shifted(me, "z", 1)},
        {"z": shifted(me, "z", 3)},
        {"yl": 1 - me["yl"]},
    )


UNIT = D // ROWS


class PathsW:
    def __init__(self, me, side, far):
        z, y = me["z"], me["yl"]
        zp, zm, zo, yo = shifted(me, "z", 1), shifted(me, "z", 3), shifted(me, "z", 2), 1 - y
        self.own, self.own_o = 2 * z + y, 2 * z + yo
        self.gp, self.gpo = 2 * zp + y, 2 * zp + yo
        self.gm, self.gmo = 2 * zm + y, 2 * zm + yo
        self.go, self.goo = 2 * zo + y, 2 * zo + yo
        self.dp, self.dm, self.dy = w_devices(me)
        cut = ROWS - far
        self.all, self.near, self.rest = (0, ROWS), (0, side), (side, ROWS)
        self.up, self.down, self.up_near = (cut, ROWS), (0, cut), (cut, side)


class GatherW(PathsW):
    SEMS = 12

    def __init__(self, me, dst, sends, side=44, far=36):
        super().__init__(me, side, far)
        self.dst, self.s = dst, sends

    def part(self, g, cols):
        return self.dst.at[g, :, cols[0] * UNIT : cols[1] * UNIT]

    def put(self, kind, g, cols, device):
        def piece():
            return self.part(g, cols)

        if cols[0] < cols[1]:
            self.s.send(kind, piece, piece, device)

    def got(self, kind, g, cols, device):
        if cols[0] < cols[1]:
            self.s.recv(kind, self.part(g, cols), device)

    def start(self):
        self.put(2, self.own, self.all, self.dy)
        self.put(0, self.own, self.all, self.dp)
        self.put(1, self.own, self.all, self.dm)

    def middle(self):
        dp, dm, dy = self.dp, self.dm, self.dy
        self.got(2, self.own_o, self.all, dy)
        self.put(3, self.own_o, self.near, dp)
        self.put(4, self.own_o, self.near, dm)
        self.got(0, self.gm, self.all, dm)
        self.put(5, self.gm, self.up, dp)
        self.put(6, self.gm, self.rest, dy)
        self.got(1, self.gp, self.all, dp)
        self.put(7, self.gp, self.down, dm)
        self.put(8, self.gp, self.rest, dy)

    def late(self):
        dp, dm, dy = self.dp, self.dm, self.dy
        self.got(3, self.gmo, self.near, dm)
        self.put(9, self.gmo, self.up_near, dp)
        self.got(4, self.gpo, self.near, dp)
        self.put(10, self.gpo, self.down, dm)
        self.got(5, self.go, self.up, dm)
        self.put(11, self.go, self.rest, dy)

    def last(self):
        dp, dm, dy = self.dp, self.dm, self.dy
        self.got(7, self.go, self.down, dp)
        self.got(6, self.gmo, self.rest, dy)
        self.got(8, self.gpo, self.rest, dy)
        self.got(9, self.goo, self.up_near, dm)
        self.got(10, self.goo, self.down, dp)
        self.got(11, self.goo, self.rest, dy)

    def end(self):
        self.late()
        self.last()


class SumW(PathsW):
    SEMS = 12
    BLOCKS = 7

    def __init__(self, me, part, land, sends, side=44, far=36):
        super().__init__(me, side, far)
        self.part, self.land, self.s = part, land, sends
        self.cols = [
            self.rest, self.rest, self.rest, self.up_near, self.down, self.up, self.down, self.near, self.near,
            self.all, self.all, self.all,
        ]
        used, self.at = [0] * self.BLOCKS, [None] * 12
        for kind in sorted(range(12), key=lambda k: self.cols[k][0] - self.cols[k][1]):
            n = self.cols[kind][1] - self.cols[kind][0]
            block = next(i for i in range(self.BLOCKS) if used[i] + n <= ROWS)
            self.at[kind] = (block, used[block], used[block] + n)
            used[block] += n

    def piece(self, g, cols):
        return self.part.at[g, :, cols[0] * UNIT : cols[1] * UNIT]

    def slot(self, kind):
        block, lo, hi = self.at[kind]
        return self.land.at[block, :, lo * UNIT : hi * UNIT]

    def put(self, kind, g, device):
        if self.cols[kind][0] < self.cols[kind][1]:
            self.s.send(kind, lambda: self.piece(g, self.cols[kind]), lambda: self.slot(kind), device)

    def add(self, kind, g, device):
        if self.cols[kind][0] < self.cols[kind][1]:
            rows = self.slot(kind)
            self.s.recv(kind, rows, device)
            mine = self.piece(g, self.cols[kind])
            mine[...] = (mine[...].astype(f32) + rows[...].astype(f32)).astype(bf16)

    def leaf(self):
        dp, dm, dy = self.dp, self.dm, self.dy
        self.put(0, self.goo, dy)
        self.put(3, self.goo, dm)
        self.put(4, self.goo, dp)
        self.put(6, self.go, dp)
        self.put(1, self.gmo, dy)
        self.put(2, self.gpo, dy)

    def two(self):
        dp, dm, dy = self.dp, self.dm, self.dy
        self.add(0, self.go, dy)
        self.put(5, self.go, dm)
        self.add(3, self.gmo, dp)
        self.put(7, self.gmo, dm)
        self.add(4, self.gpo, dm)
        self.put(8, self.gpo, dp)

    def three(self):
        dp, dm, dy = self.dp, self.dm, self.dy
        self.add(1, self.gm, dy)
        self.add(5, self.gm, dp)
        self.put(9, self.gm, dm)
        self.add(2, self.gp, dy)
        self.add(6, self.gp, dm)
        self.put(10, self.gp, dp)
        self.add(7, self.own_o, dp)
        self.add(8, self.own_o, dm)
        self.put(11, self.own_o, dy)

    def total(self):
        self.s.recv(9, self.slot(9), self.dp)
        self.s.recv(10, self.slot(10), self.dm)
        self.s.recv(11, self.slot(11), self.dy)
        total = self.part[self.own].astype(f32) + self.slot(9)[...].astype(f32)
        return total + self.slot(10)[...].astype(f32) + self.slot(11)[...].astype(f32)


def t_devices(me):
    return (
        {"x": shifted(me, "x", 1)},
        {"x": shifted(me, "x", 3)},
        {"t": 1 - me["t"]},
        {"c": 1 - me["c"]},
    )


class GatherT:
    SEMS = 19

    def __init__(self, me, dst, sends):
        self.dst, self.s = dst, sends
        x, c, t = me["x"], me["c"], me["t"]
        xp, xm, xo = shifted(me, "x", 1), shifted(me, "x", 3), shifted(me, "x", 2)
        to, oc = 1 - t, 1 - c
        places = {
            "own": (x, t), "to": (x, to), "p": (xp, t), "po": (xp, to),
            "m": (xm, t), "mo": (xm, to), "o": (xo, t), "oo": (xo, to),
        }
        self.ids = {k: (v[0], c, v[1]) for k, v in places.items()}
        self.sib = {k: (v[0], oc, v[1]) for k, v in places.items()}
        self.dp, self.dm, self.dt, self.dc = t_devices(me)

    def part(self, place, half):
        lo, hi = {None: (0, 8), 0: (0, 4), 1: (4, 8)}[half]
        return self.dst.at[(slice(lo, hi),) + place]

    def put(self, kind, name, device, half=None):
        p = self.ids[name]

        def piece():
            return self.part(p, half)

        self.s.send(kind, piece, piece, device)

    def got(self, kind, name, device, half=None, sib=False):
        p = (self.sib if sib else self.ids)[name]
        self.s.recv(kind, self.part(p, half), device)

    def start(self):
        self.put(2, "own", self.dt)
        self.put(0, "own", self.dp)
        self.put(1, "own", self.dm)
        self.put(3, "own", self.dc)

    def middle(self):
        dp, dm, dt, dc = self.dp, self.dm, self.dt, self.dc
        self.got(2, "to", dt)
        self.put(4, "to", dp)
        self.put(5, "to", dm)
        self.put(6, "to", dc)
        self.got(0, "m", dm)
        self.put(7, "m", dp, 0)
        self.put(8, "m", dc)
        self.got(1, "p", dp)
        self.put(9, "p", dm, 1)
        self.put(10, "p", dc)

    def late(self):
        dp, dm, dc = self.dp, self.dm, self.dc
        self.got(4, "mo", dm)
        self.put(11, "mo", dp, 0)
        self.put(12, "mo", dc)
        self.got(5, "po", dp)
        self.put(13, "po", dm, 1)
        self.put(14, "po", dc)
        self.got(7, "o", dm, 0)
        self.put(15, "o", dc, 0)
        self.got(9, "o", dp, 1)
        self.put(16, "o", dc, 1)

    def last(self):
        dp, dm, dc = self.dp, self.dm, self.dc
        self.got(11, "oo", dm, 0)
        self.put(17, "oo", dc, 0)
        self.got(13, "oo", dp, 1)
        self.put(18, "oo", dc, 1)

    SIBLING = (
        ((3, "own", None), (6, "to", None)),
        ((10, "p", None), (14, "po", None)),
        ((8, "m", None), (12, "mo", None)),
        ((15, "o", 0), (16, "o", 1), (17, "oo", 0), (18, "oo", 1)),
    )

    def column(self, i):
        for kind, name, half in self.SIBLING[i]:
            self.got(kind, name, self.dc, half, True)

    def end(self):
        self.late()
        self.last()
        for i in range(4):
            self.column(i)


class GatherD(GatherT):
    SEMS = 15
    ROUTES = (
        ("p", "m"), ("m", "p"), ("to", "to"), ("po", "mo"), ("mo", "po"), ("o", "o"), ("oo", "oo"),
    )

    def start(self):
        for kind, (name, _) in enumerate(self.ROUTES):
            x, _, t = self.ids[name]
            self.put(kind, "own", {"x": x, "t": t})
        self.put(7, "own", self.dc)

    def pass_on(self, kinds):
        for kind in kinds:
            name = self.ROUTES[kind][1]
            x, _, t = self.ids[name]
            self.got(kind, name, {"x": x, "t": t})
            self.put(8 + kind, name, self.dc)

    def middle(self):
        self.pass_on((0, 1, 2))

    def late(self):
        self.pass_on((3, 4, 5, 6))

    def last(self):
        pass

    def column(self, i):
        if i == 0:
            self.got(7, "own", self.dc, None, True)
            for kind, (_, name) in enumerate(self.ROUTES):
                self.got(8 + kind, name, self.dc, None, True)


def sems(n):
    return [DMA((n,)), DMA((n,))]


GROUPS = (2 * KC, QC, QC, 2 * FC, FC)
STARTS = (QC, 0, QKV, QKV + QC, QKV + QC + 2 * FC)
GAINS = 2 * D + 2 * HD
PEERS_W = [(dz, dy) for dz in range(4) for dy in range(2) if dz or dy]
PEERS_T = [(dx, dc, dt) for dx in range(4) for dc in range(2) for dt in range(2) if dx or dc or dt]


def rms(v):
    return lax.rsqrt(jnp.mean(v * v, axis=-1, keepdims=True) + epsilon)


def mul_rows(a, b):
    return lax.dot_general(a, b, (((1,), (1,)), ((), ())), preferred_element_type=f32)


def mul(a, b):
    return jnp.dot(a, b, preferred_element_type=f32)


def mul_tokens(a, b):
    return lax.dot_general(a, b, (((0,), (0,)), ((), ())), preferred_element_type=f32)


def row_sums(v):
    ones = jnp.ones((8, v.shape[1]), f32)
    return lax.dot_general(
        ones, v, (((1,), (1,)), ((), ())), preferred_element_type=f32, precision=lax.Precision.HIGHEST
    )[0:1]


def head_back(u, g, gain, cosine, sine):
    rolled = jnp.concatenate([g[:, HD // 2 :], g[:, : HD // 2]], axis=1)
    g = g * cosine - rolled * sine
    inv = rms(u)
    normal = u * inv
    total = jnp.sum(g * normal, axis=0, keepdims=True)
    scaled = g * gain
    return inv * (scaled - normal * jnp.mean(scaled * normal, axis=-1, keepdims=True)), total


class SumT:
    SEMS = 9

    def __init__(self, me, src, part, half, land, final, sends):
        self.src, self.part, self.half, self.land, self.final, self.s = src, part, half, land, final, sends
        self.c, self.t = me["c"], me["t"]
        self.oc, self.to = 1 - me["c"], 1 - me["t"]
        self.order = (shifted(me, "x", 2), shifted(me, "x", 3), shifted(me, "x", 1), me["x"])
        self.dp, self.dm, self.dt, self.dc = t_devices(me)
        self.h = part.shape[1] // 2

    def leaf(self, which=range(4)):
        for i in which:
            self.s.send(
                i, lambda i=i: self.src.at[:, self.order[i], self.oc], lambda i=i: self.part.at[i], self.dc
            )

    def pair(self, i):
        self.s.recv(i, self.part.at[i], self.dc)
        mine = self.src[:, self.order[i], self.c]
        self.part[i] = (self.part[i].astype(f32) + mine.astype(f32)).astype(bf16)

    def halves(self):
        self.s.send(4, lambda: self.part.at[0, : self.h], lambda: self.half.at[0], self.dm)
        self.s.send(5, lambda: self.part.at[0, self.h :], lambda: self.half.at[1], self.dp)

    def left(self):
        h = self.h
        self.s.recv(4, self.half.at[0], self.dp)
        self.part[1, :h] = (self.part[1, :h].astype(f32) + self.half[0].astype(f32)).astype(bf16)
        self.s.send(6, lambda: self.part.at[1], lambda: self.land.at[0], self.dm)

    def right(self):
        h = self.h
        self.s.recv(5, self.half.at[1], self.dm)
        self.part[2, h:] = (self.part[2, h:].astype(f32) + self.half[1].astype(f32)).astype(bf16)
        self.s.send(7, lambda: self.part.at[2], lambda: self.land.at[1], self.dp)

    def two(self):
        self.pair(0)
        self.halves()
        self.pair(1)
        self.pair(2)

    def three(self):
        self.left()
        self.right()
        self.pair(3)

    def four(self):
        to = self.to
        self.s.recv(6, self.land.at[0], self.dp)
        self.s.recv(7, self.land.at[1], self.dm)
        self.part[3, :, to] = (
            self.part[3, :, to].astype(f32)
            + self.land[0, :, to].astype(f32)
            + self.land[1, :, to].astype(f32)
        ).astype(bf16)
        self.s.send(8, lambda: self.part.at[3, :, to], lambda: self.final, self.dt)

    def total(self):
        t = self.t
        own = (
            self.part[3, :, t].astype(f32)
            + self.land[0, :, t].astype(f32)
            + self.land[1, :, t].astype(f32)
        )
        self.s.recv(8, self.final, self.dt)
        return own + self.final[...].astype(f32)


class SumD(SumT):
    SEMS = 11

    def __init__(self, me, src, part, land, sends):
        super().__init__(me, src, part, None, land, None, sends)
        self.routes = [(i, t) for i in range(3) for t in (self.t, self.to)] + [(3, self.to)]

    def two(self):
        for i in range(4):
            self.pair(i)
        for k, (i, t) in enumerate(self.routes):
            self.s.send(
                4 + k, lambda i=i, t=t: self.part.at[i, :, t], lambda k=k: self.land.at[k],
                {"x": self.order[i], "t": t},
            )

    def total(self):
        own = self.part[3, :, self.t].astype(f32)
        for k in range(7):
            self.s.recv(4 + k, self.land.at[k], self.dc)
            own = own + self.land[k].astype(f32)
        return own


def sum_d_scratch(slabs, rows, cols):
    return [pltpu.VMEM((4, slabs, 2, rows, cols), bf16), pltpu.VMEM((7, slabs, rows, cols), bf16)]


def sum_t_scratch(slabs, rows, cols):
    return [
        pltpu.VMEM((4, slabs, 2, rows, cols), bf16),
        pltpu.VMEM((2, slabs // 2, 2, rows, cols), bf16),
        pltpu.VMEM((2, slabs, 2, rows, cols), bf16),
        pltpu.VMEM((slabs, rows, cols), bf16),
    ]


class Return:
    def __init__(self, me, x_ref, out, lo, hi, ssem, rsem, base, lsem):
        self.x, self.out, self.lo, self.hi = x_ref, out, lo, hi
        self.ssem, self.rsem, self.base, self.lsem = ssem, rsem, base, lsem
        self.z, self.y, self.t = me["z"], me["yl"], me["t"]
        self.own_g = 2 * self.z + self.y
        self.holder = self.own_g // 4
        self.block = self.own_g - 4 * self.holder
        self.dy = w_devices(me)[2]

    def each(self, act):
        for g in range(8):
            is_me = (self.own_g == g) & (self.holder == self.t)
            act(g, is_me)

    def start(self):
        def act(g, is_me):
            dst = self.out.at[self.block, self.t, :, self.lo : self.hi]
            to = {"z": jnp.int32(g // 2), "yl": jnp.int32(g % 2), "t": self.holder}
            k = self.base + self.block * 2 + self.t
            c = remote(self.x.at[g], dst, self.ssem.at[self.base + g], self.rsem.at[k], to)
            l = pltpu.make_async_copy(self.x.at[g], dst, self.lsem)

            @pl.when(is_me)
            def _():
                l.start()
                l.wait()

            @pl.when(jnp.logical_not(is_me))
            def _():
                c.start()

        self.each(act)

    def end(self):
        for j in range(4):
            for t2 in range(2):
                is_me = (2 * self.t + j // 2 == self.z) & (j % 2 == self.y) & (self.t == t2)

                @pl.when(jnp.logical_not(is_me))
                def _(j=j, t2=t2):
                    d = self.out.at[j, t2, :, self.lo : self.hi]
                    k = self.base + j * 2 + t2
                    remote(d, d, self.ssem.at[0], self.rsem.at[k], self.dy).wait_recv()

        def act(g, is_me):
            @pl.when(jnp.logical_not(is_me))
            def _():
                x = self.x.at[g]
                remote(x, x, self.ssem.at[self.base + g], self.rsem.at[0], self.dy).wait_send()

        self.each(act)


def rope_rows(angles):
    cosine, sine = angles[:, : HD // 2], angles[:, HD // 2 :]
    return jnp.concatenate([cosine, cosine], axis=1), jnp.concatenate([-sine, sine], axis=1)


def gray(i):
    return i + (i // 2) * (5 - 2 * i)


def seen_keys(s, b, rows, keys_first):
    shape = (KB, rows) if keys_first else (rows, KB)
    row = lax.broadcasted_iota(jnp.int32, shape, 1 if keys_first else 0)
    col = lax.broadcasted_iota(jnp.int32, shape, 0 if keys_first else 1)
    return (row >= CH) | (s * ROWS + (row & (ROWS - 1)) >= b * KB + col)


def attend_column(b, s, q_ref, kv_ref, o_ref, l_ref):
    factor = score_scale * LOG2E
    for g in range(NW):
        pair = kv_ref[g, b].reshape(KB, 2 * KC)
        k, v = pair[:, :KC], pair[:, KC:]
        for r0 in range(g * CH, NROW, 256):
            r1 = min(r0 + 256, NROW)
            p = jnp.exp2(mul_rows(q_ref[r0:r1], k) * factor)
            if r0 == g * CH:
                p = jnp.where(seen_keys(s, b, r1 - r0, False), p, 0.0)
            l_ref[r0:r1] += p[:, :128] + p[:, 128:]
            o_ref[r0:r1] += mul(p.astype(bf16), v)


def attend_back_column(slabs, b, s, q_ref, do_ref, lse_ref, delta_ref, kv_ref, dq_ref):
    factor = score_scale * LOG2E
    for g in slabs:
        pair = kv_ref[g, b].reshape(KB, 2 * KC)
        k, v = pair[:, :KC], pair[:, KC:]
        dk = jnp.zeros((KB, HD), f32)
        dv = jnp.zeros((KB, HD), f32)
        for r0 in range(g * CH, NROW, 256):
            r1 = min(r0 + 256, NROW)
            q = q_ref[r0:r1]
            do = do_ref[r0:r1]
            p = jnp.exp2(mul_rows(k, q) * factor - lse_ref[:, r0:r1])
            if r0 == g * CH:
                p = jnp.where(seen_keys(s, b, r1 - r0, True), p, 0.0)
            ds = (p * (mul_rows(v, do) - delta_ref[:, r0:r1])).astype(bf16)
            dv = dv + mul(p.astype(bf16), do)
            dk = dk + mul(ds, q)
            dq_ref[r0:r1] += mul_tokens(ds, k)
        both = jnp.concatenate([dk * score_scale, dv], axis=1).astype(bf16)
        kv_ref[g, b] = both.reshape(2, 2, ROWS, 2 * KC)


def layer_kernel(
    tok, cot, ngain, fgain, qgain, kgain, angles, wq, wk, wv, wo, wg, wu, wd,
    result, grad_input, gains, back,
    stage, normed_all, cot_all, nt_all, gm_all, kv_all, wqkv, wout, wgu, wdn, part, part_two, land,
    o_acc, l_acc, gate, up, gh, hidden, dgu, q_rows, do_rows, lse, delta, qk_pre, ctx, middle, wdq,
    ret, gsend, gw_land, gt_send, gt_land,
    u1, u2, u3, u4, d1, d2, d3, d4, k1, k2, k3, k4, k5, k6, k7, k8, o1, o2, q1, q2, v1, v2,
    ssem, rsem, lsem,
):
    me = place()
    z, y, x, c, t = (me[a] for a in AXES)
    own_g = 2 * z + y
    s = (x * 2 + c) * 2 + t
    dq = l_acc
    dp, dm, dy = w_devices(me)
    sem = pltpu.get_barrier_semaphore()
    peers = [
        {"z": shifted(me, "z", dz), "yl": shifted(me, "yl", dyl), "t": shifted(me, "t", dt)}
        for dz in range(4) for dyl in range(2) for dt in range(2) if dz or dyl or dt
    ] + [
        {"x": shifted(me, "x", dx), "c": shifted(me, "c", dc), "t": shifted(me, "t", dt)}
        for dx in range(4) for dc in range(2) for dt in range(2) if dx or dc
    ]
    for d in peers:
        pl.semaphore_signal(sem, inc=1, device_id=d, device_id_type=MESH)

    at = 0
    for w in (wq, wk, wv, wo, wg, wu, wd):
        n = w.shape[1] // 4
        for j in range(4):
            stage[j, :, at : at + n] = w[:, j * n : (j + 1) * n]
        at += n
    normed_all[own_g] = (tok[...].astype(f32) * rms(tok[...].astype(f32)) * ngain[...]).astype(bf16)
    cot_all[own_g] = cot[...]
    pl.semaphore_wait(sem, len(peers))

    count = [0]
    opened = []

    def base(n):
        count[0] += n
        return count[0] - n

    def make(kind, *args):
        got = kind(me, *args, Sends(ssem, rsem, base(kind.SEMS)))
        opened.append(got)
        return got

    full = (wqkv.at[:, :, :, :, :, QC:], wqkv.at[:, :, :, :, :, :QC], wout, wgu, wdn)
    to_base = base(40)
    holder = own_g // 4

    def to_holders(groups):
        for j in range(4):
            for t2 in range(2):
                dst_z, dst_y = 2 * t + j // 2, j % 2
                is_me = (dst_z == z) & (dst_y == y) & (t == t2)
                src = stage.at[j, 16 * t2 : 16 * t2 + 16]
                to = {"z": dst_z, "yl": dst_y, "t": jnp.int32(t2)}
                remotes, locals_ = [], []
                for k in groups:
                    piece = src.at[:, STARTS[k] : STARTS[k] + GROUPS[k]]
                    remotes.append(
                        remote(
                            piece, full[k].at[own_g, x, c, t2], ssem.at[to_base + 8 * k + 2 * j + t2],
                            rsem.at[to_base + 8 * k + own_g], to,
                        )
                    )
                    locals_.append(pltpu.make_async_copy(piece, full[k].at[own_g, x, c, t], lsem.at[k]))

                @pl.when(is_me)
                def _():
                    for l in locals_:
                        l.start()
                    for l in locals_:
                        l.wait()

                @pl.when(jnp.logical_not(is_me))
                def _():
                    for r in remotes:
                        r.start()

    def from_owners(groups):
        for g in range(8):
            from_me = (own_g == g) & (holder == t)

            @pl.when(jnp.logical_not(from_me))
            def _(g=g):
                for k in groups:
                    dst = full[k].at[g, x, c, t]
                    remote(dst, dst, ssem.at[0], rsem.at[to_base + 8 * k + g], dy).wait_recv()

    gw = make(GatherW, normed_all)
    gv, gq, go, gg, gd = [
        make(kind, w) for kind, w in zip((GatherD, GatherD, GatherD, GatherT, GatherT), full)
    ]
    gk = make(GatherT, kv_all)
    gc = GatherW(me, cot_all, Sends(ssem, rsem, base(GatherW.SEMS)), 64, 32)
    opened.append(gc)

    def head_rows(u, gain, cosine, sine):
        n = u * rms(u) * gain
        rolled = jnp.concatenate([n[:, HD // 2 :], n[:, : HD // 2]], axis=1)
        return (n * cosine + rolled * sine).astype(bf16)

    to_holders((0,))
    gw.start()
    to_holders((1, 2))
    from_owners((0,))
    gv.start()
    to_holders((3, 4))
    gw.middle()
    gv.middle()
    gw.late()
    gv.late()
    from_owners((1, 2))
    gq.start()
    go.start()
    gv.last()
    gw.last()
    for i in range(4):
        gv.column(i)

    for h in range(2):
        rows = slice(h * 256, h * 256 + 256)
        pre = mul(
            normed_all[4 * h : 4 * h + 4].reshape(256, D), wqkv[:, :, :, :, :, QC:].reshape(D, 2 * KC)
        )
        qk_pre[rows, QC:] = pre[:, :KC]
        rot = head_rows(pre[:, :KC], kgain[...], *rope_rows(angles[rows]))
        val = pre[:, KC:].astype(bf16)
        for i in range(4):
            piece = slice(i * ROWS, i * ROWS + ROWS)
            kv_all[4 * h + i, x, c, t, :, :KC] = rot[piece]
            kv_all[4 * h + i, x, c, t, :, KC:] = val[piece]
    gk.start()
    gq.middle()
    gc.start()
    o_acc[...] = jnp.zeros_like(o_acc)
    l_acc[...] = jnp.zeros_like(l_acc)
    gk.middle()
    gq.late()
    go.middle()
    gq.last()
    for i in range(4):
        gq.column(i)
    for h in range(2):
        rows = slice(h * 256, h * 256 + 256)
        pre = mul(
            normed_all[4 * h : 4 * h + 4].reshape(256, D), wqkv[:, :, :, :, :, :QC].reshape(D, QC)
        )
        qk_pre[rows, :QC] = pre
        for head in range(2):
            rot = head_rows(pre[:, head * HD : head * HD + HD], qgain[...], *rope_rows(angles[rows]))
            for i in range(4):
                at = (4 * h + i) * CH + head * ROWS
                q_rows[at : at + ROWS] = rot[i * ROWS : i * ROWS + ROWS]
    gk.column(0)

    def attend_step(i, carry):
        @pl.when(i == 1)
        def _():
            gk.late()
            go.late()
            gk.column(1)
            from_owners((3, 4))
            gg.start()
            gc.middle()

        @pl.when(i == 2)
        def _():
            gk.last()
            gk.column(2)
            go.last()
            gc.late()

        @pl.when(i == 3)
        def _():
            gk.column(3)
            gc.last()
            gg.middle()
            gd.start()

        attend_column(lax.rem(x + gray(i), 4), s, q_rows, kv_all, o_acc, l_acc)
        return carry

    lax.fori_loop(0, 4, attend_step, 0)
    for i in range(4):
        go.column(i)

    lse[...] = jnp.log2(row_sums(l_acc[...]))
    for g in range(NW):
        rows = slice(g * CH, g * CH + CH)
        o = o_acc[rows] / jnp.sum(l_acc[rows], axis=1, keepdims=True)
        o_acc[rows] = o
        ctx[g * ROWS : g * ROWS + ROWS, :HD] = o[:ROWS].astype(bf16)
        ctx[g * ROWS : g * ROWS + ROWS, HD:] = o[ROWS:].astype(bf16)

    first_half = (gw.own, gw.own_o, gw.gm, gw.gp)
    other_half = (gw.gmo, gw.gpo, gw.go, gw.goo)

    def block(g):
        return pl.ds(pl.multiple_of(g * ROWS, ROWS), ROWS)

    def out_rows(dst, a_ref, w_ref, cols, blocks):
        a = jnp.concatenate([a_ref[block(g)] for g in blocks], axis=0)
        for n in range(4):
            w = w_ref[2 * n : 2 * n + 2].reshape(512, cols)
            r = mul_rows(a, w).astype(bf16)
            for i, g in enumerate(blocks):
                dst[g, :, n * 512 : n * 512 + 512] = r[i * ROWS : i * ROWS + ROWS]

    out_rows(part, ctx, wout, QC, other_half)
    sw = make(SumW, part, land)
    sw.leaf()
    out_rows(part, ctx, wout, QC, first_half)
    sw.two()
    gg.late()
    sw.three()
    gd.middle()
    mid = tok[...].astype(f32) + sw.total()
    middle[...] = mid
    nt_all[own_g] = (mid * rms(mid) * fgain[...]).astype(bf16)
    gn = make(GatherW, nt_all)
    gn.start()
    gg.last()
    gd.late()
    gn.middle()
    gd.last()
    gn.late()
    for i in range(4):
        gg.column(i)
        gd.column(i)
    for n in range(3):
        cols = slice(n * 256, n * 256 + 256)
        gh[:, cols] = mul(cot_all[...].reshape(TOK, D), wdn[:, :, :, :, :, cols].reshape(D, 256))
    sw.s.close()

    def feed_forward(blocks):
        nt = jnp.concatenate([nt_all[g] for g in blocks], axis=0)
        for n in range(3):
            cols = slice(n * 256, n * 256 + 256)
            upper = slice(FC + n * 256, FC + n * 256 + 256)
            gate[...] = mul(nt, wgu[:, :, :, :, :, cols].reshape(D, 256))
            up[...] = mul(nt, wgu[:, :, :, :, :, upper].reshape(D, 256))
            for i, g in enumerate(blocks):
                piece, rows = slice(i * ROWS, i * ROWS + ROWS), block(g)
                gv_, uv, hv = gate[piece], up[piece], gh[rows, cols]
                sig = jax.nn.sigmoid(gv_)
                act = gv_ * sig
                hidden[rows, cols] = (act * uv).astype(bf16)
                dgu[rows, cols] = (hv * uv * (sig * (1.0 + gv_ * (1.0 - sig)))).astype(bf16)
                dgu[rows, upper] = (hv * act).astype(bf16)
        out_rows(part, dgu, wgu, 2 * FC, blocks)

    feed_forward(first_half)
    gn.last()
    feed_forward(other_half)
    sb = make(SumW, part, land)
    sb.leaf()
    for got in (gg, gd, gw, gc, gn):
        got.s.close()
    out_rows(part_two, hidden, wdn, FC, first_half)
    out_rows(part_two, hidden, wdn, FC, other_half)

    def weight_grads(lo, hi):
        def step(g, carry):
            cols = pl.ds(pl.multiple_of(g * 256, 256), 256)
            a = nt_all[:, :, cols].reshape(TOK, 256)
            for n in range(3):
                w = slice(n * 512, n * 512 + 512)
                wgu[g, :, :, :, :, w] = mul_tokens(a, dgu[:, w]).astype(bf16).reshape(4, 2, 2, 16, 512)
            b = cot_all[:, :, cols].reshape(TOK, 256)
            for n in range(3):
                w = slice(n * 256, n * 256 + 256)
                wdn[g, :, :, :, :, w] = mul_tokens(b, hidden[:, w]).astype(bf16).reshape(4, 2, 2, 16, 256)
            return carry

        lax.fori_loop(lo, hi, step, 0)

    weight_grads(0, 2)
    sb.two()
    for j in range(4):
        for t2 in range(2):
            is_me = (2 * t + j // 2 == z) & (j % 2 == y) & (t == t2)

            @pl.when(jnp.logical_not(is_me))
            def _(j=j, t2=t2):
                src = stage.at[j, 16 * t2 : 16 * t2 + 16]
                for k in range(5):
                    piece = src.at[:, STARTS[k] : STARTS[k] + GROUPS[k]]
                    remote(
                        piece, piece, ssem.at[to_base + 8 * k + 2 * j + t2], rsem.at[0], dy
                    ).wait_send()
    weight_grads(2, 5)
    sb.three()
    weight_grads(5, 8)
    su = make(SumT, wgu, u1, u2, u3, u4)
    sd = make(SumT, wdn, d1, d2, d3, d4)
    su.leaf()
    sd.leaf()
    gnt = sb.total()
    mid = middle[...]
    inv = rms(mid)
    normal = mid * inv
    gsend[:, D : 2 * D] = jnp.sum(gnt * normal, axis=0, keepdims=True)
    scaled = gnt * fgain[...]
    gm = cot[...].astype(f32) + inv * (
        scaled - normal * jnp.mean(scaled * normal, axis=-1, keepdims=True)
    )
    grad_input[...] = gm
    gm_all[own_g] = gm.astype(bf16)
    ga = make(GatherW, gm_all)
    ga.start()
    su.pair(0)
    su.halves()
    sd.pair(0)
    sd.halves()
    ga.middle()
    su.pair(1)
    su.left()
    su.pair(2)
    su.right()
    ga.late()
    sd.pair(1)
    sd.left()
    sd.pair(2)
    sd.right()
    ga.last()
    grad_ctx = mul(gm_all[...].reshape(TOK, D), wout[...].reshape(D, QC)).astype(bf16)
    for g in range(NW):
        for head in range(2):
            do_rows[g * CH + head * ROWS : g * CH + head * ROWS + ROWS] = grad_ctx[
                g * ROWS : g * ROWS + ROWS, head * HD : head * HD + HD
            ]
    delta[...] = row_sums(do_rows[...].astype(f32) * o_acc[...])
    dq[...] = jnp.zeros_like(dq)
    gk.s.close()
    sr = make(SumW, part_two, nt_all)
    ka = make(SumT, kv_all.at[0:4], k1, k2, k3, k4)
    kb = make(SumT, kv_all.at[4:8], k5, k6, k7, k8)
    sr.leaf()

    def weight_step(dst, at, a_ref, b_ref, lo, hi):
        def step(g, carry):
            a = a_ref[:, :, pl.ds(pl.multiple_of(g * 256, 256), 256)].reshape(TOK, 256)
            dst[g, :, :, :, :, at : at + 256] = (
                mul_tokens(a, b_ref[:, lo:hi]).astype(bf16).reshape(4, 2, 2, 16, 256)
            )
            return carry

        lax.fori_loop(0, NW, step, 0)

    go.s.close()
    weight_step(wout, 0, gm_all, ctx, 0, QC)
    so = make(SumD, wout, o1, o2)
    so.leaf()
    su.pair(3)
    su.four()
    sd.pair(3)
    sq = make(SumD, wdq, q1, q2)
    sv = make(SumD, wqkv.at[:, :, :, :, :, QC:], v1, v2)
    edges = (0, 3 * QC, 3 * QC + 2 * FC, COLS)
    ra, ru, rd = returns = [
        Return(me, m, back, lo, hi, ssem, rsem, base(8), lsem.at[6])
        for m, lo, hi in zip((ret, su.final, sd.final), edges[:-1], edges[1:])
    ]

    def give_back(summed, r):
        summed.final[...] = summed.total().astype(bf16)
        r.start()

    def back_light(i, carry):
        attend_back_column(
            range(4, 8), lax.rem(x + gray(3 - i), 4), s, q_rows, do_rows, lse, delta, kv_all, dq
        )
        for k in range(4):

            @pl.when(i == k)
            def _(k=k):
                kb.leaf((k,))

        @pl.when(i == 0)
        def _():
            sd.four()

        @pl.when(i == 1)
        def _():
            sr.two()

        @pl.when(i == 2)
        def _():
            so.two()

        @pl.when(i == 3)
        def _():
            give_back(su, ru)

        return carry

    def back_heavy(i, carry):
        args = (lax.rem(x + gray(3 - i), 4), s, q_rows, do_rows, lse, delta, kv_all, dq)
        attend_back_column(range(0, 1), *args)

        @pl.when(i == 0)
        def _():
            kb.pair(0)
            kb.halves()
            kb.pair(1)
            kb.pair(2)

        @pl.when(i == 1)
        def _():
            ka.pair(0)
            ka.halves()
            kb.pair(3)

        @pl.when(i == 2)
        def _():
            ka.pair(1)
            ka.left()
            kb.four()

        @pl.when(i == 3)
        def _():
            ka.pair(2)
            ka.right()

        attend_back_column(range(1, 4), *args)
        for k in range(4):

            @pl.when(i == k)
            def _(k=k):
                ka.leaf((k,))

        @pl.when(i == 0)
        def _():
            kb.left()
            kb.right()
            sr.three()

        @pl.when(i == 1)
        def _():
            give_back(sd, rd)

        @pl.when(i == 2)
        def _():
            result[...] = (middle[...] + sr.total()).astype(bf16)

        return carry

    lax.fori_loop(0, 4, back_light, 0)
    lax.fori_loop(0, 4, back_heavy, 0)

    gp = dgu.at[:, :QKV]
    cosine, sine = rope_rows(angles[...])
    for head in range(2):
        u = qk_pre[:, head * HD : head * HD + HD]
        g = dq[...].reshape(NW, 2, ROWS, HD)[:, head].reshape(TOK, HD) * score_scale
        dpre, gain = head_back(u, g, qgain[...], cosine, sine)
        gp[:, head * HD : head * HD + HD] = dpre.astype(bf16)
        where = slice(2 * D, 2 * D + HD)
        gsend[:, where] = gain if head == 0 else gsend[:, where] + gain

    ka.pair(3)
    ka.four()
    ret[:, :, :QC] = so.total().astype(bf16)
    weight_step(wdq, 0, normed_all, gp, 0, QC)
    sq.leaf()
    for h, summed in ((1, kb), (0, ka)):
        if h == 0:
            sq.two()
        rows = slice(h * 256, h * 256 + 256)
        own_kv = summed.total().reshape(256, 2 * KC)
        dpre, gain = head_back(qk_pre[rows, QC:], own_kv[:, :KC], kgain[...], cosine[rows], sine[rows])
        gp[rows, QC : QC + KC] = dpre.astype(bf16)
        gp[rows, QC + KC :] = own_kv[:, KC:].astype(bf16)
        where = slice(2 * D + HD, 2 * D + 2 * HD)
        gsend[:, where] = gain if h == 1 else gsend[:, where] + gain
    sb.s.close()
    out_rows(part, gp, wqkv, QKV, other_half)
    sl = make(SumW, part, land)
    sl.leaf()
    out_rows(part, gp, wqkv, QKV, first_half)
    gv.s.close()
    gq.s.close()
    weight_step(wqkv, QC, normed_all, gp, QC, QKV)
    sv.leaf()
    total = jnp.zeros((1, D), f32)
    for g in range(NW):
        both = part[g].astype(f32) * normed_all[g].astype(f32)
        total = total + jnp.sum(both, axis=0, keepdims=True)
    gsend[:, :D] = total / ngain[...]
    sl.two()
    sv.two()

    bw = base(len(PEERS_W))
    bt = base(len(PEERS_T))
    first = []
    for i, (dz, dyl) in enumerate(PEERS_W):
        d = {"z": shifted(me, "z", dz), "yl": shifted(me, "yl", dyl)}
        first.append(remote(gsend, gw_land.at[i], ssem.at[bw + i], rsem.at[bw + i], d))
        first[-1].start()
    sl.three()
    ret[:, :, QC : 2 * QC] = sq.total().astype(bf16)
    total = gsend[...]
    for i, r in enumerate(first):
        r.wait_recv()
        total = total + gw_land[i]
    gt_send[...] = total
    second = []
    for i, (dx, dc, dt) in enumerate(PEERS_T):
        d = {"x": shifted(me, "x", dx), "c": shifted(me, "c", dc), "t": shifted(me, "t", dt)}
        second.append(remote(gt_send, gt_land.at[i], ssem.at[bt + i], rsem.at[bt + i], d))
        second[-1].start()
    ret[:, :, 2 * QC :] = sv.total().astype(bf16)
    ra.start()
    for got in opened:
        if got not in (sl, sv):
            got.s.close()
    ru.end()
    rd.end()
    for i, r in enumerate(second):
        r.wait_recv()
        total = total + gt_land[i]
    gains[...] = total
    for r in first + second:
        r.wait_send()
    gnorm = sl.total()
    xs = tok[...].astype(f32)
    inv = rms(xs)
    normal = xs * inv
    scaled = gnorm * ngain[...]
    grad_input[...] += inv * (
        scaled - normal * jnp.mean(scaled * normal, axis=-1, keepdims=True)
    )
    ra.end()
    for got in opened:
        got.s.close()
    assert count[0] == LAYER_SEMS, count[0]


LAYER_SEMS = (
    4 * GatherW.SEMS + 3 * GatherT.SEMS + 3 * GatherD.SEMS + 4 * SumW.SEMS + 4 * SumT.SEMS + 3 * SumD.SEMS + 40 + 3 * 8
    + len(PEERS_W) + len(PEERS_T)
)


def layer(*args):
    def out(shape, dtype):
        return jax.ShapeDtypeStruct(shape, dtype)

    def vmem(shape, dtype=bf16):
        return pltpu.VMEM(shape, dtype)

    def weight(cols):
        return vmem((NW, 4, 2, 2, 16, cols))

    rows = vmem((NW, ROWS, D))
    return pl.pallas_call(
        layer_kernel,
        out_shape=(
            out((ROWS, D), bf16), out((ROWS, D), f32), out((1, GAINS), f32), out((4, 2, 16, COLS), bf16),
        ),
        in_specs=[VM] * len(args),
        out_specs=(VM,) * 4,
        scratch_shapes=[
            vmem((4, 32, COLS)), rows, rows, rows, rows, vmem((NW, 4, 2, 2, ROWS, 2 * KC)),
            weight(QKV), weight(QC), weight(2 * FC), weight(FC), rows, rows,
            vmem((SumW.BLOCKS, ROWS, D)),
            vmem((NROW, HD), f32), vmem((NROW, HD), f32), vmem((256, 256), f32), vmem((256, 256), f32),
            vmem((TOK, FC), f32), vmem((TOK, FC)), vmem((TOK, 2 * FC)), vmem((NROW, HD)), vmem((NROW, HD)),
            vmem((1, NROW), f32), vmem((1, NROW), f32), vmem((TOK, QC + KC), f32), vmem((TOK, QC)),
            vmem((ROWS, D), f32), weight(QC),
            vmem((NW, 16, 3 * QC)), vmem((1, GAINS), f32), vmem((len(PEERS_W), 1, GAINS), f32),
            vmem((1, GAINS), f32), vmem((len(PEERS_T), 1, GAINS), f32),
        ]
        + sum_t_scratch(NW, 16, 2 * FC)
        + sum_t_scratch(NW, 16, FC)
        + sum_t_scratch(4, ROWS, 2 * KC)
        + sum_t_scratch(4, ROWS, 2 * KC)
        + sum_d_scratch(NW, 16, QC)
        + sum_d_scratch(NW, 16, QC)
        + sum_d_scratch(NW, 16, QC)
        + sems(LAYER_SEMS) + [DMA((7,))],
        compiler_params=params(0),
        name="layer",
    )(*args)


def finish_kernel(
    result_in, grad_in, gains_in, back,
    result, grad_input, gain_one, gain_q, gain_k, gain_two, g_out, g_q, g_k, g_v, g_gate, g_up, g_down,
):
    result[...] = result_in[...]
    grad_input[...] = grad_in[...]
    gain_one[...] = gains_in[:, :D]
    gain_two[...] = gains_in[:, D : 2 * D]
    gain_q[...] = gains_in[:, 2 * D : 2 * D + HD]
    gain_k[...] = gains_in[:, 2 * D + HD :]
    at = 0
    for grad in (g_out, g_q, g_k, g_v, g_gate, g_up, g_down):
        n = grad.shape[1] // 4
        for j in range(4):
            grad[:, j * n : j * n + n] = back[j, :, :, at : at + n].reshape(32, n).astype(f32)
        at += n


def finish(*args):
    def out(rows, cols, dtype=f32):
        return jax.ShapeDtypeStruct((rows, cols), dtype)

    widths = (QC, QC, KC, KC, FC, FC, FC)
    return pl.pallas_call(
        finish_kernel,
        out_shape=(
            out(ROWS, D, bf16), out(ROWS, D), out(1, D), out(1, HD), out(1, HD), out(1, D),
        ) + tuple(out(32, 4 * n) for n in widths),
        in_specs=[VM] * 4,
        out_specs=(VM,) * 13,
        compiler_params=params(),
        name="finish",
    )(*args)


def local(
    tokens, norm_gain, w_query, key_matrix, value_matrix, query_gain, key_gain, w_out, ffn_gain,
    w_gate, w_up, w_down, cotangent,
):
    s = (lax.axis_index("x") * 2 + lax.axis_index("c")) * 2 + lax.axis_index("t")
    at = jnp.arange(TOK, dtype=jnp.int32)
    position = (at // ROWS) * (NT * ROWS) + s * ROWS + at % ROWS
    half = HD // 2
    column = jnp.arange(HD, dtype=jnp.int32)
    exponent = (2 * (column % half)).astype(f32) / HD
    angles = position.astype(f32)[:, None] * (1.0 / rope_base**exponent)[None, :]
    table = jnp.where(column[None, :] < half, jnp.cos(angles), jnp.sin(angles))
    result, grad_input, gains, back = layer(
        tokens, cotangent, norm_gain.reshape(1, D), ffn_gain.reshape(1, D), query_gain.reshape(1, HD),
        key_gain.reshape(1, HD), table,
        w_query, key_matrix, value_matrix, w_out, w_gate, w_up, w_down,
    )
    (
        result, grad_input, gain_one, gain_q, gain_k, gain_two, grad_out, grad_query, grad_key, grad_value,
        grad_gate, grad_up, grad_down,
    ) = finish(result, grad_input, gains, back)
    return (
        result, grad_input, gain_one.reshape(D), grad_query, grad_key, grad_value, gain_q.reshape(HD),
        gain_k.reshape(HD), grad_out, gain_two.reshape(D), grad_gate, grad_up, grad_down,
    )


def solution(mesh):
    fine = Mesh(mesh.devices.reshape(4, 2, 4, 2, 2), AXES)
    rows = P(AXES, None)
    weight = P(("z", "yl", "x", "c"), "t")
    return jax.shard_map(
        local,
        mesh=fine,
        in_specs=(rows, P(), weight, weight, weight, P(), P(), weight, P(), weight, weight, weight, rows),
        out_specs=(
            rows, rows, P(), weight, weight, weight, P(), P(), weight, P(), weight, weight, weight,
        ),
        check_vma=False,
    )
```
